128 devices in a mesh: seq: 16 (over z, x_hi, core), ctx: 8 (over y, x_lo).
Axes of the slice: x: 4 (x_hi: 2, x_lo: 2; x = x_hi * 2 + x_lo), y: 4, z: 4, core: 2. Of those that a mesh axis runs over, the one named last changes fastest.
Arguments:
- tokens: bfloat16 [16, 1024, 1024], P('seq', 'ctx'), may hold values from -6 to 6
- cotangent: bfloat16 [16, 1024, 1024], P('seq', 'ctx'), may hold values from -6 to 6
- segments: int32 [16, 1024], P('seq'), may hold values from 0 to 47, as said below
- positions: int32 [16, 1024], P('seq', 'ctx'), may hold values from 0 to 1021, as said below
- attention_gain: bfloat16 [1024], P(('seq', 'ctx')), may hold values from 0.25 to 1.75
- projection: bfloat16 [1024, 4096], P(('seq', 'ctx')), may hold values from -0.1875 to 0.1875
- head_gain: bfloat16 [256], P(('seq', 'ctx')), may hold values from 0.25 to 1.75
- output_weight: bfloat16 [2048, 1024], P(('seq', 'ctx')), may hold values from -0.75 to 0.75
- feed_gain: bfloat16 [1024], P(('seq', 'ctx')), may hold values from 0.25 to 1.75
- expansion: bfloat16 [1024, 6144], P(('seq', 'ctx')), may hold values from -0.1875 to 0.1875
- contraction: bfloat16 [3072, 1024], P(('seq', 'ctx')), may hold values from -0.21875 to 0.21875
Outputs:
- layer_out: bfloat16 [16, 1024, 1024], P('seq', 'ctx')
- grad_tokens: float32 [16, 1024, 1024], P('seq', 'ctx')
- grad_attention_gain: float32 [1024], P(('seq', 'ctx'))
- grad_projection: float32 [1024, 4096], P(('seq', 'ctx'))
- grad_head_gain: float32 [256], P(('seq', 'ctx'))
- grad_output_weight: float32 [2048, 1024], P(('seq', 'ctx'))
- grad_feed_gain: float32 [1024], P(('seq', 'ctx'))
- grad_expansion: float32 [1024, 6144], P(('seq', 'ctx'))
- grad_contraction: float32 [3072, 1024], P(('seq', 'ctx'))
The draws below stay inside these ranges and needn't reach their ends.
Inputs may be any that keep to these rules, and one draw needn't show every extreme that they name: `segments`: along each sequence the ids never fall; sequence s holds the documents 3 s, 3 s + 1 and 3 s + 2; the first and the last of them hold 1 to 127 tokens each, the middle one the rest. `positions`: a token's index within its document, 0 at the document's first token.
All inputs are finite; a program needn't handle non-finite values.
Results may differ from the reference program's by a relative error of at most 0.03.
Values may be sent and summed in bfloat16 or wider, within the bound.
A program may use at most 192 MiB of HBM per device.

```python
import jax
import jax.numpy as jnp
from jax import lax

D = 1024
QUERY_HEADS = 16
KEY_VALUE_HEADS = 8
HEAD_SIZE = 128
FF = 3072
SEQ_LEN = 1024
SEQS = 16
SLICE = 128
QKV = 4096


def document_edges(key):
    sequence = jnp.arange(SEQS, dtype=jnp.int32)[:, None]
    first_drawn = jax.random.randint(jax.random.fold_in(key, 101), (SEQS, 1), 1, SLICE)
    last_drawn = SEQ_LEN - jax.random.randint(jax.random.fold_in(key, 102), (SEQS, 1), 1, SLICE)
    first_edge = jnp.where(sequence == 0, 1, first_drawn)
    last_edge = jnp.where(sequence == 0, SEQ_LEN - 1, last_drawn)
    token_index = jnp.arange(SEQ_LEN, dtype=jnp.int32)[None, :]
    past_first = (token_index >= first_edge).astype(jnp.int32)
    past_last = (token_index >= last_edge).astype(jnp.int32)
    return (token_index, first_edge, last_edge, past_first, past_last)


def draw_segments(key, part):
    token_index, first_edge, last_edge, past_first, past_last = document_edges(key)
    sequence = jnp.arange(SEQS, dtype=jnp.int32)[:, None]
    return 3 * sequence + past_first + past_last


def draw_positions(key, part):
    token_index, first_edge, last_edge, past_first, past_last = document_edges(key)
    start_at = past_last * last_edge + (past_first - past_last) * first_edge
    return token_index - start_at


def level_of(key, extent, pieces, least, top_value):
    gain, own = 1.0, jax.random.fold_in(key, 6)
    for axis_at, parts in pieces:
        heights = jnp.exp(jax.random.uniform(jax.random.fold_in(own, axis_at), (parts,), jnp.float32, least / len(pieces), top_value / len(pieces)))
        gain = gain * jnp.repeat(heights, extent[axis_at] // parts).reshape([-1 if axis == axis_at else 1 for axis in range(len(extent))])
    return gain


def scatter_about(own_key, dims, deviation, reach, split=(), kind=jnp.bfloat16):
    entries = deviation * jax.random.normal(own_key, dims, jnp.float32)
    if split:
        entries = entries * level_of(own_key, dims, split, -0.22, 0.18)
    return jnp.clip(entries, -reach, reach).astype(kind)


def setup_inputs(seed: int = 0) -> dict:
    key_of = jax.random.split(jax.random.key(seed), 12)
    return {
        "tokens": scatter_about(key_of[0], (SEQS, SEQ_LEN, D), 1.0, 6.0, ((0, 16), (1, 8))),
        "cotangent": scatter_about(key_of[1], (SEQS, SEQ_LEN, D), 1.0, 6.0, ((0, 16), (1, 8))),
        "segments": draw_segments(jax.random.fold_in(key_of[11], 71), 0),
        "positions": draw_positions(jax.random.fold_in(key_of[11], 71), 0),
        "attention_gain": jnp.clip(1.0 + 0.15 * jax.random.normal(key_of[4], (D,), jnp.float32), 0.25, 1.75).astype(jnp.bfloat16),
        "projection": scatter_about(key_of[5], (D, QKV), D ** -0.5, 0.1875, ((0, 128),)),
        "head_gain": jnp.clip(1.0 + 0.15 * jax.random.normal(key_of[6], (2 * HEAD_SIZE,), jnp.float32), 0.25, 1.75).astype(jnp.bfloat16),
        "output_weight": scatter_about(key_of[7], (QUERY_HEADS * HEAD_SIZE, D), (QUERY_HEADS * HEAD_SIZE // 32) ** -0.5, 0.75, ((0, 128),)),
        "feed_gain": jnp.clip(1.0 + 0.15 * jax.random.normal(key_of[8], (D,), jnp.float32), 0.25, 1.75).astype(jnp.bfloat16),
        "expansion": scatter_about(key_of[9], (D, 2 * FF), D ** -0.5, 0.1875, ((0, 128),)),
        "contraction": scatter_about(key_of[10], (FF, D), (FF // 4) ** -0.5, 0.21875, ((0, 128),)),
    }


EPS = 1e-06
THETA = 1000000.0
NEGATIVE = -1e+30
HIGHEST = lax.Precision.HIGHEST

@jax.custom_vjp
def reduced_precision(v):
    return lax.optimization_barrier(v.astype(jnp.bfloat16)).astype(jnp.float32)

@jax.custom_vjp
def low_back(v):
    return v

def low_keep(v):
    return (reduced_precision(v), None)

def low_pass(kept, grad):
    return (grad,)

def back_keep(v):
    return (v, None)

def back_low(kept, grad):
    return (reduced_precision(grad),)
reduced_precision.defvjp(low_keep, low_pass)
low_back.defvjp(back_keep, back_low)

def normalize(values, gain_vector):
    factor = lax.rsqrt(lax.optimization_barrier(jnp.mean(values * values, axis=-1, keepdims=True)) + EPS)
    return values * factor * gain_vector

def rotate(values, cosine, sine_table):
    half_size = values.shape[-1] // 2
    turned = jnp.concatenate([-values[..., half_size:], values[..., :half_size]], axis=-1)
    return values * cosine + turned * sine_table

def angles(places):
    indices = jnp.arange(HEAD_SIZE // 2, dtype=jnp.float32)
    inverse = 1.0 / THETA ** (indices * (2.0 / HEAD_SIZE))
    phases = places.astype(jnp.float32)[..., None] * inverse
    phases = jnp.concatenate([phases, phases], axis=-1)
    return (jnp.cos(phases), jnp.sin(phases))

def layer(inputs, segment_row, places, weights):
    attention_gain, projection, head_gain, output_weight, feed_gain, expansion, contraction = weights
    complete_length = inputs.shape[0]
    sharing_ratio = QUERY_HEADS // KEY_VALUE_HEADS
    normed_attn = reduced_precision(normalize(inputs, attention_gain))
    projected_rows = low_back(jnp.dot(normed_attn, projection, precision=HIGHEST))
    cosine, sine_table = angles(places)
    query_rows = projected_rows[:, :QUERY_HEADS * HEAD_SIZE].reshape(complete_length, KEY_VALUE_HEADS, sharing_ratio, HEAD_SIZE)
    key_portion = projected_rows[:, QUERY_HEADS * HEAD_SIZE:(QUERY_HEADS + KEY_VALUE_HEADS) * HEAD_SIZE].reshape(complete_length, KEY_VALUE_HEADS, HEAD_SIZE)
    value_portion = reduced_precision(projected_rows[:, (QUERY_HEADS + KEY_VALUE_HEADS) * HEAD_SIZE:].reshape(complete_length, KEY_VALUE_HEADS, HEAD_SIZE))
    query_rows = reduced_precision(rotate(normalize(query_rows, head_gain[:HEAD_SIZE]), cosine[:, None, None, :], sine_table[:, None, None, :]))
    key_portion = reduced_precision(rotate(normalize(key_portion, head_gain[HEAD_SIZE:]), cosine[:, None, :], sine_table[:, None, :]))
    scores = low_back(jnp.einsum('qgrd,kgd->grqk', query_rows, key_portion, precision=HIGHEST) * HEAD_SIZE ** (-0.5))
    token_index = jnp.arange(complete_length, dtype=jnp.int32)
    allowed = (token_index[None, :] <= token_index[:, None]) & (segment_row[None, :] == segment_row[:, None])
    attention = reduced_precision(jax.nn.softmax(jnp.where(allowed, scores, NEGATIVE), axis=-1))
    mixed_heads = jnp.einsum('grqk,kgd->qgrd', attention, value_portion, precision=HIGHEST).reshape(complete_length, QUERY_HEADS * HEAD_SIZE)
    mixed_heads = reduced_precision(low_back(mixed_heads))
    hidden = inputs + low_back(jnp.dot(mixed_heads, output_weight, precision=HIGHEST))
    normed_mlp = reduced_precision(normalize(hidden, feed_gain))
    gate_up = low_back(jnp.dot(normed_mlp, expansion, precision=HIGHEST))
    activation = reduced_precision(jax.nn.silu(gate_up[:, :FF]) * gate_up[:, FF:])
    return hidden + jnp.dot(activation, contraction, precision=HIGHEST)

def forward(inputs, weights, segments, positions):
    stepper = jax.checkpoint(layer)

    def advance(carry, member):
        return (carry, stepper(member[0], member[1], member[2], weights))
    _, outputs = lax.scan(advance, jnp.zeros((), jnp.float32), (inputs, segments, positions))
    return outputs

def reference(tokens, cotangent, segments, positions, attention_gain, projection, head_gain, output_weight, feed_gain, expansion, contraction):
    weights = tuple((member.astype(jnp.float32) for member in (attention_gain, projection, head_gain, output_weight, feed_gain, expansion, contraction)))

    def apply(inputs, params):
        return forward(inputs, params, segments, positions)
    outputs, pullback = jax.vjp(apply, tokens.astype(jnp.float32), weights)
    grad_tokens, grads = pullback(cotangent.astype(jnp.float32))
    return (outputs.astype(jnp.bfloat16), grad_tokens, grads[0], grads[1], grads[2], grads[3], grads[4], grads[5], grads[6])
```

```python
import jax
import jax.numpy as jnp
from jax import lax
from jax.experimental import pallas as pl
from jax.experimental.pallas import tpu as pltpu
from jax.sharding import PartitionSpec as P

F32 = jnp.float32
BF16 = jnp.bfloat16
MESH = pl.DeviceIdType.MESH
EPS = 1e-06
THETA = 1000000.0
NEGATIVE = -1e30
D = 1024
HEAD = 128
FF = 3072
FL = 768
TOK = 128
SEQ = 1024
QB = 256
SCALE = HEAD**-0.5


def dot(a, b, da=1, db=0):
    return lax.dot_general(a, b, (((da,), (db,)), ((), ())), preferred_element_type=F32)


def rows(start, size):
    return pl.ds(pl.multiple_of(start, size), size)


SCRATCH = dict(
    pa=((8, 8, 512), BF16),
    pw=((D, 512), BF16),
    ea=((8, 8, 1536), BF16),
    ew=((D, 1536), BF16),
    ow=((256, D), BF16),
    cb=((32, 24, D), BF16),
    cw=((FL, D), BF16),
    ga=((8, 24, 128), F32),
    gb=((8, 24, 128), F32),
    xs=((SEQ, D), BF16),
    ns=((SEQ, D), BF16),
    rx=((SEQ, 1), F32),
    pj=((SEQ, 384), F32),
    qs=((2, SEQ, HEAD), BF16),
    ks=((SEQ, HEAD), BF16),
    vs=((SEQ, HEAD), BF16),
    lse=((2, SEQ, 1), F32),
    mx=((SEQ, 256), BF16),
    ps=((SEQ, D), BF16),
    r1=((8, TOK, D), BF16),
    hid=((TOK, D), F32),
    nm=((512, D), BF16),
    dy=((512, D), BF16),
    gact=((512, FL), F32),
    act=((512, FL), BF16),
    ggu=((512, 1536), BF16),
    gs=((4, TOK, D), BF16),
    r2=((4, TOK, D), BF16),
    los=((4, TOK, D), BF16),
    r3=((4, TOK, D), BF16),
    gh=((TOK, D), F32),
    g8=((SEQ, D), BF16),
    gm=((SEQ, 256), BF16),
    dk=((SEQ, HEAD), F32),
    dv=((SEQ, HEAD), F32),
    dq=((2, QB, HEAD), F32),
    gp=((SEQ, 512), BF16),
    gacc=((24, 128), F32),
    gsum=((24, 128), F32),
    gfr=((24, 128), F32),
    gall=((24, 128), F32),
    attg=((1, D), F32),
    hgq=((1, HEAD), F32),
    hgk=((1, HEAD), F32),
    gg0=((24, 128), F32),
    gg1=((24, 128), F32),
    ggt=((24, 128), F32),
    ggt2=((24, 128), F32),
    gg2=((8, 24, 128), F32),
    gg3=((8, 24, 128), F32),
    ge=((2, 8, 64, 1536), BF16),
    ge1=((8, 64, 1536), BF16),
    ges=((8, 64, 1536), BF16),
    ge2=((8, 64, 1536), BF16),
    gef=((8, 8, 1536), BF16),
    ge3=((8, 8, 1536), BF16),
    gc=((2, 2, 8, 24, D), BF16),
    gc1=((2, 8, 24, D), BF16),
    gcs=((2, 2, 4, 24, D), BF16),
    gc2=((4, 4, 24, D), BF16),
    gcf=((4, 24, D), BF16),
    gc3=((4, 24, D), BF16),
    gpr=((2, 8, 64, 512), BF16),
    gp1=((8, 64, 512), BF16),
    gps=((8, 64, 512), BF16),
    gp2=((8, 64, 512), BF16),
    gpf=((8, 8, 512), BF16),
    gp3=((8, 8, 512), BF16),
    go=((2, 128, D), BF16),
    go1=((128, D), BF16),
    gos=((128, D), BF16),
    go2=((8, 16, D), BF16),
)
RECV = dict(
    gfr=1,
    pa=(8, 3), ea=(8, 2), ga=8, x=8, o1=8, c1=4, dy=4, pb=8, eb=8, gb=8, ps=8, es=8, os=1,
    c2=(4, 4), c3=2, r1=8, nm=4, r2=4, r3=4, g8=8, r4=8,
    e1=1, e2=8, e3=8, c4=2, c5=4, c6=4, p1=1, p2=8, p3=8, w1=1, w2=8, a1=1, a2=8, a3=8,
)
N_SEND = 320
NAMES = (
    ["x", "dyi", "pi", "oi", "ei", "ci", "gi", "segr", "segc", "cos", "sin"]
    + ["lo", "gt", "gpo", "goo", "geo", "gco", "ggo"]
    + list(SCRATCH)
    + ["s_" + n for n in RECV]
    + ["send"]
)


class Box:
    pass


def kernel(*refs):
    r = Box()
    for name, ref in zip(NAMES, refs, strict=True):
        setattr(r, name, ref)
    s, c = lax.axis_index("seq"), lax.axis_index("ctx")
    z, xh, core = s // 4, (s // 2) % 2, s % 2
    y, xl = c // 2, c % 2
    w = s // 2
    sib = 1 - core

    def at(zz, xx, cc, ctx):
        return {"seq": zz * 4 + xx * 2 + cc, "ctx": ctx}

    def on_w(ww, cc, ctx):
        return {"seq": ww * 2 + cc, "ctx": ctx}

    me_sib = on_w(w, sib, c)
    ctx_peer = [None] + [lax.rem(c + k, 8) for k in range(1, 8)]
    ctx_from = [None] + [lax.rem(c + 8 - k, 8) for k in range(1, 8)]
    w_peer = [None] + [lax.rem(w + k, 8) for k in range(1, 8)]
    w_from = [None] + [lax.rem(w + 8 - k, 8) for k in range(1, 8)]
    y_peer = [None] + [lax.rem(y + k, 4) for k in range(1, 4)]
    y_from = [None] + [lax.rem(y + 4 - k, 4) for k in range(1, 4)]
    x_line = [(xh, 1 - xl), (1 - xh, xl), (1 - xh, 1 - xl)]
    diag_o = c == w
    diag_c = y == z

    sends = []

    def copy(src, dst, sem, dev):
        cp = pltpu.make_async_remote_copy(
            src_ref=src, dst_ref=dst, send_sem=r.send.at[len(sends)], recv_sem=sem,
            device_id=dev, device_id_type=MESH,
        )
        return cp

    def send(src, dst, sem, dev, unless=None):
        cp = copy(src, dst, sem, dev)
        sends.append((cp, unless))
        if unless is None:
            cp.start()
        else:
            pl.when(jnp.logical_not(unless))(cp.start)

    def finish(some):
        for cp, unless in some:
            if unless is None:
                cp.wait_send()
            else:
                pl.when(jnp.logical_not(unless))(cp.wait_send)

    def got(dst, sem):
        pltpu.make_async_remote_copy(
            src_ref=dst, dst_ref=dst, send_sem=r.send.at[N_SEND - 1], recv_sem=sem,
            device_id=me_sib, device_id_type=MESH,
        ).wait_recv()

    bar = pltpu.get_barrier_semaphore()

    def greet(dev):
        pl.semaphore_signal(bar, inc=1, device_id=dev, device_id_type=MESH)

    greet(me_sib)
    for k in range(1, 8):
        greet({"seq": s, "ctx": ctx_peer[k]})
        greet(on_w(w_peer[k], core, c))
        greet(on_w(w_peer[k], core, w))
        greet(on_w(c, core, ctx_peer[k]))
    greet(at(z, x_line[2][0], core, 2 * y + x_line[2][1]))

    @pl.when(jnp.logical_not(diag_o))
    def _():
        greet(on_w(w, core, w))
        greet(on_w(c, core, c))

    for zz in range(4):

        @pl.when(jnp.logical_not(diag_c & (z == zz)))
        def _():
            greet(at(zz, xh, core, 2 * z + xl))
            greet(at(y, xh, core, 2 * zz + xl))

    pl.semaphore_wait(bar, 40 - jnp.where(diag_o, 2, 0) - jnp.where(diag_c, 2, 0))

    my = rows(c * TOK, TOK)
    for k in range(1, 8):
        to = ctx_peer[k]
        dev = {"seq": s, "ctx": to}
        send(r.gi, r.ga.at[c], r.s_ga.at[k], dev)
        for part, (start, size) in enumerate(((0, 256), (2048, 128), (3072, 128))):
            send(
                r.pi.at[:, pl.ds(pl.multiple_of(start + to * size, size), size)],
                r.pa.at[c, :, pl.ds((0, 256, 384)[part], size)],
                r.s_pa.at[k, part],
                dev,
            )
    for k in (1, 7, 2, 6, 3, 5, 4):
        send(r.x, r.xs.at[my], r.s_x.at[k], {"seq": s, "ctx": ctx_peer[k]})
    for k in range(1, 8):
        to = ctx_peer[k]
        for part in range(2):
            send(
                r.ei.at[:, pl.ds(pl.multiple_of(part * FF + (to // 2) * FL, FL), FL)],
                r.ea.at[c, :, pl.ds(part * FL, FL)],
                r.s_ea.at[k, part],
                {"seq": s, "ctx": to},
            )
    for k in range(8):
        send(
            r.oi,
            r.ow.at[pl.ds(pl.multiple_of(core * 128 + c * 16, 16), 16)],
            r.s_o1.at[c],
            on_w(lax.rem(w + k, 8), core, w),
            unless=diag_o if k == 0 else None,
        )
    for zz in range(4):
        send(
            r.ci,
            r.cb.at[(xh * 2 + core) * 8 + c],
            r.s_c1.at[y],
            at(zz, xh, core, 2 * z + xl),
            unless=diag_c & (z == zz),
        )

    r.xs[my, :] = r.x[...]
    for part, (start, size) in enumerate(((0, 256), (2048, 128), (3072, 128))):
        r.pa[c, :, pl.ds((0, 256, 384)[part], size)] = r.pi[
            :, pl.ds(pl.multiple_of(start + c * size, size), size)
        ]
    for part in range(2):
        r.ea[c, :, pl.ds(part * FL, FL)] = r.ei[
            :, pl.ds(pl.multiple_of(part * FF + y * FL, FL), FL)
        ]

    @pl.when(diag_o)
    def _():
        r.ow[pl.ds(pl.multiple_of(core * 128 + c * 16, 16), 16), :] = r.oi[...]

    @pl.when(diag_c)
    def _():
        r.cb[(xh * 2 + core) * 8 + c] = r.ci[...]

    total = r.gi[...]
    for k in range(1, 8):
        got(r.ga.at[ctx_from[k]], r.s_ga.at[k])
        total = total + r.ga[ctx_from[k]]
    r.gsum[...] = total
    for k in range(1, 8):
        for part, size in enumerate((256, 128, 128)):
            got(
                r.pa.at[ctx_from[k], :, pl.ds((0, 256, 384)[part], size)],
                r.s_pa.at[k, part],
            )
    mine = rows(s * 64, 64)
    r.pw[mine, :] = jnp.concatenate([r.pa[j].astype(F32) for j in range(8)], 0).astype(BF16)
    for k in range(1, 8):
        send(r.gsum, r.gb.at[w], r.s_gb.at[k], on_w(w_peer[k], core, c))
        send(r.pw.at[mine], r.pw.at[mine], r.s_pb.at[k], on_w(w_peer[k], core, c))
    send(r.pw.at[mine], r.pw.at[mine], r.s_ps.at[0], me_sib)
    for k in range(1, 8):
        for part in range(2):
            got(
                r.ea.at[ctx_from[k], :, pl.ds(part * FL, FL)],
                r.s_ea.at[k, part],
            )
    r.ew[mine, :] = jnp.concatenate([r.ea[j].astype(F32) for j in range(8)], 0).astype(BF16)
    for k in range(1, 8):
        send(r.ew.at[mine], r.ew.at[mine], r.s_eb.at[k], on_w(w_peer[k], core, c))
    send(r.ew.at[mine], r.ew.at[mine], r.s_es.at[0], me_sib)

    total = r.gsum[...]
    for k in range(1, 8):
        got(r.gb.at[w_from[k]], r.s_gb.at[k])
        total = total + r.gb[w_from[k]]
    r.gacc[...] = total
    send(r.gacc, r.gfr, r.s_gfr.at[0], me_sib)
    for k in range(1, 8):
        blk = r.pw.at[rows((w_from[k] * 2 + core) * 64, 64)]
        got(blk, r.s_pb.at[k])
        send(blk, blk, r.s_ps.at[k], me_sib)
    got(r.gfr, r.s_gfr.at[0])
    r.gall[...] = r.gacc[...] + r.gfr[...]
    got(r.pw.at[rows((w * 2 + sib) * 64, 64)], r.s_ps.at[0])
    for k in range(1, 8):
        got(r.pw.at[rows((w_from[k] * 2 + sib) * 64, 64)], r.s_ps.at[k])

    def wide(first):
        return jnp.concatenate([r.gall[first + j : first + j + 1, :] for j in range(8)], 1)

    gain_a, gain_f = wide(0), wide(8)
    gain_q, gain_k = r.gall[16:17, :], r.gall[17:18, :]

    def turn(v):
        return pltpu.roll(v, HEAD // 2, 1)

    def project(k, _):
        b = lax.rem(c + 8 - k, 8)
        at_b = rows(b * TOK, TOK)

        @pl.when(k > 0)
        def _():
            got(r.xs.at[at_b], r.s_x.at[k])

        v = r.xs[at_b, :].astype(F32)
        inv = lax.rsqrt(jnp.mean(v * v, axis=1, keepdims=True) + EPS)
        n = (v * inv * gain_a).astype(BF16)
        r.ns[at_b, :] = n
        r.rx[at_b, :] = inv
        out = dot(n, r.pw[...])
        r.pj[at_b, :] = out[:, :384]
        cosine, sine = r.cos[at_b, :], r.sin[at_b, :]
        for j in range(3):
            h = out[:, j * HEAD : (j + 1) * HEAD]
            hi = lax.rsqrt(jnp.mean(h * h, axis=1, keepdims=True) + EPS)
            h = h * hi * (gain_q if j < 2 else gain_k)
            h = (h * cosine + turn(h) * sine).astype(BF16)
            if j < 2:
                r.qs[j, at_b, :] = h
            else:
                r.ks[at_b, :] = h
        r.vs[at_b, :] = out[:, 384:].astype(BF16)
        return 0

    lax.fori_loop(0, 8, project, 0)

    my4 = rows(y * TOK, TOK)
    for k in range(1, 4):
        send(r.dyi, r.dy.at[my4], r.s_dy.at[k], {"seq": s, "ctx": 2 * y_peer[k] + xl})
    r.dy[my4, :] = r.dyi[...]

    for j in range(8):

        @pl.when(jnp.logical_not(diag_o & (c == j)))
        def _():
            got(r.ow.at[pl.ds(pl.multiple_of(core * 128 + j * 16, 16), 16)], r.s_o1.at[j])

    half = r.ow.at[rows(core * 128, 128)]
    send(half, half, r.s_os.at[0], me_sib)
    got(r.ow.at[rows(sib * 128, 128)], r.s_os.at[0])

    def mask(i):
        n, first = (i + 1) * QB, i * QB
        t = first + lax.broadcasted_iota(jnp.int32, (QB, n), 0)
        u = lax.broadcasted_iota(jnp.int32, (QB, n), 1)
        return (u <= t) & (r.segr[:, :n] == r.segc[first : first + QB, :])

    before = len(sends)
    for i in range(4):
        n, first = (i + 1) * QB, i * QB
        qr = pl.ds(first, QB)
        ok = mask(i)
        for h in range(2):
            sc = dot(r.qs[h, qr, :], r.ks[:n, :], 1, 1) * SCALE
            sc = jnp.where(ok, sc, NEGATIVE)
            top = jnp.max(sc, axis=1, keepdims=True)
            e = jnp.exp(sc - top)
            tot = jnp.sum(e, axis=1, keepdims=True)
            r.lse[h, qr, :] = top + jnp.log(tot)
            p = (e * (1.0 / tot)).astype(BF16)
            r.mx[qr, h * HEAD : (h + 1) * HEAD] = dot(p, r.vs[:n, :]).astype(BF16)
        r.ps[qr, :] = dot(r.mx[qr, :], r.ow[...]).astype(BF16)
        for to in (2 * i, 2 * i + 1):
            send(
                r.ps.at[pl.ds(to * TOK, TOK)], r.r1.at[c], r.s_r1.at[c],
                {"seq": s, "ctx": to}, unless=c == to,
            )

    r1_sends = sends[before:]

    for k in range(1, 8):
        blk = r.ew.at[rows((w_from[k] * 2 + core) * 64, 64)]
        got(blk, r.s_eb.at[k])
        send(blk, blk, r.s_es.at[k], me_sib)
    for j in range(4):
        blk = r.cb.at[(xh * 2 + core) * 8 + 2 * j + xl]

        @pl.when(jnp.logical_not(diag_c & (y == j)))
        def _():
            got(blk, r.s_c1.at[j])

        for n, (xx, ll) in enumerate(x_line):
            send(blk, blk, r.s_c2.at[n, j], at(z, xx, core, 2 * y + ll))

    hidden = r.x[...].astype(F32) + r.ps[my, :].astype(F32)
    for k in range(1, 8):
        got(r.r1.at[ctx_from[k]], r.s_r1.at[ctx_from[k]])
        hidden = hidden + r.r1[ctx_from[k]].astype(F32)
    r.hid[...] = hidden
    inv_h = lax.rsqrt(jnp.mean(hidden * hidden, axis=1, keepdims=True) + EPS)
    r.nm[my4, :] = (hidden * inv_h * gain_f).astype(BF16)
    for k in range(1, 4):
        send(
            r.nm.at[my4], r.nm.at[my4], r.s_nm.at[k], {"seq": s, "ctx": 2 * y_peer[k] + xl}
        )

    for n, (xx, ll) in enumerate(x_line):
        for j in range(4):
            got(r.cb.at[(xx * 2 + core) * 8 + 2 * j + ll], r.s_c2.at[n, j])
    for j in range(2):
        blk = r.cb.at[pl.ds(pl.multiple_of((2 * j + core) * 8, 8), 8)]
        send(blk, blk, r.s_c3.at[j], me_sib)
    for k in range(1, 4):
        got(r.dy.at[rows(y_from[k] * TOK, TOK)], r.s_dy.at[k])
    got(r.ew.at[rows((w * 2 + sib) * 64, 64)], r.s_es.at[0])
    for k in range(1, 8):
        got(r.ew.at[rows((w_from[k] * 2 + sib) * 64, 64)], r.s_es.at[k])
    for j in range(2):
        got(r.cb.at[pl.ds(pl.multiple_of((2 * j + sib) * 8, 8), 8)], r.s_c3.at[j])
    for j in range(16):
        r.cw[48 * j : 48 * j + 48, :] = jnp.concatenate(
            [r.cb[2 * j].astype(F32), r.cb[2 * j + 1].astype(F32)], 0
        ).astype(BF16)

    def grad_act(k, _):
        b = rows(k * TOK, TOK)
        r.gact[b, :] = dot(r.dy[b, :], r.cw[...], 1, 1)
        return 0

    lax.fori_loop(0, 4, grad_act, 0)

    for k in range(4):
        b4 = y if k == 0 else y_from[k]
        b = rows(b4 * TOK, TOK)
        if k:
            got(r.nm.at[b], r.s_nm.at[k])
        gu = dot(r.nm[b, :], r.ew[...])
        gate, up = gu[:, :FL], gu[:, FL:]
        sg = 1.0 / (1.0 + jnp.exp(-gate))
        sl = gate * sg
        r.act[b, :] = (sl * up).astype(BF16)
        gt = r.gact[b, :]
        r.ggu[b, :FL] = (gt * up * sg * (1.0 + gate * (1.0 - sg))).astype(BF16)
        r.ggu[b, FL:] = (gt * sl).astype(BF16)
        r.gs[b4] = dot(r.ggu[b, :], r.ew[...], 1, 1).astype(BF16)
        if k:
            send(r.gs.at[b4], r.r2.at[y], r.s_r2.at[k], {"seq": s, "ctx": 2 * b4 + xl})
    for k in range(4):
        b4 = y if k == 0 else y_from[k]
        r.los[b4] = dot(r.act[rows(b4 * TOK, TOK), :], r.cw[...]).astype(BF16)
        if k:
            send(r.los.at[b4], r.r3.at[y], r.s_r3.at[k], {"seq": s, "ctx": 2 * b4 + xl})

    for j in range(4):
        g = dot(r.nm[:, j * 256 : (j + 1) * 256], r.ggu[...], 0, 0).astype(BF16)
        for q in range(4):
            r.ge[q % 2, 2 * j + q // 2] = g[64 * q : 64 * q + 64, :]
    send(r.ge.at[sib], r.ge1, r.s_e1.at[0], me_sib)
    for j in range(2):
        g = dot(r.act[:, j * 384 : (j + 1) * 384], r.dy[...], 0, 0)
        for q in range(16):
            r.gc[q // 8, j, q % 8] = g[24 * q : 24 * q + 24, :].astype(BF16)
    for j in range(2):
        send(r.gc.at[sib, j], r.gc1.at[j], r.s_c4.at[j], me_sib)

    g_mlp = r.gs[y].astype(F32)
    for k in range(1, 4):
        got(r.r2.at[y_peer[k]], r.s_r2.at[k])
        g_mlp = g_mlp + r.r2[y_peer[k]].astype(F32)
    hidden = r.hid[...]
    inv_h = lax.rsqrt(jnp.mean(hidden * hidden, axis=1, keepdims=True) + EPS)
    unit = hidden * inv_h
    feed = jnp.sum(g_mlp * unit, axis=0, keepdims=True)
    g = g_mlp * gain_f
    g = r.dyi[...].astype(F32) + inv_h * (g - unit * jnp.mean(g * unit, axis=1, keepdims=True))
    r.gh[...] = g
    r.g8[my, :] = g.astype(BF16)
    for k in (1, 7, 2, 6, 3, 5, 4):
        send(r.g8.at[my], r.g8.at[my], r.s_g8.at[k], {"seq": s, "ctx": ctx_peer[k]})
    r.gg0[...] = jnp.zeros((24, 128), F32)
    for j in range(8):
        r.gg0[8 + j : 9 + j, :] = feed[:, 128 * j : 128 * j + 128]

    got(r.ge1, r.s_e1.at[0])

    def pair_e(j, _):
        r.ges[j] = (r.ge[core, j].astype(F32) + r.ge1[j].astype(F32)).astype(BF16)
        return 0

    lax.fori_loop(0, 8, pair_e, 0)
    for k in range(1, 8):
        send(r.ges.at[w_peer[k]], r.ge2.at[w], r.s_e2.at[k], on_w(w_peer[k], core, c))
    for j in range(2):
        got(r.gc1.at[j], r.s_c4.at[j])
        for q in range(8):
            r.gcs[j, q % 2, q // 2] = (
                r.gc[core, j, q].astype(F32) + r.gc1[j, q].astype(F32)
            ).astype(BF16)
    for n, (xx, ll) in enumerate(x_line):
        send(
            r.gcs.at[xx, ll], r.gc2.at[xh * 2 + xl], r.s_c5.at[n],
            at(z, xx, core, 2 * y + ll),
        )

    total = r.hid[...] + r.los[y].astype(F32)
    for k in range(1, 4):
        got(r.r3.at[y_peer[k]], r.s_r3.at[k])
        total = total + r.r3[y_peer[k]].astype(F32)
    r.lo[...] = total.astype(BF16)

    for k in range(1, 8):
        got(r.g8.at[rows(ctx_from[k] * TOK, TOK)], r.s_g8.at[k])

    def grad_mixed(j, _):
        b = rows(j * QB, QB)
        r.gm[b, :] = dot(r.g8[b, :], r.ow[...], 1, 1).astype(BF16)
        return 0

    lax.fori_loop(0, 4, grad_mixed, 0)
    finish(r1_sends)
    r.attg[...] = jnp.zeros((1, D), F32)
    r.hgq[...] = jnp.zeros((1, HEAD), F32)
    r.hgk[...] = jnp.zeros((1, HEAD), F32)
    for i in (3, 2, 1, 0):
        n, first = (i + 1) * QB, i * QB
        qr = pl.ds(first, QB)
        ok = mask(i)
        for h in range(2):
            q, kk = r.qs[h, qr, :], r.ks[:n, :]
            gmh = r.gm[qr, h * HEAD : (h + 1) * HEAD]
            sc = dot(q, kk, 1, 1) * SCALE
            p = jnp.where(ok, jnp.exp(sc - r.lse[h, qr, :]), 0.0)
            gat = dot(gmh, r.vs[:n, :], 1, 1)
            ds = (p * (gat - jnp.sum(p * gat, axis=1, keepdims=True))).astype(BF16)
            r.dq[h] = dot(ds, kk) * SCALE
            dk = dot(ds, q, 0, 0) * SCALE
            dv = dot(p.astype(BF16), gmh, 0, 0)
            if i == 3 and h == 0:
                r.dk[...] = dk
                r.dv[...] = dv
            else:
                r.dk[:n, :] += dk
                r.dv[:n, :] += dv
        cosine, sine = r.cos[qr, :], r.sin[qr, :]
        for j in range(3):
            wv = r.dq[j] if j < 2 else r.dk[qr, :]
            gn = wv * cosine - turn(wv) * sine
            v = r.pj[qr, j * HEAD : (j + 1) * HEAD]
            inv = lax.rsqrt(jnp.mean(v * v, axis=1, keepdims=True) + EPS)
            unit = v * inv
            acc = r.hgq if j < 2 else r.hgk
            acc[...] += jnp.sum(gn * unit, axis=0, keepdims=True)
            t = gn * (gain_q if j < 2 else gain_k)
            gx = inv * (t - unit * jnp.mean(t * unit, axis=1, keepdims=True))
            r.gp[qr, j * HEAD : (j + 1) * HEAD] = gx.astype(BF16)
        r.gp[qr, 384:512] = r.dv[qr, :].astype(BF16)
        part = dot(r.gp[qr, :], r.pw[...], 1, 1)
        r.ps[qr, :] = part.astype(BF16)
        for to in (2 * i, 2 * i + 1):
            send(
                r.ps.at[pl.ds(to * TOK, TOK)], r.r1.at[c], r.s_r4.at[c],
                {"seq": s, "ctx": to}, unless=c == to,
            )
        r.attg[...] += jnp.sum(
            part * (r.xs[qr, :].astype(F32) * r.rx[qr, :]), axis=0, keepdims=True
        )

    for j in range(8):
        r.gg0[j : j + 1, :] = r.attg[:, 128 * j : 128 * j + 128]
    r.gg0[16:17, :] = r.hgq[...]
    r.gg0[17:18, :] = r.hgk[...]
    send(r.gg0, r.gg1, r.s_a1.at[0], me_sib)

    for j in range(4):
        g = dot(r.ns[:, j * 256 : (j + 1) * 256], r.gp[...], 0, 0).astype(BF16)
        for q in range(4):
            r.gpr[q % 2, 2 * j + q // 2] = g[64 * q : 64 * q + 64, :]
    send(r.gpr.at[sib], r.gp1, r.s_p1.at[0], me_sib)
    r.go[0] = dot(r.mx[:, :128], r.g8[...], 0, 0).astype(BF16)
    r.go[1] = dot(r.mx[:, 128:], r.g8[...], 0, 0).astype(BF16)
    send(r.go.at[sib], r.go1, r.s_w1.at[0], me_sib)

    got(r.gg1, r.s_a1.at[0])
    r.ggt[...] = r.gg0[...] + r.gg1[...]
    for k in range(1, 8):
        send(r.ggt, r.gg2.at[w], r.s_a2.at[k], on_w(w_peer[k], core, c))

    got(r.gp1, r.s_p1.at[0])
    for j in range(8):
        r.gps[j] = (r.gpr[core, j].astype(F32) + r.gp1[j].astype(F32)).astype(BF16)
    for k in range(1, 8):
        send(r.gps.at[w_peer[k]], r.gp2.at[w], r.s_p2.at[k], on_w(w_peer[k], core, c))
    got(r.go1, r.s_w1.at[0])
    r.gos[...] = (r.go[core].astype(F32) + r.go1[...].astype(F32)).astype(BF16)
    for j in range(8):
        send(
            r.gos.at[pl.ds(16 * j, 16)], r.go2.at[w], r.s_w2.at[w], on_w(c, core, j),
            unless=diag_o & (c == j),
        )

    @pl.when(diag_o)
    def _():
        r.go2[w] = r.gos[rows(16 * c, 16), :]

    total = r.ges[w].astype(F32)
    for k in range(1, 8):
        got(r.ge2.at[w_from[k]], r.s_e2.at[k])
        total = total + r.ge2[w_from[k]].astype(F32)
    for j in range(8):
        r.gef[j] = total[8 * j : 8 * j + 8, :].astype(BF16)
    for k in range(1, 8):
        send(r.gef.at[ctx_peer[k]], r.ge3.at[c], r.s_e3.at[k], {"seq": s, "ctx": ctx_peer[k]})
    r.ge3[c] = r.gef[c]
    for n, (xx, ll) in enumerate(x_line):
        got(r.gc2.at[xx * 2 + ll], r.s_c5.at[n])
    for j in range(4):
        total = r.gcs[xh, xl, j].astype(F32)
        for xx, ll in x_line:
            total = total + r.gc2[xx * 2 + ll, j].astype(F32)
        r.gcf[j] = total.astype(BF16)
        send(
            r.gcf.at[j], r.gc3.at[z], r.s_c6.at[z], at(y, xh, core, 2 * j + xl),
            unless=diag_c & (y == j),
        )

    @pl.when(diag_c)
    def _():
        r.gc3[z] = r.gcf[y]

    total = r.ggt[...]
    for k in range(1, 8):
        got(r.gg2.at[w_from[k]], r.s_a2.at[k])
        total = total + r.gg2[w_from[k]]
    r.ggt2[...] = total
    for k in range(1, 8):
        send(r.ggt2, r.gg3.at[c], r.s_a3.at[k], {"seq": s, "ctx": ctx_peer[k]})

    total = r.gps[w].astype(F32)
    for k in range(1, 8):
        got(r.gp2.at[w_from[k]], r.s_p2.at[k])
        total = total + r.gp2[w_from[k]].astype(F32)
    for j in range(8):
        r.gpf[j] = total[8 * j : 8 * j + 8, :].astype(BF16)
    for k in range(1, 8):
        send(r.gpf.at[ctx_peer[k]], r.gp3.at[c], r.s_p3.at[k], {"seq": s, "ctx": ctx_peer[k]})
    r.gp3[c] = r.gpf[c]

    for k in range(1, 8):
        got(r.ge3.at[ctx_from[k]], r.s_e3.at[k])
    for j in range(4):
        t = r.ge3[2 * j].astype(F32) + r.ge3[2 * j + 1].astype(F32)
        r.geo[:, j * FL : (j + 1) * FL] = t[:, :FL]
        r.geo[:, FF + j * FL : FF + (j + 1) * FL] = t[:, FL:]
    for j in range(4):

        @pl.when(jnp.logical_not(diag_c & (z == j)))
        def _():
            got(r.gc3.at[j], r.s_c6.at[j])

    r.gco[...] = (r.gc3[0].astype(F32) + r.gc3[1].astype(F32)) + (
        r.gc3[2].astype(F32) + r.gc3[3].astype(F32)
    )
    total = jnp.zeros((16, D), F32)
    for j in range(8):

        @pl.when(jnp.logical_not(diag_o & (w == j)))
        def _():
            got(r.go2.at[j], r.s_w2.at[j])

        total = total + r.go2[j].astype(F32)
    r.goo[...] = total

    total = r.gh[...]
    g = r.ps[my, :].astype(F32)
    for k in range(1, 8):
        got(r.r1.at[ctx_from[k]], r.s_r4.at[ctx_from[k]])
        g = g + r.r1[ctx_from[k]].astype(F32)
    v = r.x[...].astype(F32)
    inv = lax.rsqrt(jnp.mean(v * v, axis=1, keepdims=True) + EPS)
    unit = v * inv
    g = g * gain_a
    r.gt[...] = total + inv * (g - unit * jnp.mean(g * unit, axis=1, keepdims=True))

    for k in range(1, 8):
        got(r.gp3.at[ctx_from[k]], r.s_p3.at[k])
    for j in range(8):
        t = r.gp3[j].astype(F32)
        r.gpo[:, j * 256 : (j + 1) * 256] = t[:, :256]
        r.gpo[:, 2048 + j * 128 : 2048 + (j + 1) * 128] = t[:, 256:384]
        r.gpo[:, 3072 + j * 128 : 3072 + (j + 1) * 128] = t[:, 384:]
    total = r.ggt2[...]
    for k in range(1, 8):
        got(r.gg3.at[ctx_from[k]], r.s_a3.at[k])
        total = total + r.gg3[ctx_from[k]]
    r.ggo[...] = total

    finish(sends[:before] + sends[before + len(r1_sends) :])


def per_device(x, dy, segments, positions, ag, proj, hg, out, fg, expn, con):
    del positions
    s, c = lax.axis_index("seq"), lax.axis_index("ctx")
    dev = 8 * s + c
    flat = jnp.zeros((3072,), F32)
    flat = lax.dynamic_update_slice(flat, ag.astype(F32), (8 * dev,))
    flat = lax.dynamic_update_slice(flat, fg.astype(F32), (1024 + 8 * dev,))
    flat = lax.dynamic_update_slice(flat, hg.astype(F32), (2048 + 2 * dev,))
    seg = segments.reshape(SEQ)
    start = jnp.sum((seg[None, :] < seg[:, None]).astype(jnp.int32), axis=1)
    place = (jnp.arange(SEQ, dtype=jnp.int32) - start).astype(F32)
    index = jnp.arange(HEAD // 2, dtype=F32)
    phase = place[:, None] * (1.0 / THETA ** (index * (2.0 / HEAD)))
    cosine, sine = jnp.cos(phase), jnp.sin(phase)
    cosine = jnp.concatenate([cosine, cosine], 1)
    sine = jnp.concatenate([-sine, sine], 1)
    vmem = pl.BlockSpec(memory_space=pltpu.VMEM)
    scratch = [pltpu.VMEM(shape, kind) for shape, kind in SCRATCH.values()]
    sems = [pltpu.SemaphoreType.DMA(n if isinstance(n, tuple) else (n,)) for n in RECV.values()]
    res = pl.pallas_call(
        kernel,
        name="layer",
        out_shape=(
            jax.ShapeDtypeStruct((TOK, D), BF16),
            jax.ShapeDtypeStruct((TOK, D), F32),
            jax.ShapeDtypeStruct((8, 4096), F32),
            jax.ShapeDtypeStruct((16, D), F32),
            jax.ShapeDtypeStruct((8, 6144), F32),
            jax.ShapeDtypeStruct((24, D), F32),
            jax.ShapeDtypeStruct((24, 128), F32),
        ),
        in_specs=[vmem] * 11,
        out_specs=(vmem,) * 7,
        scratch_shapes=scratch + sems + [pltpu.SemaphoreType.DMA((N_SEND,))],
        compiler_params=pltpu.CompilerParams(
            collective_id=0, has_side_effects=True, vmem_limit_bytes=62 * 2**20
        ),
    )(
        x.reshape(TOK, D), dy.reshape(TOK, D), proj, out, expn, con, flat.reshape(24, 128),
        seg.reshape(1, SEQ), seg.reshape(SEQ, 1), cosine, sine,
    )
    lo, gt, gpo, goo, geo, gco, ggo = res
    gains = ggo.reshape(3072)
    return (
        lo.reshape(1, TOK, D),
        gt.reshape(1, TOK, D),
        lax.dynamic_slice(gains, (8 * dev,), (8,)),
        gpo,
        lax.dynamic_slice(gains, (2048 + 2 * dev,), (2,)),
        goo,
        lax.dynamic_slice(gains, (1024 + 8 * dev,), (8,)),
        geo,
        gco,
    )


def solution(mesh):
    return jax.shard_map(
        per_device,
        mesh=mesh,
        in_specs=(
            P("seq", "ctx", None),
            P("seq", "ctx", None),
            P("seq", None),
            P("seq", "ctx"),
            P(("seq", "ctx")),
            P(("seq", "ctx"), None),
            P(("seq", "ctx")),
            P(("seq", "ctx"), None),
            P(("seq", "ctx")),
            P(("seq", "ctx"), None),
            P(("seq", "ctx"), None),
        ),
        out_specs=(
            P("seq", "ctx", None),
            P("seq", "ctx", None),
            P(("seq", "ctx")),
            P(("seq", "ctx"), None),
            P(("seq", "ctx")),
            P(("seq", "ctx"), None),
            P(("seq", "ctx")),
            P(("seq", "ctx"), None),
            P(("seq", "ctx"), None),
        ),
        check_vma=False,
    )
```

```python
import math

import jax
import jax.numpy as jnp
from jax import lax
from jax.experimental import pallas as pl
from jax.experimental.pallas import tpu as pltpu
from jax.sharding import PartitionSpec as P

F32 = jnp.float32
BF16 = jnp.bfloat16
MESH = pl.DeviceIdType.MESH
EPS = 1e-06
THETA = 1000000.0
NEGATIVE = -1e30
D = 1024
HEAD = 128
FF = 3072
FL = 768
TOK = 128
SEQ = 1024
QB = 256
SCALE = HEAD**-0.5


def dot(a, b, da=1, db=0):
    return lax.dot_general(a, b, (((da,), (db,)), ((), ())), preferred_element_type=F32)


def rows(start, size):
    return pl.ds(pl.multiple_of(start, size), size)


SCRATCH = dict(
    pa=((8, 8, D), BF16),
    pw=((D, D), BF16),
    ea=((8, 8, 1536), BF16),
    ew=((D, 1536), BF16),
    ow=((512, D), BF16),
    cb=((32, 24, D), BF16),
    cw=((FL, D), BF16),
    gi=((24, 128), F32),
    ga=((8, 24, 128), F32),
    gb=((8, 24, 128), F32),
    gsum=((24, 128), F32),
    gacc=((24, 128), F32),
    gfr=((24, 128), F32),
    gall=((24, 128), F32),
    cos=((512, HEAD), F32),
    sin=((512, HEAD), F32),
    segc=((QB, 128), jnp.int32),
    xs=((512, D), BF16),
    ns=((512, D), BF16),
    pj=((512, 768), F32),
    qs=((2, 4, QB, HEAD), BF16),
    kv=((8, 4, TOK, HEAD), BF16),
    mx=((512, 512), BF16),
    ps=((4, TOK, D), BF16),
    r1=((4, TOK, D), BF16),
    hid=((TOK, D), F32),
    nm=((512, D), BF16),
    dy=((512, D), BF16),
    act=((512, FL), BF16),
    ggu=((512, 1536), BF16),
    gs=((4, TOK, D), BF16),
    r2=((4, TOK, D), BF16),
    los=((4, TOK, D), BF16),
    r3=((4, TOK, D), BF16),
    gh=((TOK, D), F32),
    g4=((512, D), BF16),
    gm=((2, 4, QB, HEAD), BF16),
    f4=((4096, HEAD), F32),
    dq=((2, 4, QB, HEAD), F32),
    ds=((2, 4, 2, TOK, HEAD), BF16),
    dr=((2, 4, 2, TOK, HEAD), BF16),
    gp=((512, D), BF16),
    attg=((1, D), F32),
    hgq=((1, HEAD), F32),
    hgk=((1, HEAD), F32),
    gg0=((24, 128), F32),
    gg1=((24, 128), F32),
    ggt=((24, 128), F32),
    ggt2=((24, 128), F32),
    gg2=((8, 24, 128), F32),
    gg3=((8, 24, 128), F32),
    ge=((2, 8, 64, 1536), BF16),
    ge1=((8, 64, 1536), BF16),
    ges=((8, 64, 1536), BF16),
    ge2=((4, 2, 64, 1536), BF16),
    get=((2, 64, 1536), BF16),
    gex=((64, 1536), BF16),
    gef=((8, 8, 1536), BF16),
    ge3=((8, 8, 1536), BF16),
    gc=((2, 2, 8, 24, D), BF16),
    gc1=((2, 8, 24, D), BF16),
    gcs=((2, 2, 4, 24, D), BF16),
    gc2=((4, 4, 24, D), BF16),
    gcf=((4, 24, D), BF16),
    gc3=((4, 24, D), BF16),
    go=((2, 2, 8, 16, D), BF16),
    go1=((2, 8, 16, D), BF16),
    gos=((2, 2, 4, 16, D), BF16),
    go2=((4, 4, 16, D), BF16),
    gof=((4, 16, D), BF16),
    go3=((4, 16, D), BF16),
    gpx=((1536, D), BF16),
    gp1=((512, D), BF16),
    gp2=((8, 64, D), BF16),
    gpf=((8, 8, D), BF16),
    gp3=((8, 8, D), BF16),
)
RECV = dict(
    pa=(8, 3), ea=(8, 2), ga=8, gb=8, gfr=1, x=4, dy=4, pb=(2, 8), eb=(2, 4), ps=(2, 8), es=8,
    o1=4, o2=(4, 4), o3=2, c1=4, c2=(4, 4), c3=2, kv=4, r1=4, nm=4, r2=4, r3=4, g4=4, dr=(2, 4), r4=4,
    e1=1, e2=4, ex=1, e3=8, c4=2, c5=4, c6=4, o4=2, o5=4, o6=4, p1=2, p2=(2, 8), p3=8, a1=1, a2=8, a3=8,
)
N_SEND = 320
NAMES = (
    ["x", "dyi", "pi", "oi", "ei", "ci", "agi", "fgi", "hgi", "segr"]
    + ["lo", "gt", "gpo", "goo", "geo", "gco", "ggo"]
    + list(SCRATCH)
    + ["s_" + n for n in RECV]
    + ["send", "loc"]
)
PLACES = (
    (0, (0, 256)), (256, (512, 128)), (384, (768, 128)),
    (512, (256, 256)), (768, (640, 128)), (896, (896, 128)),
)
HEADS = (0, 128, 256, 384, 512, 768)
PCOLS = ((0, 512, 0), (2048, 256, 512), (3072, 256, 768))


class Box:
    pass


def kernel(*refs):
    r = Box()
    for name, ref in zip(NAMES, refs, strict=True):
        setattr(r, name, ref)
    s, c = lax.axis_index("seq"), lax.axis_index("ctx")
    z, xh, core = s // 4, (s // 2) % 2, s % 2
    y, xl = c // 2, c % 2
    w = s // 2
    sib = 1 - core

    def at(zz, xx, cc, ctx):
        return {"seq": zz * 4 + xx * 2 + cc, "ctx": ctx}

    def on_w(ww, cc, ctx):
        return {"seq": ww * 2 + cc, "ctx": ctx}

    me_sib = on_w(w, sib, c)
    ctx_peer = [None] + [lax.rem(c + k, 8) for k in range(1, 8)]
    ctx_from = [None] + [lax.rem(c + 8 - k, 8) for k in range(1, 8)]
    w_peer = [None] + [lax.rem(w + k, 8) for k in range(1, 8)]
    w_from = [None] + [lax.rem(w + 8 - k, 8) for k in range(1, 8)]
    y_peer = [None] + [lax.rem(y + k, 4) for k in range(1, 4)]
    y_from = [None] + [lax.rem(y + 4 - k, 4) for k in range(1, 4)]
    z_peer = [None] + [lax.rem(z + k, 4) for k in range(1, 4)]
    z_from = [None] + [lax.rem(z + 4 - k, 4) for k in range(1, 4)]
    x_line = [(xh, 1 - xl), (1 - xh, xl), (1 - xh, 1 - xl)]
    diag = y == z

    def e_block(zz, xx, cc):
        return r.ew.at[rows((zz * 4 + xx * 2 + cc) * 64, 64)]

    sends = []

    def copy(src, dst, sem, dev):
        cp = pltpu.make_async_remote_copy(
            src_ref=src, dst_ref=dst, send_sem=r.send.at[len(sends)], recv_sem=sem,
            device_id=dev, device_id_type=MESH,
        )
        return cp

    def send(src, dst, sem, dev, unless=None):
        cp = copy(src, dst, sem, dev)
        sends.append((cp, unless))
        if unless is None:
            cp.start()
        else:
            pl.when(jnp.logical_not(unless))(cp.start)

    def finish(some):
        for cp, unless in some:
            if unless is None:
                cp.wait_send()
            else:
                pl.when(jnp.logical_not(unless))(cp.wait_send)

    def got(dst, sem):
        pltpu.make_async_remote_copy(
            src_ref=dst, dst_ref=dst, send_sem=r.send.at[N_SEND - 1], recv_sem=sem,
            device_id=me_sib, device_id_type=MESH,
        ).wait_recv()

    bar = pltpu.get_barrier_semaphore()

    def greet(dev):
        pl.semaphore_signal(bar, inc=1, device_id=dev, device_id_type=MESH)

    greet(me_sib)
    for k in range(1, 8):
        greet({"seq": s, "ctx": ctx_peer[k]})
        greet(on_w(w_peer[k], core, c))
    greet(at(z, x_line[2][0], core, 2 * y + x_line[2][1]))
    for zz in range(4):

        @pl.when(jnp.logical_not(diag & (z == zz)))
        def _():
            greet(at(zz, xh, core, 2 * z + xl))
            greet(at(y, xh, core, 2 * zz + xl))

    own = []

    def own_copy(src, dst):
        cp = pltpu.make_async_copy(src, dst, r.loc.at[len(own)])
        own.append(cp)
        cp.start()

    my4 = rows(y * TOK, TOK)
    own_copy(r.x, r.xs.at[my4])
    own_copy(r.dyi, r.dy.at[my4])
    for start, size, place in PCOLS:
        own_copy(
            r.pi.at[:, pl.ds(pl.multiple_of(start + y * size, size), size)],
            r.pa.at[c, :, pl.ds(place, size)],
        )
    for part in range(2):
        own_copy(
            r.ei.at[:, pl.ds(pl.multiple_of(part * FF + y * FL, FL), FL)],
            r.ea.at[c, :, pl.ds(part * FL, FL)],
        )

    tile_row = lax.broadcasted_iota(jnp.int32, (8, 128), 0)
    tile_lane = lax.broadcasted_iota(jnp.int32, (8, 128), 1)
    flat = tile_row * 128 + tile_lane
    place = 8 * s + c
    for n, (ref, size) in enumerate(((r.agi, 8), (r.fgi, 8), (r.hgi, 2))):
        values = ref[...].astype(F32)
        tile = jnp.zeros((8, 128), F32)
        for j in range(size):
            tile = jnp.where(flat == place * size + j, values[:, j : j + 1], tile)
        r.gi[8 * n : 8 * n + 8, :] = tile

    pl.semaphore_wait(bar, 24 - jnp.where(diag, 2, 0))

    for part in (1, 2, 0):
        start, size, place = PCOLS[part]
        for k in range(1, 8):
            to = ctx_peer[k]
            send(
                r.pi.at[:, pl.ds(pl.multiple_of(start + (to // 2) * size, size), size)],
                r.pa.at[c, :, pl.ds(place, size)],
                r.s_pa.at[k, part],
                {"seq": s, "ctx": to},
            )
    for k in (1, 3, 2):
        send(r.x, r.xs.at[my4], r.s_x.at[k], {"seq": s, "ctx": 2 * y_peer[k] + xl})
    for k in range(1, 8):
        send(r.gi, r.ga.at[c], r.s_ga.at[k], {"seq": s, "ctx": ctx_peer[k]})

    @pl.when(diag)
    def _():
        a = pltpu.make_async_copy(
            r.oi,
            r.ow.at[pl.ds(pl.multiple_of(((xh * 2 + core) * 8 + c) * 16, 16), 16)],
            r.loc.at[14],
        )
        b = pltpu.make_async_copy(r.ci, r.cb.at[(xh * 2 + core) * 8 + c], r.loc.at[15])
        a.start()
        b.start()
        a.wait()
        b.wait()

    for cp in own:
        cp.wait()

    lane = lax.broadcasted_iota(jnp.int32, (1, HEAD), 1)
    index = jnp.where(lane < HEAD // 2, lane, lane - HEAD // 2).astype(F32)
    inverse = jnp.exp(index * (-2.0 / HEAD * math.log(THETA)))
    sign = jnp.where(lane < HEAD // 2, -1.0, 1.0)
    eye = lax.broadcasted_iota(jnp.int32, (TOK, TOK), 0) == lax.broadcasted_iota(
        jnp.int32, (TOK, TOK), 1
    )
    for j in range(4):
        b = pl.ds(j * TOK, TOK)
        seg = r.segr[:, pl.ds(pl.multiple_of((2 * j + xl) * TOK, TOK), TOK)]
        seg = jnp.sum(jnp.where(eye, seg.astype(F32), 0.0), axis=1, keepdims=True)
        r.segc[:, j : j + 1] = jnp.concatenate([seg, seg], 0).astype(jnp.int32)
        before = jnp.sum((r.segr[...].astype(F32) < seg).astype(F32), axis=1, keepdims=True)
        t = lax.broadcasted_iota(jnp.int32, (TOK, 1), 0) + (2 * j + xl) * TOK
        phase = (t.astype(F32) - before) * inverse
        r.cos[b, :] = jnp.cos(phase)
        r.sin[b, :] = jnp.sin(phase) * sign

    own_rows = rows(s * 64, 64)
    kv_half, q_half = pl.ds(512, 512), pl.ds(0, 512)

    def spread(n, half):
        blk = r.pw.at[own_rows, half]
        for k in range(1, 8):
            send(blk, blk, r.s_pb.at[n, k], on_w(w_peer[k], core, c))
        send(blk, blk, r.s_ps.at[n, 0], me_sib)

    def pass_on(n, half):
        for k in range(1, 8):
            blk = r.pw.at[rows((w_from[k] * 2 + core) * 64, 64), half]
            got(blk, r.s_pb.at[n, k])
            send(blk, blk, r.s_ps.at[n, k], me_sib)

    def from_sibling(n, half):
        for k in range(8):
            ww = w if k == 0 else w_from[k]
            got(r.pw.at[rows((ww * 2 + sib) * 64, 64), half], r.s_ps.at[n, k])

    def joined(start, size):
        return jnp.concatenate(
            [r.pa[j, :, start : start + size].astype(F32) for j in range(8)], 0
        ).astype(BF16)

    for part in (1, 2):
        for k in range(1, 8):
            _, size, place = PCOLS[part]
            got(r.pa.at[ctx_from[k], :, pl.ds(place, size)], r.s_pa.at[k, part])
    for g in range(2):
        r.pw[own_rows, 512 + g * 256 : 640 + g * 256] = joined(512 + g * 128, 128)
        r.pw[own_rows, 640 + g * 256 : 768 + g * 256] = joined(768 + g * 128, 128)
    spread(0, kv_half)
    for k in range(1, 8):
        got(r.pa.at[ctx_from[k], :, pl.ds(0, 512)], r.s_pa.at[k, 0])
    r.pw[own_rows, 0:512] = joined(0, 512)
    total = r.gi[...]
    for k in range(1, 8):
        got(r.ga.at[ctx_from[k]], r.s_ga.at[k])
        total = total + r.ga[ctx_from[k]]
    r.gsum[...] = total
    for k in range(1, 8):
        send(r.gsum, r.gb.at[w], r.s_gb.at[k], on_w(w_peer[k], core, c))
    spread(1, q_half)
    for zz in range(4):
        send(
            r.oi,
            r.ow.at[pl.ds(pl.multiple_of(((xh * 2 + core) * 8 + c) * 16, 16), 16)],
            r.s_o1.at[y],
            at(zz, xh, core, 2 * z + xl),
            unless=diag & (z == zz),
        )
    pass_on(0, kv_half)
    total = r.gsum[...]
    for k in range(1, 8):
        got(r.gb.at[w_from[k]], r.s_gb.at[k])
        total = total + r.gb[w_from[k]]
    r.gacc[...] = total
    send(r.gacc, r.gfr, r.s_gfr.at[0], me_sib)
    for k in range(1, 8):
        to = ctx_peer[k]
        for part in range(2):
            send(
                r.ei.at[:, pl.ds(pl.multiple_of(part * FF + (to // 2) * FL, FL), FL)],
                r.ea.at[c, :, pl.ds(part * FL, FL)],
                r.s_ea.at[k, part],
                {"seq": s, "ctx": to},
            )
    got(r.gfr, r.s_gfr.at[0])
    r.gall[...] = r.gacc[...] + r.gfr[...]
    from_sibling(0, kv_half)

    def wide(first):
        return jnp.concatenate([r.gall[first + j : first + j + 1, :] for j in range(8)], 1)

    gain_a, gain_f = wide(0), wide(8)
    gain_q, gain_k = r.gall[16:17, :], r.gall[17:18, :]

    def turn(v):
        return pltpu.roll(v, HEAD // 2, 1)

    x_partner = {"seq": s, "ctx": 2 * y + 1 - xl}
    def headed(u, b, h):
        r.pj[b, h * HEAD : (h + 1) * HEAD] = u
        ui = lax.rsqrt(jnp.mean(u * u, axis=1, keepdims=True) + EPS)
        u = u * ui * (gain_q if h < 4 else gain_k)
        return (u * r.cos[b, :] + turn(u) * r.sin[b, :]).astype(BF16)

    for k in (0, 1, 3, 2):
        j = y if k == 0 else y_from[k]
        b = rows(j * TOK, TOK)
        if k:
            got(r.xs.at[b], r.s_x.at[k])
        v = r.xs[b, :].astype(F32)
        inv = lax.rsqrt(jnp.mean(v * v, axis=1, keepdims=True) + EPS)
        n = (v * inv * gain_a).astype(BF16)
        r.ns[b, :] = n
        out = dot(n, r.pw[:, 512:])
        mine = 2 * j + xl
        for g in range(2):
            r.kv[mine, g] = headed(out[:, g * 256 : g * 256 + HEAD], b, 4 + g)
            r.kv[mine, 2 + g] = out[:, g * 256 + HEAD : g * 256 + 256].astype(BF16)
        send(r.kv.at[mine], r.kv.at[mine], r.s_kv.at[j], x_partner)

    for k in range(1, 8):
        for part in range(2):
            got(r.ea.at[ctx_from[k], :, pl.ds(part * FL, FL)], r.s_ea.at[k, part])
    r.ew[own_rows, :] = jnp.concatenate([r.ea[j].astype(F32) for j in range(8)], 0).astype(BF16)
    own_e = r.ew.at[own_rows]
    for k in (1, 3, 2):
        send(own_e, own_e, r.s_eb.at[0, k], at(z_peer[k], xh, core, c))
    send(own_e, own_e, r.s_es.at[0], me_sib)
    for zz in range(4):
        send(
            r.ci,
            r.cb.at[(xh * 2 + core) * 8 + c],
            r.s_c1.at[y],
            at(zz, xh, core, 2 * z + xl),
            unless=diag & (z == zz),
        )

    for j in range(4):
        blk = r.ow.at[pl.ds(pl.multiple_of(((xh * 2 + core) * 8 + 2 * j + xl) * 16, 16), 16)]

        @pl.when(jnp.logical_not(diag & (y == j)))
        def _():
            got(blk, r.s_o1.at[j])

        for n, (xx, ll) in enumerate(x_line):
            send(blk, blk, r.s_o2.at[n, j], at(z, xx, core, 2 * y + ll))
    pass_on(1, q_half)
    from_sibling(1, q_half)
    for j in range(4):
        b = pl.ds(j * TOK, TOK)
        out = dot(r.ns[b, :], r.pw[:, :512])
        for h in range(4):
            u = headed(out[:, h * HEAD : (h + 1) * HEAD], b, h)
            r.qs[h // 2, j, pl.ds((h % 2) * TOK, TOK), :] = u
    send(own_e, own_e, r.s_eb.at[0, 0], at(z, 1 - xh, core, c))
    for k in (1, 3, 2):
        send(r.dyi, r.dy.at[my4], r.s_dy.at[k], {"seq": s, "ctx": 2 * y_peer[k] + xl})

    for n, (xx, ll) in enumerate(x_line):
        for j in range(4):
            got(
                r.ow.at[pl.ds(pl.multiple_of(((xx * 2 + core) * 8 + 2 * j + ll) * 16, 16), 16)],
                r.s_o2.at[n, j],
            )
    for j in range(2):
        blk = r.ow.at[rows((2 * j + core) * 128, 128)]
        send(blk, blk, r.s_o3.at[j], me_sib)

    def mask(j):
        n = (2 * j + 2) * TOK
        row = lax.broadcasted_iota(jnp.int32, (QB, n), 0)
        t = (2 * j + xl) * TOK + jnp.where(row < TOK, row, row - TOK)
        u = lax.broadcasted_iota(jnp.int32, (QB, n), 1)
        return (u <= t) & (r.segr[:, :n] == r.segc[:, j : j + 1])

    def at_p(g, j):
        n = (2 * j + 2) * TOK
        if j == 1:
            return r.gpx.at[D : D + QB, g * n : (g + 1) * n]
        first = g * QB + (0 if j == 3 else 2 * QB)
        return r.gpx.at[first : first + QB, 0:n] if j else r.gpx.at[first : first + QB, D - n : D]

    def keys(h, j):
        n = 2 * j + 2
        return r.kv[:n, h].reshape(n * TOK, HEAD)

    before = len(sends)
    for j in range(4):
        got(r.kv.at[2 * j + 1 - xl], r.s_kv.at[j])
        ok = mask(j)
        b = pl.ds(j * TOK, TOK)
        for g in range(2):
            sc = dot(r.qs[g, j], keys(g, j), 1, 1) * SCALE
            sc = jnp.where(ok, sc, NEGATIVE)
            top = jnp.max(sc, axis=1, keepdims=True)
            e = jnp.exp(sc - top)
            tot = jnp.sum(e, axis=1, keepdims=True)
            p = (e * (1.0 / tot)).astype(BF16)
            at_p(g, j)[...] = p
            o = dot(p, keys(2 + g, j)).astype(BF16)
            r.mx[b, (2 * g) * HEAD : (2 * g + 1) * HEAD] = o[:TOK, :]
            r.mx[b, (2 * g + 1) * HEAD : (2 * g + 2) * HEAD] = o[TOK:, :]
        if j == 0:
            for n in range(2):
                got(r.ow.at[rows((2 * n + sib) * 128, 128)], r.s_o3.at[n])
        r.ps[j] = dot(r.mx[b, :], r.ow[...]).astype(BF16)
        send(r.ps.at[j], r.r1.at[y], r.s_r1.at[y], {"seq": s, "ctx": 2 * j + xl}, unless=y == j)

    r1_sends = sends[before:]

    blk = e_block(z, 1 - xh, core)
    got(blk, r.s_eb.at[0, 0])
    for k in (1, 3, 2):
        send(blk, blk, r.s_eb.at[1, k], at(z_peer[k], xh, core, c))
    send(blk, blk, r.s_es.at[4], me_sib)
    for k in (1, 3, 2):
        blk = e_block(z_from[k], xh, core)
        got(blk, r.s_eb.at[0, k])
        send(blk, blk, r.s_es.at[k], me_sib)
    for j in range(4):
        blk = r.cb.at[(xh * 2 + core) * 8 + 2 * j + xl]

        @pl.when(jnp.logical_not(diag & (y == j)))
        def _():
            got(blk, r.s_c1.at[j])

        for n, (xx, ll) in enumerate(x_line):
            send(blk, blk, r.s_c2.at[n, j], at(z, xx, core, 2 * y + ll))

    hidden = r.xs[my4, :].astype(F32) + r.ps[y].astype(F32)
    for k in range(1, 4):
        got(r.r1.at[y_from[k]], r.s_r1.at[y_from[k]])
        hidden = hidden + r.r1[y_from[k]].astype(F32)
    r.hid[...] = hidden
    inv_h = lax.rsqrt(jnp.mean(hidden * hidden, axis=1, keepdims=True) + EPS)
    r.nm[my4, :] = (hidden * inv_h * gain_f).astype(BF16)
    for k in (1, 3, 2):
        send(
            r.nm.at[my4], r.nm.at[my4], r.s_nm.at[k], {"seq": s, "ctx": 2 * y_peer[k] + xl}
        )

    for k in (1, 3, 2):
        blk = e_block(z_from[k], 1 - xh, core)
        got(blk, r.s_eb.at[1, k])
        send(blk, blk, r.s_es.at[4 + k], me_sib)

    for n, (xx, ll) in enumerate(x_line):
        for j in range(4):
            got(r.cb.at[(xx * 2 + core) * 8 + 2 * j + ll], r.s_c2.at[n, j])
    for j in range(2):
        blk = r.cb.at[pl.ds(pl.multiple_of((2 * j + core) * 8, 8), 8)]
        send(blk, blk, r.s_c3.at[j], me_sib)
    for k in range(1, 4):
        got(r.dy.at[rows(y_from[k] * TOK, TOK)], r.s_dy.at[k])
    for n in range(2):
        for k in range(4):
            zz = z if k == 0 else z_from[k]
            got(e_block(zz, xh if n == 0 else 1 - xh, sib), r.s_es.at[4 * n + k])
    for j in range(2):
        got(r.cb.at[pl.ds(pl.multiple_of((2 * j + sib) * 8, 8), 8)], r.s_c3.at[j])
    for j in range(16):
        r.cw[48 * j : 48 * j + 48, :] = jnp.concatenate(
            [r.cb[2 * j].astype(F32), r.cb[2 * j + 1].astype(F32)], 0
        ).astype(BF16)

    def grad_act(k, _):
        b = rows(k * TOK, TOK)
        g = dot(r.dy[b, :], r.cw[...], 1, 1)
        for h in range(6):
            r.f4[rows(h * 512 + k * TOK, TOK), :] = g[:, h * HEAD : (h + 1) * HEAD]
        return 0

    lax.fori_loop(0, 4, grad_act, 0)

    for k in (0, 1, 3, 2):
        b4 = y if k == 0 else y_from[k]
        b = rows(b4 * TOK, TOK)
        if k:
            got(r.nm.at[b], r.s_nm.at[k])
        gu = dot(r.nm[b, :], r.ew[...])
        gate, up = gu[:, :FL], gu[:, FL:]
        sg = 1.0 / (1.0 + jnp.exp(-gate))
        sl = gate * sg
        r.act[b, :] = (sl * up).astype(BF16)
        gt = jnp.concatenate([r.f4[rows(h * 512 + b4 * TOK, TOK), :] for h in range(6)], 1)
        r.ggu[b, :FL] = (gt * up * sg * (1.0 + gate * (1.0 - sg))).astype(BF16)
        r.ggu[b, FL:] = (gt * sl).astype(BF16)
        r.gs[b4] = dot(r.ggu[b, :], r.ew[...], 1, 1).astype(BF16)
        if k:
            send(r.gs.at[b4], r.r2.at[y], r.s_r2.at[k], {"seq": s, "ctx": 2 * b4 + xl})
    for k in (0, 1, 3, 2):
        b4 = y if k == 0 else y_from[k]
        r.los[b4] = dot(r.act[rows(b4 * TOK, TOK), :], r.cw[...]).astype(BF16)

    for j in range(4):
        g = dot(r.nm[:, j * 256 : (j + 1) * 256], r.ggu[...], 0, 0).astype(BF16)
        for q in range(4):
            r.ge[q % 2, 2 * j + q // 2] = g[64 * q : 64 * q + 64, :]
    send(r.ge.at[sib], r.ge1, r.s_e1.at[0], me_sib)
    for j in range(2):
        g = dot(r.act[:, j * 384 : (j + 1) * 384], r.dy[...], 0, 0)
        for q in range(16):
            r.gc[q // 8, j, q % 8] = g[24 * q : 24 * q + 24, :].astype(BF16)
    for j in range(2):
        send(r.gc.at[sib, j], r.gc1.at[j], r.s_c4.at[j], me_sib)

    g_mlp = r.gs[y].astype(F32)
    for k in range(1, 4):
        got(r.r2.at[y_peer[k]], r.s_r2.at[k])
        g_mlp = g_mlp + r.r2[y_peer[k]].astype(F32)
    hidden = r.hid[...]
    inv_h = lax.rsqrt(jnp.mean(hidden * hidden, axis=1, keepdims=True) + EPS)
    unit = hidden * inv_h
    feed = jnp.sum(g_mlp * unit, axis=0, keepdims=True)
    g = g_mlp * gain_f
    g = r.dy[my4, :].astype(F32) + inv_h * (g - unit * jnp.mean(g * unit, axis=1, keepdims=True))
    r.gh[...] = g
    r.g4[my4, :] = g.astype(BF16)
    for k in (1, 3, 2):
        send(
            r.g4.at[my4], r.g4.at[my4], r.s_g4.at[k], {"seq": s, "ctx": 2 * y_peer[k] + xl}
        )
    r.gg0[...] = jnp.zeros((24, 128), F32)
    for j in range(8):
        r.gg0[8 + j : 9 + j, :] = feed[:, 128 * j : 128 * j + 128]

    got(r.ge1, r.s_e1.at[0])

    def pair_e(j, _):
        r.ges[j] = (r.ge[core, j].astype(F32) + r.ge1[j].astype(F32)).astype(BF16)
        return 0

    lax.fori_loop(0, 8, pair_e, 0)
    for k in (1, 3, 2):
        send(
            r.ges.at[pl.ds(pl.multiple_of(2 * z_peer[k], 2), 2)], r.ge2.at[z], r.s_e2.at[k],
            at(z_peer[k], xh, core, c),
        )
    for j in range(2):
        got(r.gc1.at[j], r.s_c4.at[j])
        for q in range(8):
            r.gcs[j, q % 2, q // 2] = (
                r.gc[core, j, q].astype(F32) + r.gc1[j, q].astype(F32)
            ).astype(BF16)
    for n, (xx, ll) in enumerate(x_line):
        send(
            r.gcs.at[xx, ll], r.gc2.at[xh * 2 + xl], r.s_c5.at[n],
            at(z, xx, core, 2 * y + ll),
        )

    for k in (0, 1, 3, 2):
        j = y if k == 0 else y_from[k]
        b = rows(j * TOK, TOK)
        if k:
            got(r.g4.at[b], r.s_g4.at[k])
        gm = dot(r.g4[b, :], r.ow[...], 1, 1).astype(BF16)
        for h in range(4):
            r.gm[h // 2, j, pl.ds((h % 2) * TOK, TOK), :] = gm[:, h * HEAD : (h + 1) * HEAD]

    for k in (1, 3, 2):
        b4 = y_from[k]
        send(r.los.at[b4], r.r3.at[y], r.s_r3.at[k], {"seq": s, "ctx": 2 * b4 + xl})

    for j in range(2):
        g = dot(r.mx[:, j * 256 : (j + 1) * 256], r.g4[...], 0, 0).astype(BF16)
        for q in range(16):
            r.go[q // 8, j, q % 8] = g[16 * q : 16 * q + 16, :]
    for j in range(2):
        send(r.go.at[sib, j], r.go1.at[j], r.s_o4.at[j], me_sib)

    for g in range(2):
        for j in (3, 2, 1, 0):
            n = (2 * j + 2) * TOK
            q, kk, gmh = r.qs[g, j], keys(g, j), r.gm[g, j]
            low = at_p(g, j)[...]
            p = low.astype(F32)
            gat = dot(gmh, keys(2 + g, j), 1, 1)
            ds = (p * (gat - jnp.sum(p * gat, axis=1, keepdims=True))).astype(BF16)
            r.dq[g, j] = dot(ds, kk) * SCALE
            dk = dot(ds, q, 0, 0) * SCALE
            dv = dot(low, gmh, 0, 0)
            kr, vr = g * SEQ, (2 + g) * SEQ
            if j == 3:
                r.f4[kr : kr + n, :] = dk
                r.f4[vr : vr + n, :] = dv
            else:
                r.f4[kr : kr + n, :] += dk
                r.f4[vr : vr + n, :] += dv
            theirs = (2 * j + 1 - xl) * TOK
            r.ds[g, j, 0] = r.f4[rows(kr + theirs, TOK), :].astype(BF16)
            r.ds[g, j, 1] = r.f4[rows(vr + theirs, TOK), :].astype(BF16)
            send(r.ds.at[g, j], r.dr.at[g, j], r.s_dr.at[g, j], x_partner)

    total = r.hid[...] + r.los[y].astype(F32)
    for k in range(1, 4):
        got(r.r3.at[y_peer[k]], r.s_r3.at[k])
        total = total + r.r3[y_peer[k]].astype(F32)
    r.lo[...] = total.astype(BF16)

    for k in (1, 3, 2):
        got(r.ge2.at[z_from[k]], r.s_e2.at[k])
    for xx in range(2):
        total = r.ges[2 * z + xx].astype(F32)
        for k in range(1, 4):
            total = total + r.ge2[z_from[k], xx].astype(F32)
        r.get[xx] = total.astype(BF16)
    send(r.get.at[1 - xh], r.gex, r.s_ex.at[0], at(z, 1 - xh, core, c))

    for j in range(2):
        got(r.go1.at[j], r.s_o4.at[j])
        for q in range(8):
            r.gos[j, q % 2, q // 2] = (
                r.go[core, j, q].astype(F32) + r.go1[j, q].astype(F32)
            ).astype(BF16)
    for n, (xx, ll) in enumerate(x_line):
        send(
            r.gos.at[xx, ll], r.go2.at[xh * 2 + xl], r.s_o5.at[n],
            at(z, xx, core, 2 * y + ll),
        )

    finish(r1_sends)
    r.attg[...] = jnp.zeros((1, D), F32)
    r.hgq[...] = jnp.zeros((1, HEAD), F32)
    r.hgk[...] = jnp.zeros((1, HEAD), F32)

    def norms(g, j):
        b = rows(j * TOK, TOK)
        mine = (2 * j + xl) * TOK
        cosine, sine = r.cos[b, :], r.sin[b, :]
        got(r.dr.at[g, j], r.s_dr.at[g, j])
        for h in (2 * g, 2 * g + 1, 4 + g):
            if h < 4:
                wv = r.dq[g, j, (h % 2) * TOK : (h % 2 + 1) * TOK, :]
            else:
                wv = r.f4[rows(g * SEQ + mine, TOK), :] + r.dr[g, j, 0].astype(F32)
            gn = wv * cosine - turn(wv) * sine
            v = r.pj[b, h * HEAD : (h + 1) * HEAD]
            inv = lax.rsqrt(jnp.mean(v * v, axis=1, keepdims=True) + EPS)
            unit = v * inv
            acc = r.hgq if h < 4 else r.hgk
            acc[...] += jnp.sum(gn * unit, axis=0, keepdims=True)
            t = gn * (gain_q if h < 4 else gain_k)
            gx = inv * (t - unit * jnp.mean(t * unit, axis=1, keepdims=True))
            r.gp[b, HEADS[h] : HEADS[h] + HEAD] = gx.astype(BF16)
        r.gp[b, 640 + g * 256 : 768 + g * 256] = (
            r.f4[rows((2 + g) * SEQ + mine, TOK), :] + r.dr[g, j, 1].astype(F32)
        ).astype(BF16)

    def grad_projection(g):
        half = pl.ds(g * 512, 512)
        for j in range(4):
            left = r.ns[:, j * 256 : (j + 1) * 256]
            for n in range(2):
                t = dot(left, r.gp[:, n * 512 + g * 256 : n * 512 + (g + 1) * 256], 0, 0)
                t = t.astype(BF16)
                at_lane = g * 512 + n * 256
                for q in range(4):
                    first = (q % 2) * 512 + (2 * j + q // 2) * 64
                    r.gpx[first : first + 64, at_lane : at_lane + 256] = t[64 * q : 64 * q + 64, :]
        send(r.gpx.at[rows(sib * 512, 512), half], r.gp1.at[:, half], r.s_p1.at[g], me_sib)

    def pair_projection(g):
        half = pl.ds(g * 512, 512)
        got(r.gp1.at[:, half], r.s_p1.at[g])
        r.gpx[D:, half] = (
            r.gpx[rows(core * 512, 512), half].astype(F32) + r.gp1[:, half].astype(F32)
        ).astype(BF16)
        for k in range(1, 8):
            send(
                r.gpx.at[rows(D + w_peer[k] * 64, 64), half], r.gp2.at[w, :, half],
                r.s_p2.at[g, k], on_w(w_peer[k], core, c),
            )

    for j in (3, 2, 1, 0):
        norms(0, j)
    grad_projection(0)
    for j in (3, 2, 1, 0):
        norms(1, j)
    grad_projection(1)
    pair_projection(0)
    for k in (2, 1, 3, 0):
        j = y_peer[k] if k else y
        b = rows(j * TOK, TOK)
        part = dot(r.gp[b, :], r.pw[...], 1, 1)
        r.ps[j] = part.astype(BF16)
        if k:
            send(r.ps.at[j], r.r1.at[y], r.s_r4.at[y], {"seq": s, "ctx": 2 * j + xl})
        v = r.xs[b, :].astype(F32)
        inv = lax.rsqrt(jnp.mean(v * v, axis=1, keepdims=True) + EPS)
        r.attg[...] += jnp.sum(part * (v * inv), axis=0, keepdims=True)

    for j in range(8):
        r.gg0[j : j + 1, :] = r.attg[:, 128 * j : 128 * j + 128]
    r.gg0[16:17, :] = r.hgq[...]
    r.gg0[17:18, :] = r.hgk[...]
    send(r.gg0, r.gg1, r.s_a1.at[0], me_sib)

    got(r.gg1, r.s_a1.at[0])
    r.ggt[...] = r.gg0[...] + r.gg1[...]
    for k in range(1, 8):
        send(r.ggt, r.gg2.at[w], r.s_a2.at[k], on_w(w_peer[k], core, c))

    pair_projection(1)

    got(r.gex, r.s_ex.at[0])
    total = r.get[xh].astype(F32) + r.gex[...].astype(F32)
    for j in range(8):
        r.gef[j] = total[8 * j : 8 * j + 8, :].astype(BF16)
    for k in range(1, 8):
        send(r.gef.at[ctx_peer[k]], r.ge3.at[c], r.s_e3.at[k], {"seq": s, "ctx": ctx_peer[k]})
    r.ge3[c] = r.gef[c]
    for n, (xx, ll) in enumerate(x_line):
        got(r.gc2.at[xx * 2 + ll], r.s_c5.at[n])
    for n, (xx, ll) in enumerate(x_line):
        got(r.go2.at[xx * 2 + ll], r.s_o5.at[n])
    for mine, theirs, out, last, sem in (
        (r.gcs, r.gc2, r.gcf, r.gc3, r.s_c6), (r.gos, r.go2, r.gof, r.go3, r.s_o6),
    ):
        for j in range(4):
            total = mine[xh, xl, j].astype(F32)
            for xx, ll in x_line:
                total = total + theirs[xx * 2 + ll, j].astype(F32)
            out[j] = total.astype(BF16)
            send(
                out.at[j], last.at[z], sem.at[z], at(y, xh, core, 2 * j + xl),
                unless=diag & (y == j),
            )

    @pl.when(diag)
    def _():
        r.gc3[z] = r.gcf[y]
        r.go3[z] = r.gof[y]

    total = r.ggt[...]
    for k in range(1, 8):
        got(r.gg2.at[w_from[k]], r.s_a2.at[k])
        total = total + r.gg2[w_from[k]]
    r.ggt2[...] = total
    for k in range(1, 8):
        send(r.ggt2, r.gg3.at[c], r.s_a3.at[k], {"seq": s, "ctx": ctx_peer[k]})

    for g in range(2):
        for k in range(1, 8):
            got(r.gp2.at[w_from[k], :, pl.ds(g * 512, 512)], r.s_p2.at[g, k])
    total = r.gpx[rows(D + w * 64, 64), :].astype(F32)
    for k in range(1, 8):
        total = total + r.gp2[w_from[k]].astype(F32)
    for j in range(8):
        r.gpf[j] = total[8 * j : 8 * j + 8, :].astype(BF16)
    for k in range(1, 8):
        send(r.gpf.at[ctx_peer[k]], r.gp3.at[c], r.s_p3.at[k], {"seq": s, "ctx": ctx_peer[k]})
    r.gp3[c] = r.gpf[c]

    for k in range(1, 8):
        got(r.ge3.at[ctx_from[k]], r.s_e3.at[k])
    for j in range(4):
        t = r.ge3[2 * j].astype(F32) + r.ge3[2 * j + 1].astype(F32)
        r.geo[:, j * FL : (j + 1) * FL] = t[:, :FL]
        r.geo[:, FF + j * FL : FF + (j + 1) * FL] = t[:, FL:]
    for j in range(4):

        @pl.when(jnp.logical_not(diag & (z == j)))
        def _():
            got(r.gc3.at[j], r.s_c6.at[j])
            got(r.go3.at[j], r.s_o6.at[j])

    for last, out in ((r.gc3, r.gco), (r.go3, r.goo)):
        out[...] = (last[0].astype(F32) + last[1].astype(F32)) + (
            last[2].astype(F32) + last[3].astype(F32)
        )

    total = r.gh[...]
    g = r.ps[y].astype(F32)
    for k in range(1, 4):
        got(r.r1.at[y_from[k]], r.s_r4.at[y_from[k]])
        g = g + r.r1[y_from[k]].astype(F32)
    v = r.xs[my4, :].astype(F32)
    inv = lax.rsqrt(jnp.mean(v * v, axis=1, keepdims=True) + EPS)
    unit = v * inv
    g = g * gain_a
    r.gt[...] = total + inv * (g - unit * jnp.mean(g * unit, axis=1, keepdims=True))

    for k in range(1, 8):
        got(r.gp3.at[ctx_from[k]], r.s_p3.at[k])
    for j in range(4):
        t = r.gp3[2 * j].astype(F32) + r.gp3[2 * j + 1].astype(F32)
        for place, (start, size) in PLACES:
            n = 0 if start < 512 else 1 if start < 768 else 2
            to = PCOLS[n][0] + j * PCOLS[n][1] + start - PCOLS[n][2]
            r.gpo[:, to : to + size] = t[:, place : place + size]
    total = r.ggt2[...]
    for k in range(1, 8):
        got(r.gg3.at[ctx_from[k]], r.s_a3.at[k])
        total = total + r.gg3[ctx_from[k]]
    r.ggo[...] = total

    finish(sends[:before] + sends[before + len(r1_sends) :])


def hand_over(ggo, lo, gt, gpo, goo, geo, gco, *refs):
    outs, (ag, fg, hg), kept, sem = refs[:6], refs[6:9], refs[9:15], refs[15]
    ins = (lo, gt, gpo, goo, geo, gco)
    loads = [pltpu.make_async_copy(ins[n], kept[n], sem.at[n]) for n in range(6)]
    stores = [pltpu.make_async_copy(kept[n], outs[n], sem.at[6 + n]) for n in range(6)]
    for cp in loads:
        cp.start()
    for load, store in zip(loads, stores, strict=True):
        load.wait()
        store.start()
    place = 8 * lax.axis_index("seq") + lax.axis_index("ctx")
    row = lax.broadcasted_iota(jnp.int32, (8, 128), 0)
    lane = lax.broadcasted_iota(jnp.int32, (8, 128), 1)
    for n, (ref, size) in enumerate(((ag, 8), (fg, 8), (hg, 2))):
        tile = ggo[8 * n : 8 * n + 8, :]
        got = jnp.zeros((1, size), F32)
        at = lax.broadcasted_iota(jnp.int32, (1, size), 1)
        for j in range(size):
            value = jnp.where(row * 128 + lane == place * size + j, tile, 0.0)
            value = jnp.sum(jnp.sum(value, axis=1, keepdims=True), axis=0, keepdims=True)
            got = jnp.where(at == j, value, got)
        ref[...] = got
    for cp in stores:
        cp.wait()


def per_device(x, dy, segments, positions, ag, proj, hg, out, fg, expn, con):
    del positions
    vmem = pl.BlockSpec(memory_space=pltpu.VMEM)
    hbm = pl.BlockSpec(memory_space=pl.ANY)
    scratch = [pltpu.VMEM(shape, kind) for shape, kind in SCRATCH.values()]
    sems = [pltpu.SemaphoreType.DMA(n if isinstance(n, tuple) else (n,)) for n in RECV.values()]
    res = pl.pallas_call(
        kernel,
        name="layer",
        out_shape=(
            jax.ShapeDtypeStruct((TOK, D), BF16),
            jax.ShapeDtypeStruct((TOK, D), F32),
            jax.ShapeDtypeStruct((8, 4096), F32),
            jax.ShapeDtypeStruct((16, D), F32),
            jax.ShapeDtypeStruct((8, 6144), F32),
            jax.ShapeDtypeStruct((24, D), F32),
            jax.ShapeDtypeStruct((24, 128), F32),
        ),
        in_specs=[hbm] * 6 + [vmem] * 4,
        out_specs=(vmem,) * 7,
        scratch_shapes=scratch
        + sems
        + [pltpu.SemaphoreType.DMA((N_SEND,)), pltpu.SemaphoreType.DMA((16,))],
        compiler_params=pltpu.CompilerParams(
            collective_id=0, has_side_effects=True, vmem_limit_bytes=63 * 2**20
        ),
    )(
        x.reshape(TOK, D), dy.reshape(TOK, D), proj, out, expn, con,
        ag.reshape(1, 8), fg.reshape(1, 8), hg.reshape(1, 2), segments,
    )
    big, gains = res[:6], res[6]
    lo, gt, gpo, goo, geo, gco, gag, gfg, ghg = pl.pallas_call(
        hand_over,
        name="hand_over",
        out_shape=tuple(jax.ShapeDtypeStruct(a.shape, a.dtype) for a in big)
        + tuple(jax.ShapeDtypeStruct((1, n), F32) for n in (8, 8, 2)),
        in_specs=[vmem] + [pl.BlockSpec(memory_space=pltpu.HBM)] * 6,
        out_specs=(pl.BlockSpec(memory_space=pltpu.HBM),) * 6 + (vmem,) * 3,
        scratch_shapes=[pltpu.VMEM(a.shape, a.dtype) for a in big]
        + [pltpu.SemaphoreType.DMA((12,))],
        compiler_params=pltpu.CompilerParams(vmem_limit_bytes=63 * 2**20),
    )(gains, *big)
    return (
        lo.reshape(1, TOK, D),
        gt.reshape(1, TOK, D),
        gag.reshape(8),
        gpo,
        ghg.reshape(2),
        goo,
        gfg.reshape(8),
        geo,
        gco,
    )


def solution(mesh):
    return jax.shard_map(
        per_device,
        mesh=mesh,
        in_specs=(
            P("seq", "ctx", None),
            P("seq", "ctx", None),
            P("seq", None),
            P("seq", "ctx"),
            P(("seq", "ctx")),
            P(("seq", "ctx"), None),
            P(("seq", "ctx")),
            P(("seq", "ctx"), None),
            P(("seq", "ctx")),
            P(("seq", "ctx"), None),
            P(("seq", "ctx"), None),
        ),
        out_specs=(
            P("seq", "ctx", None),
            P("seq", "ctx", None),
            P(("seq", "ctx")),
            P(("seq", "ctx"), None),
            P(("seq", "ctx")),
            P(("seq", "ctx"), None),
            P(("seq", "ctx")),
            P(("seq", "ctx"), None),
            P(("seq", "ctx"), None),
        ),
        check_vma=False,
    )
```

```python
import math

import jax
import jax.numpy as jnp
from jax import lax
from jax.experimental import pallas as pl
from jax.experimental.pallas import tpu as pltpu
from jax.sharding import PartitionSpec as P

F32 = jnp.float32
BF16 = jnp.bfloat16
MESH = pl.DeviceIdType.MESH
EPS = 1e-06
THETA = 1000000.0
NEGATIVE = -1e30
D = 1024
HEAD = 128
FF = 3072
FL = 768
TOK = 128
SEQ = 1024
QB = 256
SCALE = HEAD**-0.5


def dot(a, b, da=1, db=0):
    return lax.dot_general(a, b, (((da,), (db,)), ((), ())), preferred_element_type=F32)


def rows(start, size):
    return pl.ds(pl.multiple_of(start, size), size)


SCRATCH = dict(
    pa=((8, 8, D), BF16),
    pw=((8, 2, 64, D), BF16),
    ea=((8, 8, 1536), BF16),
    ew=((4, 2, 2, 64, 1536), BF16),
    ow=((2, 2, 4, 2, 16, D), BF16),
    cb=((2, 2, 4, 2, 24, D), BF16),
    cw=((FL, D), BF16),
    gi=((24, 128), F32),
    ga=((8, 24, 128), F32),
    gb=((8, 24, 128), F32),
    gsum=((24, 128), F32),
    gacc=((24, 128), F32),
    gfr=((24, 128), F32),
    gall=((24, 128), F32),
    cos=((512, HEAD), F32),
    sin=((512, HEAD), F32),
    segc=((QB, 128), jnp.int32),
    xs=((512, D), BF16),
    ns=((512, D), BF16),
    pj=((512, 768), F32),
    qs=((2, 4, QB, HEAD), BF16),
    kv=((8, 4, TOK, HEAD), BF16),
    mx=((512, 512), BF16),
    ps=((4, TOK, D), BF16),
    r1=((4, TOK, D), BF16),
    hid=((TOK, D), F32),
    nm=((512, D), BF16),
    dy=((512, D), BF16),
    act=((512, FL), BF16),
    ggu=((512, 1536), BF16),
    gs=((4, TOK, D), BF16),
    r2=((4, TOK, D), BF16),
    los=((4, TOK, D), BF16),
    r3=((4, TOK, D), BF16),
    gh=((TOK, D), F32),
    g4=((512, D), BF16),
    gm=((2, 4, QB, HEAD), BF16),
    f4=((4096, HEAD), F32),
    dq=((2, 4, QB, HEAD), F32),
    ds=((2, 4, 2, TOK, HEAD), BF16),
    dr=((2, 4, 2, TOK, HEAD), BF16),
    gp=((512, D), BF16),
    attg=((1, D), F32),
    hgq=((1, HEAD), F32),
    hgk=((1, HEAD), F32),
    gg0=((24, 128), F32),
    gg1=((24, 128), F32),
    ggt=((24, 128), F32),
    ggt2=((24, 128), F32),
    gg2=((8, 24, 128), F32),
    gg3=((8, 24, 128), F32),
    ge=((2, 8, 64, 1536), BF16),
    ge1=((8, 64, 1536), BF16),
    ges=((8, 64, 1536), BF16),
    ge2=((4, 2, 64, 1536), BF16),
    get=((2, 64, 1536), BF16),
    gex=((64, 1536), BF16),
    gef=((8, 8, 1536), BF16),
    ge3=((8, 8, 1536), BF16),
    gc=((2, 2, 8, 24, D), BF16),
    gc1=((2, 8, 24, D), BF16),
    gcs=((2, 2, 4, 24, D), BF16),
    gc2=((4, 4, 24, D), BF16),
    gcf=((4, 24, D), BF16),
    gc3=((4, 24, D), BF16),
    go=((2, 2, 8, 16, D), BF16),
    go1=((2, 8, 16, D), BF16),
    gos=((2, 2, 4, 16, D), BF16),
    go2=((4, 4, 16, D), BF16),
    gof=((4, 16, D), BF16),
    go3=((4, 16, D), BF16),
    gpx=((1536, D), BF16),
    gp1=((512, D), BF16),
    gp2=((8, 64, D), BF16),
    gpf=((8, 8, D), BF16),
    gp3=((8, 8, D), BF16),
)
RECV = dict(
    pa=(8, 2), ea=8, ga=8, gb=8, gfr=1, x=4, dy=4, pb=(2, 8), eb=(2, 4), ps=2, es=2,
    o1=4, o2=4, o3=2, c1=4, c2=4, c3=2, kv=4, r1=4, nm=4, r2=4, r3=4, g4=4, dr=(2, 4), r4=4,
    e1=1, e2=4, ex=1, e3=8, c4=2, c5=4, c6=4, o4=2, o5=4, o6=4, p1=2, p2=(2, 8), p3=8, a1=1, a2=8, a3=8,
)
N_SEND = 160
NAMES = (
    ["x", "dyi", "pi", "oi", "ei", "ci", "agi", "fgi", "hgi", "segr"]
    + ["lo", "gt", "gpo", "goo", "geo", "gco", "ggo"]
    + list(SCRATCH)
    + ["s_" + n for n in RECV]
    + ["send", "loc"]
)
PLACES = (
    (0, (0, 256)), (256, (512, 128)), (384, (768, 128)),
    (512, (256, 256)), (768, (640, 128)), (896, (896, 128)),
)
HEADS = (0, 128, 256, 384, 512, 768)
PCOLS = ((0, 512, 0), (2048, 256, 512), (3072, 256, 768))


class Box:
    pass


def kernel(*refs):
    r = Box()
    for name, ref in zip(NAMES, refs, strict=True):
        setattr(r, name, ref)
    s, c = lax.axis_index("seq"), lax.axis_index("ctx")
    z, xh, core = s // 4, (s // 2) % 2, s % 2
    y, xl = c // 2, c % 2
    w = s // 2
    sib = 1 - core

    def at(zz, xx, cc, ctx):
        return {"seq": zz * 4 + xx * 2 + cc, "ctx": ctx}

    def on_w(ww, cc, ctx):
        return {"seq": ww * 2 + cc, "ctx": ctx}

    me_sib = on_w(w, sib, c)
    ctx_peer = [None] + [lax.rem(c + k, 8) for k in range(1, 8)]
    ctx_from = [None] + [lax.rem(c + 8 - k, 8) for k in range(1, 8)]
    w_peer = [None] + [lax.rem(w + k, 8) for k in range(1, 8)]
    w_from = [None] + [lax.rem(w + 8 - k, 8) for k in range(1, 8)]
    y_peer = [None] + [lax.rem(y + k, 4) for k in range(1, 4)]
    y_from = [None] + [lax.rem(y + 4 - k, 4) for k in range(1, 4)]
    z_peer = [None] + [lax.rem(z + k, 4) for k in range(1, 4)]
    z_from = [None] + [lax.rem(z + 4 - k, 4) for k in range(1, 4)]
    x_line = [(xh, 1 - xl), (1 - xh, xl), (1 - xh, 1 - xl)]
    diag = y == z

    def e_block(zz, xx, cc):
        return r.ew.at[zz, xx, cc]

    def all_p(start, stop):
        return r.pw[:, :, :, start:stop].reshape(D, stop - start)

    def all_e():
        return r.ew[...].reshape(D, 1536)

    def all_o():
        return r.ow[...].reshape(512, D)

    free, sends = list(range(N_SEND - 1)), []

    def send(src, dst, sem, dev, unless=None):
        at = free.pop(0)
        cp = pltpu.make_async_remote_copy(
            src_ref=src, dst_ref=dst, send_sem=r.send.at[at], recv_sem=sem,
            device_id=dev, device_id_type=MESH,
        )
        sends.append((cp, unless, at))
        if unless is None:
            cp.start()
        else:
            pl.when(jnp.logical_not(unless))(cp.start)

    def finish(some):
        for entry in some:
            cp, unless, at = entry
            if unless is None:
                cp.wait_send()
            else:
                pl.when(jnp.logical_not(unless))(cp.wait_send)
            free.append(at)
        sends[:] = [e for e in sends if not any(e is f for f in some)]

    def got(dst, sem):
        pltpu.make_async_remote_copy(
            src_ref=dst, dst_ref=dst, send_sem=r.send.at[N_SEND - 1], recv_sem=sem,
            device_id=me_sib, device_id_type=MESH,
        ).wait_recv()

    bar = pltpu.get_barrier_semaphore()

    def greet(dev):
        pl.semaphore_signal(bar, inc=1, device_id=dev, device_id_type=MESH)

    greet(me_sib)
    for k in range(1, 8):
        greet({"seq": s, "ctx": ctx_peer[k]})
        greet(on_w(w_peer[k], core, c))
    greet(at(z, x_line[2][0], core, 2 * y + x_line[2][1]))
    for zz in range(4):

        @pl.when(jnp.logical_not(diag & (z == zz)))
        def _():
            greet(at(zz, xh, core, 2 * z + xl))
            greet(at(y, xh, core, 2 * zz + xl))

    own = []

    def own_copy(src, dst):
        cp = pltpu.make_async_copy(src, dst, r.loc.at[len(own)])
        own.append(cp)
        cp.start()

    my4 = rows(y * TOK, TOK)
    own_copy(r.x, r.xs.at[my4])
    own_copy(r.dyi, r.dy.at[my4])
    for start, size, place in PCOLS:
        own_copy(
            r.pi.at[:, pl.ds(pl.multiple_of(start + y * size, size), size)],
            r.pa.at[c, :, pl.ds(place, size)],
        )
    for part in range(2):
        own_copy(
            r.ei.at[:, pl.ds(pl.multiple_of(part * FF + y * FL, FL), FL)],
            r.ea.at[c, :, pl.ds(part * FL, FL)],
        )

    tile_row = lax.broadcasted_iota(jnp.int32, (8, 128), 0)
    tile_lane = lax.broadcasted_iota(jnp.int32, (8, 128), 1)
    flat = tile_row * 128 + tile_lane
    place = 8 * s + c
    for n, (ref, size) in enumerate(((r.agi, 8), (r.fgi, 8), (r.hgi, 2))):
        values = ref[...].astype(F32)
        tile = jnp.zeros((8, 128), F32)
        for j in range(size):
            tile = jnp.where(flat == place * size + j, values[:, j : j + 1], tile)
        r.gi[8 * n : 8 * n + 8, :] = tile

    pl.semaphore_wait(bar, 24 - jnp.where(diag, 2, 0))

    for k in range(1, 8):
        send(r.gi, r.ga.at[c], r.s_ga.at[k], {"seq": s, "ctx": ctx_peer[k]})
    for part in (1, 2, 0):
        start, size, place = PCOLS[part]
        for k in range(1, 8):
            to = ctx_peer[k]
            send(
                r.pi.at[:, pl.ds(pl.multiple_of(start + (to // 2) * size, size), size)],
                r.pa.at[c, :, pl.ds(place, size)],
                r.s_pa.at[k, min(part, 1)],
                {"seq": s, "ctx": to},
            )
    for k in (1, 3, 2):
        send(r.x, r.xs.at[my4], r.s_x.at[k], {"seq": s, "ctx": 2 * y_peer[k] + xl})

    @pl.when(diag)
    def _():
        a = pltpu.make_async_copy(
            r.oi,
            r.ow.at[xh, core, y, xl],
            r.loc.at[14],
        )
        b = pltpu.make_async_copy(r.ci, r.cb.at[xh, core, y, xl], r.loc.at[15])
        a.start()
        b.start()
        a.wait()
        b.wait()

    for cp in own:
        cp.wait()

    lane = lax.broadcasted_iota(jnp.int32, (1, HEAD), 1)
    index = jnp.where(lane < HEAD // 2, lane, lane - HEAD // 2).astype(F32)
    inverse = jnp.exp(index * (-2.0 / HEAD * math.log(THETA)))
    sign = jnp.where(lane < HEAD // 2, -1.0, 1.0)
    eye = lax.broadcasted_iota(jnp.int32, (TOK, TOK), 0) == lax.broadcasted_iota(
        jnp.int32, (TOK, TOK), 1
    )
    for j in range(4):
        b = pl.ds(j * TOK, TOK)
        seg = r.segr[:, pl.ds(pl.multiple_of((2 * j + xl) * TOK, TOK), TOK)]
        seg = jnp.sum(jnp.where(eye, seg.astype(F32), 0.0), axis=1, keepdims=True)
        r.segc[:, j : j + 1] = jnp.concatenate([seg, seg], 0).astype(jnp.int32)
        before = jnp.sum((r.segr[...].astype(F32) < seg).astype(F32), axis=1, keepdims=True)
        t = lax.broadcasted_iota(jnp.int32, (TOK, 1), 0) + (2 * j + xl) * TOK
        phase = (t.astype(F32) - before) * inverse
        r.cos[b, :] = jnp.cos(phase)
        r.sin[b, :] = jnp.sin(phase) * sign

    kv_half, q_half = pl.ds(512, 512), pl.ds(0, 512)

    def spread(n, half):
        blk = r.pw.at[w, core, :, half]
        for k in range(1, 8):
            send(blk, blk, r.s_pb.at[n, k], on_w(w_peer[k], core, c))

    def pass_on(n, half):
        for k in range(1, 8):
            got(r.pw.at[w_from[k], core, :, half], r.s_pb.at[n, k])
        blk = r.pw.at[:, core, :, half]
        send(blk, blk, r.s_ps.at[n], me_sib)

    def from_sibling(n, half):
        got(r.pw.at[:, sib, :, half], r.s_ps.at[n])

    def joined(start, size):
        return jnp.concatenate(
            [r.pa[j, :, start : start + size].astype(F32) for j in range(8)], 0
        ).astype(BF16)

    total = r.gi[...]
    for k in range(1, 8):
        got(r.ga.at[ctx_from[k]], r.s_ga.at[k])
        total = total + r.ga[ctx_from[k]]
    r.gsum[...] = total
    for k in range(1, 8):
        send(r.gsum, r.gb.at[w], r.s_gb.at[k], on_w(w_peer[k], core, c))
    for k in range(1, 8):
        got(r.pa.at[ctx_from[k], :, kv_half], r.s_pa.at[k, 1])
    for g in range(2):
        r.pw[w, core, :, 512 + g * 256 : 640 + g * 256] = joined(512 + g * 128, 128)
        r.pw[w, core, :, 640 + g * 256 : 768 + g * 256] = joined(768 + g * 128, 128)
    spread(0, kv_half)
    for k in range(1, 8):
        to = ctx_peer[k]
        for part in range(2):
            send(
                r.ei.at[:, pl.ds(pl.multiple_of(part * FF + (to // 2) * FL, FL), FL)],
                r.ea.at[c, :, pl.ds(part * FL, FL)],
                r.s_ea.at[k],
                {"seq": s, "ctx": to},
            )
    for k in range(1, 8):
        got(r.pa.at[ctx_from[k], :, q_half], r.s_pa.at[k, 0])
    r.pw[w, core, :, 0:512] = joined(0, 512)
    total = r.gsum[...]
    for k in range(1, 8):
        got(r.gb.at[w_from[k]], r.s_gb.at[k])
        total = total + r.gb[w_from[k]]
    r.gacc[...] = total
    send(r.gacc, r.gfr, r.s_gfr.at[0], me_sib)
    for zz in range(4):
        send(
            r.oi,
            r.ow.at[xh, core, y, xl],
            r.s_o1.at[y],
            at(zz, xh, core, 2 * z + xl),
            unless=diag & (z == zz),
        )
    pass_on(0, kv_half)
    spread(1, q_half)
    got(r.gfr, r.s_gfr.at[0])
    r.gall[...] = r.gacc[...] + r.gfr[...]
    from_sibling(0, kv_half)

    def wide(first):
        return jnp.concatenate([r.gall[first + j : first + j + 1, :] for j in range(8)], 1)

    gain_a, gain_f = wide(0), wide(8)
    gain_q, gain_k = r.gall[16:17, :], r.gall[17:18, :]

    def turn(v):
        return pltpu.roll(v, HEAD // 2, 1)

    x_partner = {"seq": s, "ctx": 2 * y + 1 - xl}
    def headed(u, b, h):
        r.pj[b, h * HEAD : (h + 1) * HEAD] = u
        ui = lax.rsqrt(jnp.mean(u * u, axis=1, keepdims=True) + EPS)
        u = u * ui * (gain_q if h < 4 else gain_k)
        return (u * r.cos[b, :] + turn(u) * r.sin[b, :]).astype(BF16)

    for k in (0, 1, 3, 2):
        j = y if k == 0 else y_from[k]
        b = rows(j * TOK, TOK)
        if k:
            got(r.xs.at[b], r.s_x.at[k])
        v = r.xs[b, :].astype(F32)
        inv = lax.rsqrt(jnp.mean(v * v, axis=1, keepdims=True) + EPS)
        n = (v * inv * gain_a).astype(BF16)
        r.ns[b, :] = n
        out = dot(n, all_p(512, D))
        mine = 2 * j + xl
        for g in range(2):
            r.kv[mine, g] = headed(out[:, g * 256 : g * 256 + HEAD], b, 4 + g)
            r.kv[mine, 2 + g] = out[:, g * 256 + HEAD : g * 256 + 256].astype(BF16)
        send(r.kv.at[mine], r.kv.at[mine], r.s_kv.at[j], x_partner)

    for k in (1, 3, 2):
        send(r.dyi, r.dy.at[my4], r.s_dy.at[k], {"seq": s, "ctx": 2 * y_peer[k] + xl})

    for k in range(1, 8):
        got(r.ea.at[ctx_from[k]], r.s_ea.at[k])
    r.ew[z, xh, core] = jnp.concatenate([r.ea[j].astype(F32) for j in range(8)], 0).astype(BF16)
    own_e = r.ew.at[z, xh, core]
    for k in (1, 3, 2):
        send(own_e, own_e, r.s_eb.at[0, k], at(z_peer[k], xh, core, c))
    for zz in range(4):
        send(
            r.ci,
            r.cb.at[xh, core, y, xl],
            r.s_c1.at[y],
            at(zz, xh, core, 2 * z + xl),
            unless=diag & (z == zz),
        )

    pass_on(1, q_half)
    from_sibling(1, q_half)
    for j in range(4):
        b = pl.ds(j * TOK, TOK)
        out = dot(r.ns[b, :], all_p(0, 512))
        for h in range(4):
            u = headed(out[:, h * HEAD : (h + 1) * HEAD], b, h)
            r.qs[h // 2, j, pl.ds((h % 2) * TOK, TOK), :] = u
    for j in range(4):

        @pl.when(jnp.logical_not(diag & (y == j)))
        def _():
            got(r.ow.at[xh, core, j, xl], r.s_o1.at[j])

    blk = r.ow.at[xh, core, :, xl]
    for n, (xx, ll) in enumerate(x_line):
        send(blk, blk, r.s_o2.at[n], at(z, xx, core, 2 * y + ll))
    send(own_e, own_e, r.s_eb.at[0, 0], at(z, 1 - xh, core, c))


    def mask(j):
        n = (2 * j + 2) * TOK
        row = lax.broadcasted_iota(jnp.int32, (QB, n), 0)
        t = (2 * j + xl) * TOK + jnp.where(row < TOK, row, row - TOK)
        u = lax.broadcasted_iota(jnp.int32, (QB, n), 1)
        return (u <= t) & (r.segr[:, :n] == r.segc[:, j : j + 1])

    def at_p(g, j):
        n = (2 * j + 2) * TOK
        if j == 1:
            return r.gpx.at[D : D + QB, g * n : (g + 1) * n]
        first = g * QB + (0 if j == 3 else 2 * QB)
        return r.gpx.at[first : first + QB, 0:n] if j else r.gpx.at[first : first + QB, D - n : D]

    def keys(h, j):
        n = 2 * j + 2
        return r.kv[:n, h].reshape(n * TOK, HEAD)

    for j in range(4):
        got(r.kv.at[2 * j + 1 - xl], r.s_kv.at[j])
        ok = mask(j)
        b = pl.ds(j * TOK, TOK)
        for g in range(2):
            sc = dot(r.qs[g, j], keys(g, j), 1, 1) * SCALE
            sc = jnp.where(ok, sc, NEGATIVE)
            top = jnp.max(sc, axis=1, keepdims=True)
            e = jnp.exp(sc - top)
            tot = jnp.sum(e, axis=1, keepdims=True)
            p = (e * (1.0 / tot)).astype(BF16)
            at_p(g, j)[...] = p
            o = dot(p, keys(2 + g, j)).astype(BF16)
            r.mx[b, (2 * g) * HEAD : (2 * g + 1) * HEAD] = o[:TOK, :]
            r.mx[b, (2 * g + 1) * HEAD : (2 * g + 2) * HEAD] = o[TOK:, :]
        if j == 2:
            for n, (xx, ll) in enumerate(x_line):
                got(r.ow.at[xx, core, :, ll], r.s_o2.at[n])
            for n in range(2):
                send(r.ow.at[n, core], r.ow.at[n, core], r.s_o3.at[n], me_sib)
    for n in range(2):
        got(r.ow.at[n, sib], r.s_o3.at[n])
    for k in (2, 1, 3, 0):
        j = y_peer[k] if k else y
        r.ps[j] = dot(r.mx[rows(j * TOK, TOK), :], all_o()).astype(BF16)
        if k:
            send(r.ps.at[j], r.r1.at[y], r.s_r1.at[y], {"seq": s, "ctx": 2 * j + xl})

    blk = e_block(z, 1 - xh, core)
    got(blk, r.s_eb.at[0, 0])
    for k in (1, 3, 2):
        send(blk, blk, r.s_eb.at[1, k], at(z_peer[k], xh, core, c))
    for k in (1, 3, 2):
        got(e_block(z_from[k], xh, core), r.s_eb.at[0, k])
    blk = r.ew.at[:, xh, core]
    send(blk, blk, r.s_es.at[0], me_sib)
    for j in range(4):

        @pl.when(jnp.logical_not(diag & (y == j)))
        def _():
            got(r.cb.at[xh, core, j, xl], r.s_c1.at[j])

    blk = r.cb.at[xh, core, :, xl]
    for n, (xx, ll) in enumerate(x_line):
        send(blk, blk, r.s_c2.at[n], at(z, xx, core, 2 * y + ll))

    hidden = r.xs[my4, :].astype(F32) + r.ps[y].astype(F32)
    for k in range(1, 4):
        got(r.r1.at[y_from[k]], r.s_r1.at[y_from[k]])
        hidden = hidden + r.r1[y_from[k]].astype(F32)
    r.hid[...] = hidden
    inv_h = lax.rsqrt(jnp.mean(hidden * hidden, axis=1, keepdims=True) + EPS)
    r.nm[my4, :] = (hidden * inv_h * gain_f).astype(BF16)
    def send_nm(k):
        send(
            r.nm.at[my4], r.nm.at[my4], r.s_nm.at[k], {"seq": s, "ctx": 2 * y_peer[k] + xl}
        )

    older = list(sends)
    send_nm(1)
    send_nm(3)
    for k in (1, 3, 2):
        got(e_block(z_from[k], 1 - xh, core), r.s_eb.at[1, k])
    blk = r.ew.at[:, 1 - xh, core]
    send(blk, blk, r.s_es.at[1], me_sib)

    for n, (xx, ll) in enumerate(x_line):
        got(r.cb.at[xx, core, :, ll], r.s_c2.at[n])
    for n in range(2):
        send(r.cb.at[n, core], r.cb.at[n, core], r.s_c3.at[n], me_sib)
    for k in range(1, 4):
        got(r.dy.at[rows(y_from[k] * TOK, TOK)], r.s_dy.at[k])
    finish(older)
    for n in range(2):
        got(r.cb.at[n, sib], r.s_c3.at[n])
    got(r.ew.at[:, xh, sib], r.s_es.at[0])
    got(r.ew.at[:, 1 - xh, sib], r.s_es.at[1])
    for j in range(16):
        r.cw[48 * j : 48 * j + 48, :] = jnp.concatenate(
            [r.cb[j // 8, j // 4 % 2, j % 4, n].astype(F32) for n in range(2)], 0
        ).astype(BF16)

    def grad_act(k, _):
        b = rows(k * TOK, TOK)
        g = dot(r.dy[b, :], r.cw[...], 1, 1)
        for h in range(6):
            r.f4[rows(h * 512 + k * TOK, TOK), :] = g[:, h * HEAD : (h + 1) * HEAD]
        return 0

    lax.fori_loop(0, 4, grad_act, 0)

    for k in (0, 1, 3, 2):
        b4 = y if k == 0 else y_from[k]
        b = rows(b4 * TOK, TOK)
        if k:
            got(r.nm.at[b], r.s_nm.at[k])
        gu = dot(r.nm[b, :], all_e())
        gate, up = gu[:, :FL], gu[:, FL:]
        sg = 1.0 / (1.0 + jnp.exp(-gate))
        sl = gate * sg
        r.act[b, :] = (sl * up).astype(BF16)
        gt = jnp.concatenate([r.f4[rows(h * 512 + b4 * TOK, TOK), :] for h in range(6)], 1)
        r.ggu[b, :FL] = (gt * up * sg * (1.0 + gate * (1.0 - sg))).astype(BF16)
        r.ggu[b, FL:] = (gt * sl).astype(BF16)
        r.gs[b4] = dot(r.ggu[b, :], all_e(), 1, 1).astype(BF16)
        if k == 0:
            send_nm(2)
        if k:
            send(r.gs.at[b4], r.r2.at[y], r.s_r2.at[k], {"seq": s, "ctx": 2 * b4 + xl})
    for k in (0, 1, 3, 2):
        b4 = y if k == 0 else y_from[k]
        r.los[b4] = dot(r.act[rows(b4 * TOK, TOK), :], r.cw[...]).astype(BF16)

    for j in range(4):
        g = dot(r.nm[:, j * 256 : (j + 1) * 256], r.ggu[...], 0, 0).astype(BF16)
        for q in range(4):
            r.ge[q % 2, 2 * j + q // 2] = g[64 * q : 64 * q + 64, :]
    send(r.ge.at[sib], r.ge1, r.s_e1.at[0], me_sib)
    for j in range(2):
        g = dot(r.act[:, j * 384 : (j + 1) * 384], r.dy[...], 0, 0)
        for q in range(16):
            r.gc[q // 8, j, q % 8] = g[24 * q : 24 * q + 24, :].astype(BF16)
    for j in range(2):
        send(r.gc.at[sib, j], r.gc1.at[j], r.s_c4.at[j], me_sib)

    g_mlp = r.gs[y].astype(F32)
    for k in range(1, 4):
        got(r.r2.at[y_peer[k]], r.s_r2.at[k])
        g_mlp = g_mlp + r.r2[y_peer[k]].astype(F32)
    hidden = r.hid[...]
    inv_h = lax.rsqrt(jnp.mean(hidden * hidden, axis=1, keepdims=True) + EPS)
    unit = hidden * inv_h
    feed = jnp.sum(g_mlp * unit, axis=0, keepdims=True)
    g = g_mlp * gain_f
    g = r.dy[my4, :].astype(F32) + inv_h * (g - unit * jnp.mean(g * unit, axis=1, keepdims=True))
    r.gh[...] = g
    r.g4[my4, :] = g.astype(BF16)
    for k in (1, 3, 2):
        send(
            r.g4.at[my4], r.g4.at[my4], r.s_g4.at[k], {"seq": s, "ctx": 2 * y_peer[k] + xl}
        )
    r.gg0[...] = jnp.zeros((24, 128), F32)
    for j in range(8):
        r.gg0[8 + j : 9 + j, :] = feed[:, 128 * j : 128 * j + 128]

    got(r.ge1, r.s_e1.at[0])

    def pair_e(j, _):
        r.ges[j] = (r.ge[core, j].astype(F32) + r.ge1[j].astype(F32)).astype(BF16)
        return 0

    lax.fori_loop(0, 8, pair_e, 0)
    for k in (1, 3, 2):
        send(
            r.ges.at[pl.ds(pl.multiple_of(2 * z_peer[k], 2), 2)], r.ge2.at[z], r.s_e2.at[k],
            at(z_peer[k], xh, core, c),
        )
    for j in range(2):
        got(r.gc1.at[j], r.s_c4.at[j])
        for q in range(8):
            r.gcs[j, q % 2, q // 2] = (
                r.gc[core, j, q].astype(F32) + r.gc1[j, q].astype(F32)
            ).astype(BF16)
    for n, (xx, ll) in enumerate(x_line):
        send(
            r.gcs.at[xx, ll], r.gc2.at[xh * 2 + xl], r.s_c5.at[n],
            at(z, xx, core, 2 * y + ll),
        )

    for k in (0, 1, 3, 2):
        j = y if k == 0 else y_from[k]
        b = rows(j * TOK, TOK)
        if k:
            got(r.g4.at[b], r.s_g4.at[k])
        gm = dot(r.g4[b, :], all_o(), 1, 1).astype(BF16)
        for h in range(4):
            r.gm[h // 2, j, pl.ds((h % 2) * TOK, TOK), :] = gm[:, h * HEAD : (h + 1) * HEAD]

    for k in (1, 3, 2):
        b4 = y_from[k]
        send(r.los.at[b4], r.r3.at[y], r.s_r3.at[k], {"seq": s, "ctx": 2 * b4 + xl})

    for j in range(2):
        g = dot(r.mx[:, j * 256 : (j + 1) * 256], r.g4[...], 0, 0).astype(BF16)
        for q in range(16):
            r.go[q // 8, j, q % 8] = g[16 * q : 16 * q + 16, :]
    for j in range(2):
        send(r.go.at[sib, j], r.go1.at[j], r.s_o4.at[j], me_sib)

    for g in range(2):
        for j in (3, 2, 1, 0):
            n = (2 * j + 2) * TOK
            q, kk, gmh = r.qs[g, j], keys(g, j), r.gm[g, j]
            low = at_p(g, j)[...]
            p = low.astype(F32)
            gat = dot(gmh, keys(2 + g, j), 1, 1)
            ds = (p * (gat - jnp.sum(p * gat, axis=1, keepdims=True))).astype(BF16)
            r.dq[g, j] = dot(ds, kk) * SCALE
            dk = dot(ds, q, 0, 0) * SCALE
            dv = dot(low, gmh, 0, 0)
            kr, vr = g * SEQ, (2 + g) * SEQ
            if j == 3:
                r.f4[kr : kr + n, :] = dk
                r.f4[vr : vr + n, :] = dv
            else:
                r.f4[kr : kr + n, :] += dk
                r.f4[vr : vr + n, :] += dv
            theirs = (2 * j + 1 - xl) * TOK
            r.ds[g, j, 0] = r.f4[rows(kr + theirs, TOK), :].astype(BF16)
            r.ds[g, j, 1] = r.f4[rows(vr + theirs, TOK), :].astype(BF16)
            send(r.ds.at[g, j], r.dr.at[g, j], r.s_dr.at[g, j], x_partner)
            if g or j != 3:
                continue
            for j in range(2):
                got(r.go1.at[j], r.s_o4.at[j])
                for q in range(8):
                    r.gos[j, q % 2, q // 2] = (
                        r.go[core, j, q].astype(F32) + r.go1[j, q].astype(F32)
                    ).astype(BF16)
            for n, (xx, ll) in enumerate(x_line):
                send(
                    r.gos.at[xx, ll], r.go2.at[xh * 2 + xl], r.s_o5.at[n],
                    at(z, xx, core, 2 * y + ll),
                )

    total = r.hid[...] + r.los[y].astype(F32)
    for k in range(1, 4):
        got(r.r3.at[y_peer[k]], r.s_r3.at[k])
        total = total + r.r3[y_peer[k]].astype(F32)
    r.lo[...] = total.astype(BF16)

    r.attg[...] = jnp.zeros((1, D), F32)
    r.hgq[...] = jnp.zeros((1, HEAD), F32)
    r.hgk[...] = jnp.zeros((1, HEAD), F32)

    def norms(g, j):
        b = rows(j * TOK, TOK)
        mine = (2 * j + xl) * TOK
        cosine, sine = r.cos[b, :], r.sin[b, :]
        got(r.dr.at[g, j], r.s_dr.at[g, j])
        for h in (2 * g, 2 * g + 1, 4 + g):
            if h < 4:
                wv = r.dq[g, j, (h % 2) * TOK : (h % 2 + 1) * TOK, :]
            else:
                wv = r.f4[rows(g * SEQ + mine, TOK), :] + r.dr[g, j, 0].astype(F32)
            gn = wv * cosine - turn(wv) * sine
            v = r.pj[b, h * HEAD : (h + 1) * HEAD]
            inv = lax.rsqrt(jnp.mean(v * v, axis=1, keepdims=True) + EPS)
            unit = v * inv
            acc = r.hgq if h < 4 else r.hgk
            acc[...] += jnp.sum(gn * unit, axis=0, keepdims=True)
            t = gn * (gain_q if h < 4 else gain_k)
            gx = inv * (t - unit * jnp.mean(t * unit, axis=1, keepdims=True))
            r.gp[b, HEADS[h] : HEADS[h] + HEAD] = gx.astype(BF16)
        r.gp[b, 640 + g * 256 : 768 + g * 256] = (
            r.f4[rows((2 + g) * SEQ + mine, TOK), :] + r.dr[g, j, 1].astype(F32)
        ).astype(BF16)

    def grad_projection(g):
        half = pl.ds(g * 512, 512)
        for j in range(4):
            left = r.ns[:, j * 256 : (j + 1) * 256]
            for n in range(2):
                t = dot(left, r.gp[:, n * 512 + g * 256 : n * 512 + (g + 1) * 256], 0, 0)
                t = t.astype(BF16)
                at_lane = g * 512 + n * 256
                for q in range(4):
                    first = (q % 2) * 512 + (2 * j + q // 2) * 64
                    r.gpx[first : first + 64, at_lane : at_lane + 256] = t[64 * q : 64 * q + 64, :]
        send(r.gpx.at[rows(sib * 512, 512), half], r.gp1.at[:, half], r.s_p1.at[g], me_sib)

    def pair_projection(g):
        half = pl.ds(g * 512, 512)
        got(r.gp1.at[:, half], r.s_p1.at[g])
        r.gpx[D:, half] = (
            r.gpx[rows(core * 512, 512), half].astype(F32) + r.gp1[:, half].astype(F32)
        ).astype(BF16)
        for k in range(1, 8):
            send(
                r.gpx.at[rows(D + w_peer[k] * 64, 64), half], r.gp2.at[w, :, half],
                r.s_p2.at[g, k], on_w(w_peer[k], core, c),
            )

    for j in (3, 2, 1, 0):
        norms(0, j)
    grad_projection(0)
    for j in (3, 2, 1, 0):
        norms(1, j)
    grad_projection(1)
    pair_projection(0)
    for k in (1, 3, 2):
        got(r.ge2.at[z_from[k]], r.s_e2.at[k])
    for xx in range(2):
        total = r.ges[2 * z + xx].astype(F32)
        for k in range(1, 4):
            total = total + r.ge2[z_from[k], xx].astype(F32)
        r.get[xx] = total.astype(BF16)
    send(r.get.at[1 - xh], r.gex, r.s_ex.at[0], at(z, 1 - xh, core, c))

    for k in (2, 1, 3, 0):
        j = y_peer[k] if k else y
        b = rows(j * TOK, TOK)
        part = dot(r.gp[b, :], all_p(0, D), 1, 1)
        r.ps[j] = part.astype(BF16)
        if k:
            send(r.ps.at[j], r.r1.at[y], r.s_r4.at[y], {"seq": s, "ctx": 2 * j + xl})
        v = r.xs[b, :].astype(F32)
        inv = lax.rsqrt(jnp.mean(v * v, axis=1, keepdims=True) + EPS)
        r.attg[...] += jnp.sum(part * (v * inv), axis=0, keepdims=True)

    for j in range(8):
        r.gg0[j : j + 1, :] = r.attg[:, 128 * j : 128 * j + 128]
    r.gg0[16:17, :] = r.hgq[...]
    r.gg0[17:18, :] = r.hgk[...]
    send(r.gg0, r.gg1, r.s_a1.at[0], me_sib)

    got(r.gg1, r.s_a1.at[0])
    r.ggt[...] = r.gg0[...] + r.gg1[...]
    for k in range(1, 8):
        send(r.ggt, r.gg2.at[w], r.s_a2.at[k], on_w(w_peer[k], core, c))

    pair_projection(1)

    got(r.gex, r.s_ex.at[0])
    total = r.get[xh].astype(F32) + r.gex[...].astype(F32)
    for j in range(8):
        r.gef[j] = total[8 * j : 8 * j + 8, :].astype(BF16)
    for k in range(1, 8):
        send(r.gef.at[ctx_peer[k]], r.ge3.at[c], r.s_e3.at[k], {"seq": s, "ctx": ctx_peer[k]})
    r.ge3[c] = r.gef[c]
    for n, (xx, ll) in enumerate(x_line):
        got(r.gc2.at[xx * 2 + ll], r.s_c5.at[n])
    for n, (xx, ll) in enumerate(x_line):
        got(r.go2.at[xx * 2 + ll], r.s_o5.at[n])
    for mine, theirs, out, last, sem in (
        (r.gcs, r.gc2, r.gcf, r.gc3, r.s_c6), (r.gos, r.go2, r.gof, r.go3, r.s_o6),
    ):
        for j in range(4):
            total = mine[xh, xl, j].astype(F32)
            for xx, ll in x_line:
                total = total + theirs[xx * 2 + ll, j].astype(F32)
            out[j] = total.astype(BF16)
            send(
                out.at[j], last.at[z], sem.at[z], at(y, xh, core, 2 * j + xl),
                unless=diag & (y == j),
            )

    @pl.when(diag)
    def _():
        r.gc3[z] = r.gcf[y]
        r.go3[z] = r.gof[y]

    total = r.ggt[...]
    for k in range(1, 8):
        got(r.gg2.at[w_from[k]], r.s_a2.at[k])
        total = total + r.gg2[w_from[k]]
    r.ggt2[...] = total
    for k in range(1, 8):
        send(r.ggt2, r.gg3.at[c], r.s_a3.at[k], {"seq": s, "ctx": ctx_peer[k]})

    for g in range(2):
        for k in range(1, 8):
            got(r.gp2.at[w_from[k], :, pl.ds(g * 512, 512)], r.s_p2.at[g, k])
    total = r.gpx[rows(D + w * 64, 64), :].astype(F32)
    for k in range(1, 8):
        total = total + r.gp2[w_from[k]].astype(F32)
    for j in range(8):
        r.gpf[j] = total[8 * j : 8 * j + 8, :].astype(BF16)
    for k in range(1, 8):
        send(r.gpf.at[ctx_peer[k]], r.gp3.at[c], r.s_p3.at[k], {"seq": s, "ctx": ctx_peer[k]})
    r.gp3[c] = r.gpf[c]

    for k in range(1, 8):
        got(r.ge3.at[ctx_from[k]], r.s_e3.at[k])
    for j in range(4):
        t = r.ge3[2 * j].astype(F32) + r.ge3[2 * j + 1].astype(F32)
        r.geo[:, j * FL : (j + 1) * FL] = t[:, :FL]
        r.geo[:, FF + j * FL : FF + (j + 1) * FL] = t[:, FL:]
    for j in range(4):

        @pl.when(jnp.logical_not(diag & (z == j)))
        def _():
            got(r.gc3.at[j], r.s_c6.at[j])
            got(r.go3.at[j], r.s_o6.at[j])

    for last, out in ((r.gc3, r.gco), (r.go3, r.goo)):
        out[...] = (last[0].astype(F32) + last[1].astype(F32)) + (
            last[2].astype(F32) + last[3].astype(F32)
        )

    total = r.gh[...]
    g = r.ps[y].astype(F32)
    for k in range(1, 4):
        got(r.r1.at[y_from[k]], r.s_r4.at[y_from[k]])
        g = g + r.r1[y_from[k]].astype(F32)
    v = r.xs[my4, :].astype(F32)
    inv = lax.rsqrt(jnp.mean(v * v, axis=1, keepdims=True) + EPS)
    unit = v * inv
    g = g * gain_a
    r.gt[...] = total + inv * (g - unit * jnp.mean(g * unit, axis=1, keepdims=True))

    for k in range(1, 8):
        got(r.gp3.at[ctx_from[k]], r.s_p3.at[k])
    for j in range(4):
        t = r.gp3[2 * j].astype(F32) + r.gp3[2 * j + 1].astype(F32)
        for place, (start, size) in PLACES:
            n = 0 if start < 512 else 1 if start < 768 else 2
            to = PCOLS[n][0] + j * PCOLS[n][1] + start - PCOLS[n][2]
            r.gpo[:, to : to + size] = t[:, place : place + size]
    total = r.ggt2[...]
    for k in range(1, 8):
        got(r.gg3.at[ctx_from[k]], r.s_a3.at[k])
        total = total + r.gg3[ctx_from[k]]
    r.ggo[...] = total

    finish(list(sends))


def hand_over(ggo, lo, gt, gpo, goo, geo, gco, *refs):
    outs, (ag, fg, hg), kept, sem = refs[:6], refs[6:9], refs[9:15], refs[15]
    ins = (lo, gt, gpo, goo, geo, gco)
    loads = [pltpu.make_async_copy(ins[n], kept[n], sem.at[n]) for n in range(6)]
    stores = [pltpu.make_async_copy(kept[n], outs[n], sem.at[6 + n]) for n in range(6)]
    for cp in loads:
        cp.start()
    for load, store in zip(loads, stores, strict=True):
        load.wait()
        store.start()
    place = 8 * lax.axis_index("seq") + lax.axis_index("ctx")
    row = lax.broadcasted_iota(jnp.int32, (8, 128), 0)
    lane = lax.broadcasted_iota(jnp.int32, (8, 128), 1)
    for n, (ref, size) in enumerate(((ag, 8), (fg, 8), (hg, 2))):
        tile = ggo[8 * n : 8 * n + 8, :]
        got = jnp.zeros((1, size), F32)
        at = lax.broadcasted_iota(jnp.int32, (1, size), 1)
        for j in range(size):
            value = jnp.where(row * 128 + lane == place * size + j, tile, 0.0)
            value = jnp.sum(jnp.sum(value, axis=1, keepdims=True), axis=0, keepdims=True)
            got = jnp.where(at == j, value, got)
        ref[...] = got
    for cp in stores:
        cp.wait()


def per_device(x, dy, segments, positions, ag, proj, hg, out, fg, expn, con):
    del positions
    vmem = pl.BlockSpec(memory_space=pltpu.VMEM)
    hbm = pl.BlockSpec(memory_space=pl.ANY)
    scratch = [pltpu.VMEM(shape, kind) for shape, kind in SCRATCH.values()]
    sems = [pltpu.SemaphoreType.DMA(n if isinstance(n, tuple) else (n,)) for n in RECV.values()]
    res = pl.pallas_call(
        kernel,
        name="layer",
        out_shape=(
            jax.ShapeDtypeStruct((TOK, D), BF16),
            jax.ShapeDtypeStruct((TOK, D), F32),
            jax.ShapeDtypeStruct((8, 4096), F32),
            jax.ShapeDtypeStruct((16, D), F32),
            jax.ShapeDtypeStruct((8, 6144), F32),
            jax.ShapeDtypeStruct((24, D), F32),
            jax.ShapeDtypeStruct((24, 128), F32),
        ),
        in_specs=[hbm] * 6 + [vmem] * 4,
        out_specs=(vmem,) * 7,
        scratch_shapes=scratch
        + sems
        + [pltpu.SemaphoreType.DMA((N_SEND,)), pltpu.SemaphoreType.DMA((16,))],
        compiler_params=pltpu.CompilerParams(
            collective_id=0, has_side_effects=True, vmem_limit_bytes=63 * 2**20
        ),
    )(
        x.reshape(TOK, D), dy.reshape(TOK, D), proj, out, expn, con,
        ag.reshape(1, 8), fg.reshape(1, 8), hg.reshape(1, 2), segments,
    )
    big, gains = res[:6], res[6]
    lo, gt, gpo, goo, geo, gco, gag, gfg, ghg = pl.pallas_call(
        hand_over,
        name="hand_over",
        out_shape=tuple(jax.ShapeDtypeStruct(a.shape, a.dtype) for a in big)
        + tuple(jax.ShapeDtypeStruct((1, n), F32) for n in (8, 8, 2)),
        in_specs=[vmem] + [pl.BlockSpec(memory_space=pltpu.HBM)] * 6,
        out_specs=(pl.BlockSpec(memory_space=pltpu.HBM),) * 6 + (vmem,) * 3,
        scratch_shapes=[pltpu.VMEM(a.shape, a.dtype) for a in big]
        + [pltpu.SemaphoreType.DMA((12,))],
        compiler_params=pltpu.CompilerParams(vmem_limit_bytes=63 * 2**20),
    )(gains, *big)
    return (
        lo.reshape(1, TOK, D),
        gt.reshape(1, TOK, D),
        gag.reshape(8),
        gpo,
        ghg.reshape(2),
        goo,
        gfg.reshape(8),
        geo,
        gco,
    )


def solution(mesh):
    return jax.shard_map(
        per_device,
        mesh=mesh,
        in_specs=(
            P("seq", "ctx", None),
            P("seq", "ctx", None),
            P("seq", None),
            P("seq", "ctx"),
            P(("seq", "ctx")),
            P(("seq", "ctx"), None),
            P(("seq", "ctx")),
            P(("seq", "ctx"), None),
            P(("seq", "ctx")),
            P(("seq", "ctx"), None),
            P(("seq", "ctx"), None),
        ),
        out_specs=(
            P("seq", "ctx", None),
            P("seq", "ctx", None),
            P(("seq", "ctx")),
            P(("seq", "ctx"), None),
            P(("seq", "ctx")),
            P(("seq", "ctx"), None),
            P(("seq", "ctx")),
            P(("seq", "ctx"), None),
            P(("seq", "ctx"), None),
        ),
        check_vma=False,
    )
```

```python
import math

import jax
import jax.numpy as jnp
from jax import lax
from jax.experimental import pallas as pl
from jax.experimental.pallas import tpu as pltpu
from jax.sharding import PartitionSpec as P

F32 = jnp.float32
BF16 = jnp.bfloat16
MESH = pl.DeviceIdType.MESH
EPS = 1e-06
THETA = 1000000.0
NEGATIVE = -1e30
D = 1024
HEAD = 128
FF = 3072
FL = 768
TOK = 128
SEQ = 1024
QB = 256
SCALE = HEAD**-0.5


def dot(a, b, da=1, db=0):
    return lax.dot_general(a, b, (((da,), (db,)), ((), ())), preferred_element_type=F32)


def rows(start, size):
    return pl.ds(pl.multiple_of(start, size), size)


SCRATCH = dict(
    pa=((8, 8, D), BF16),
    pw=((8, 2, 64, D), BF16),
    ea=((8, 8, 1536), BF16),
    ew=((4, 2, 2, 64, 1536), BF16),
    ow=((2, 2, 4, 2, 16, D), BF16),
    cb=((2, 2, 4, 2, 24, D), BF16),
    cw=((FL, D), BF16),
    gi=((24, 128), F32),
    ga=((8, 24, 128), F32),
    gb=((8, 24, 128), F32),
    gsum=((24, 128), F32),
    gacc=((24, 128), F32),
    gfr=((24, 128), F32),
    gall=((24, 128), F32),
    cos=((512, HEAD), F32),
    sin=((512, HEAD), F32),
    segc=((QB, 128), jnp.int32),
    xs=((512, D), BF16),
    ns=((512, D), BF16),
    pj=((512, 768), F32),
    qs=((2, 4, QB, HEAD), BF16),
    kv=((8, 4, TOK, HEAD), BF16),
    mx=((512, 512), BF16),
    ps=((4, TOK, D), BF16),
    r1=((4, TOK, D), BF16),
    hid=((TOK, D), F32),
    nm=((512, D), BF16),
    dy=((512, D), BF16),
    act=((512, FL), BF16),
    ggu=((512, 1536), BF16),
    gs=((4, TOK, D), BF16),
    r2=((4, TOK, D), BF16),
    los=((4, TOK, D), BF16),
    r3=((4, TOK, D), BF16),
    gh=((TOK, D), F32),
    g4=((512, D), BF16),
    gm=((2, 4, QB, HEAD), BF16),
    f4=((4096, HEAD), F32),
    dq=((2, 4, QB, HEAD), F32),
    ds=((2, 4, 2, TOK, HEAD), BF16),
    dr=((2, 4, 2, TOK, HEAD), BF16),
    gp=((512, D), BF16),
    attg=((1, D), F32),
    hgq=((1, HEAD), F32),
    hgk=((1, HEAD), F32),
    gg0=((24, 128), F32),
    gg1=((24, 128), F32),
    ggt=((24, 128), F32),
    ggt2=((24, 128), F32),
    gg2=((8, 24, 128), F32),
    gg3=((8, 24, 128), F32),
    ge=((2, 8, 64, 1536), BF16),
    ge1=((8, 64, 1536), BF16),
    ges=((8, 64, 1536), BF16),
    ge2=((4, 2, 64, 1536), BF16),
    get=((2, 64, 1536), BF16),
    gex=((64, 1536), BF16),
    gef=((8, 8, 1536), BF16),
    ge3=((8, 8, 1536), BF16),
    gc=((2, 2, 8, 24, D), BF16),
    gc1=((2, 8, 24, D), BF16),
    gcs=((2, 2, 4, 24, D), BF16),
    gc2=((4, 4, 24, D), BF16),
    gcf=((4, 24, D), BF16),
    gc3=((4, 24, D), BF16),
    go=((2, 2, 8, 16, D), BF16),
    go1=((2, 8, 16, D), BF16),
    gos=((2, 2, 4, 16, D), BF16),
    go2=((4, 4, 16, D), BF16),
    gof=((4, 16, D), BF16),
    go3=((4, 16, D), BF16),
    gpx=((1536, D), BF16),
    gp1=((512, D), BF16),
    gp2=((8, 64, D), BF16),
    gpf=((8, 8, D), BF16),
    gp3=((8, 8, D), BF16),
)
RECV = dict(
    pa=(8, 2), ea=8, ga=8, gb=8, gfr=1, x=4, dy=4, pb=(2, 8), eb=(2, 4), ps=2, es=2,
    o1=4, o2=4, o3=2, c1=4, c2=4, c3=2, kv=4, r1=4, nm=4, r2=4, r3=4, g4=4, dr=(2, 4), r4=4,
    e1=1, e2=4, ex=1, e3=8, c4=2, c5=4, c6=4, o4=2, o5=4, o6=4, p1=2, p2=(2, 8), p3=8, a1=1, a2=8, a3=8,
)
N_SEND = 88
NAMES = (
    ["x", "dyi", "pi", "oi", "ei", "ci", "agi", "fgi", "hgi", "segr"]
    + ["lo", "gt", "gpo", "goo", "geo", "gco", "ggo"]
    + list(SCRATCH)
    + ["s_" + n for n in RECV]
    + ["send", "loc"]
)
PLACES = (
    (0, (0, 256)), (256, (512, 128)), (384, (768, 128)),
    (512, (256, 256)), (768, (640, 128)), (896, (896, 128)),
)
HEADS = (0, 128, 256, 384, 512, 768)
PCOLS = ((0, 512, 0), (2048, 256, 512), (3072, 256, 768))


class Box:
    pass


def kernel(*refs):
    r = Box()
    for name, ref in zip(NAMES, refs, strict=True):
        setattr(r, name, ref)
    s, c = lax.axis_index("seq"), lax.axis_index("ctx")
    z, xh, core = s // 4, (s // 2) % 2, s % 2
    y, xl = c // 2, c % 2
    w = s // 2
    sib = 1 - core

    def at(zz, xx, cc, ctx):
        return {"seq": zz * 4 + xx * 2 + cc, "ctx": ctx}

    def on_w(ww, cc, ctx):
        return {"seq": ww * 2 + cc, "ctx": ctx}

    me_sib = on_w(w, sib, c)
    ctx_peer = [None] + [lax.rem(c + k, 8) for k in range(1, 8)]
    ctx_from = [None] + [lax.rem(c + 8 - k, 8) for k in range(1, 8)]
    w_peer = [None] + [lax.rem(w + k, 8) for k in range(1, 8)]
    w_from = [None] + [lax.rem(w + 8 - k, 8) for k in range(1, 8)]
    y_peer = [None] + [lax.rem(y + k, 4) for k in range(1, 4)]
    y_from = [None] + [lax.rem(y + 4 - k, 4) for k in range(1, 4)]
    z_peer = [None] + [lax.rem(z + k, 4) for k in range(1, 4)]
    z_from = [None] + [lax.rem(z + 4 - k, 4) for k in range(1, 4)]
    x_line = [(xh, 1 - xl), (1 - xh, xl), (1 - xh, 1 - xl)]
    diag = y == z

    def e_block(zz, xx, cc):
        return r.ew.at[zz, xx, cc]

    def all_p(start, stop):
        return r.pw[:, :, :, start:stop].reshape(D, stop - start)

    def all_e():
        return r.ew[...].reshape(D, 1536)

    def all_o():
        return r.ow[...].reshape(512, D)

    free, sends = list(range(N_SEND - 1)), []

    def send(src, dst, sem, dev, unless=None):
        at = free.pop(0)
        cp = pltpu.make_async_remote_copy(
            src_ref=src, dst_ref=dst, send_sem=r.send.at[at], recv_sem=sem,
            device_id=dev, device_id_type=MESH,
        )
        sends.append((cp, unless, at))
        if unless is None:
            cp.start()
        else:
            pl.when(jnp.logical_not(unless))(cp.start)

    def finish(some):
        for entry in some:
            cp, unless, at = entry
            if unless is None:
                cp.wait_send()
            else:
                pl.when(jnp.logical_not(unless))(cp.wait_send)
            free.append(at)
        sends[:] = [e for e in sends if not any(e is f for f in some)]

    def got(dst, sem):
        pltpu.make_async_remote_copy(
            src_ref=dst, dst_ref=dst, send_sem=r.send.at[N_SEND - 1], recv_sem=sem,
            device_id=me_sib, device_id_type=MESH,
        ).wait_recv()

    bar = pltpu.get_barrier_semaphore()

    def greet(dev):
        pl.semaphore_signal(bar, inc=1, device_id=dev, device_id_type=MESH)

    greet(me_sib)
    for k in range(1, 8):
        greet({"seq": s, "ctx": ctx_peer[k]})
        greet(on_w(w_peer[k], core, c))
    greet(at(z, x_line[2][0], core, 2 * y + x_line[2][1]))
    for zz in range(4):

        @pl.when(jnp.logical_not(diag & (z == zz)))
        def _():
            greet(at(zz, xh, core, 2 * z + xl))
            greet(at(y, xh, core, 2 * zz + xl))

    own = []

    def own_copy(src, dst):
        cp = pltpu.make_async_copy(src, dst, r.loc.at[len(own)])
        own.append(cp)
        cp.start()

    my4 = rows(y * TOK, TOK)
    own_copy(r.x, r.xs.at[my4])
    own_copy(r.dyi, r.dy.at[my4])
    for start, size, place in PCOLS:
        own_copy(
            r.pi.at[:, pl.ds(pl.multiple_of(start + y * size, size), size)],
            r.pa.at[c, :, pl.ds(place, size)],
        )
    for part in range(2):
        own_copy(
            r.ei.at[:, pl.ds(pl.multiple_of(part * FF + y * FL, FL), FL)],
            r.ea.at[c, :, pl.ds(part * FL, FL)],
        )

    tile_row = lax.broadcasted_iota(jnp.int32, (8, 128), 0)
    tile_lane = lax.broadcasted_iota(jnp.int32, (8, 128), 1)
    flat = tile_row * 128 + tile_lane
    place = 8 * s + c
    for n, (ref, size) in enumerate(((r.agi, 8), (r.fgi, 8), (r.hgi, 2))):
        values = ref[...].astype(F32)
        tile = jnp.zeros((8, 128), F32)
        for j in range(size):
            tile = jnp.where(flat == place * size + j, values[:, j : j + 1], tile)
        r.gi[8 * n : 8 * n + 8, :] = tile

    pl.semaphore_wait(bar, 24 - jnp.where(diag, 2, 0))

    for k in range(1, 8):
        send(r.gi, r.ga.at[c], r.s_ga.at[k], {"seq": s, "ctx": ctx_peer[k]})
    for part in (1, 2, 0):
        start, size, place = PCOLS[part]
        for k in range(1, 8):
            to = ctx_peer[k]
            send(
                r.pi.at[:, pl.ds(pl.multiple_of(start + (to // 2) * size, size), size)],
                r.pa.at[c, :, pl.ds(place, size)],
                r.s_pa.at[k, min(part, 1)],
                {"seq": s, "ctx": to},
            )
    for k in (1, 3):
        send(r.x, r.xs.at[my4], r.s_x.at[k], {"seq": s, "ctx": 2 * y_peer[k] + xl})

    @pl.when(diag)
    def _():
        a = pltpu.make_async_copy(
            r.oi,
            r.ow.at[xh, core, y, xl],
            r.loc.at[14],
        )
        b = pltpu.make_async_copy(r.ci, r.cb.at[xh, core, y, xl], r.loc.at[15])
        a.start()
        b.start()
        a.wait()
        b.wait()

    for cp in own:
        cp.wait()

    lane = lax.broadcasted_iota(jnp.int32, (1, HEAD), 1)
    index = jnp.where(lane < HEAD // 2, lane, lane - HEAD // 2).astype(F32)
    inverse = jnp.exp(index * (-2.0 / HEAD * math.log(THETA)))
    sign = jnp.where(lane < HEAD // 2, -1.0, 1.0)
    eye = lax.broadcasted_iota(jnp.int32, (TOK, TOK), 0) == lax.broadcasted_iota(
        jnp.int32, (TOK, TOK), 1
    )
    for j in range(4):
        b = pl.ds(j * TOK, TOK)
        seg = r.segr[:, pl.ds(pl.multiple_of((2 * j + xl) * TOK, TOK), TOK)]
        seg = jnp.sum(jnp.where(eye, seg.astype(F32), 0.0), axis=1, keepdims=True)
        r.segc[:, j : j + 1] = jnp.concatenate([seg, seg], 0).astype(jnp.int32)
        before = jnp.sum((r.segr[...].astype(F32) < seg).astype(F32), axis=1, keepdims=True)
        t = lax.broadcasted_iota(jnp.int32, (TOK, 1), 0) + (2 * j + xl) * TOK
        phase = (t.astype(F32) - before) * inverse
        r.cos[b, :] = jnp.cos(phase)
        r.sin[b, :] = jnp.sin(phase) * sign

    kv_half, q_half = pl.ds(512, 512), pl.ds(0, 512)

    def spread(n, half):
        blk = r.pw.at[w, core, :, half]
        for k in range(1, 8):
            send(blk, blk, r.s_pb.at[n, k], on_w(w_peer[k], core, c))

    def pass_on(n, half):
        for k in range(1, 8):
            got(r.pw.at[w_from[k], core, :, half], r.s_pb.at[n, k])
        blk = r.pw.at[:, core, :, half]
        send(blk, blk, r.s_ps.at[n], me_sib)

    def from_sibling(n, half):
        got(r.pw.at[:, sib, :, half], r.s_ps.at[n])

    def joined(start, size):
        return jnp.concatenate(
            [r.pa[j, :, start : start + size].astype(F32) for j in range(8)], 0
        ).astype(BF16)

    total = r.gi[...]
    for k in range(1, 8):
        got(r.ga.at[ctx_from[k]], r.s_ga.at[k])
        total = total + r.ga[ctx_from[k]]
    r.gsum[...] = total
    for k in range(1, 8):
        send(r.gsum, r.gb.at[w], r.s_gb.at[k], on_w(w_peer[k], core, c))
    for k in range(1, 8):
        got(r.pa.at[ctx_from[k], :, kv_half], r.s_pa.at[k, 1])
    for g in range(2):
        r.pw[w, core, :, 512 + g * 256 : 640 + g * 256] = joined(512 + g * 128, 128)
        r.pw[w, core, :, 640 + g * 256 : 768 + g * 256] = joined(768 + g * 128, 128)
    first_sends = list(sends)
    spread(0, kv_half)
    send(r.x, r.xs.at[my4], r.s_x.at[2], {"seq": s, "ctx": 2 * y_peer[2] + xl})
    for k in range(1, 8):
        to = ctx_peer[k]
        for part in range(2):
            send(
                r.ei.at[:, pl.ds(pl.multiple_of(part * FF + (to // 2) * FL, FL), FL)],
                r.ea.at[c, :, pl.ds(part * FL, FL)],
                r.s_ea.at[k],
                {"seq": s, "ctx": to},
            )
    for k in range(1, 8):
        got(r.pa.at[ctx_from[k], :, q_half], r.s_pa.at[k, 0])
    r.pw[w, core, :, 0:512] = joined(0, 512)
    total = r.gsum[...]
    for k in range(1, 8):
        got(r.gb.at[w_from[k]], r.s_gb.at[k])
        total = total + r.gb[w_from[k]]
    r.gacc[...] = total
    send(r.gacc, r.gfr, r.s_gfr.at[0], me_sib)
    for zz in range(4):
        send(
            r.oi,
            r.ow.at[xh, core, y, xl],
            r.s_o1.at[y],
            at(zz, xh, core, 2 * z + xl),
            unless=diag & (z == zz),
        )
    pass_on(0, kv_half)
    spread(1, q_half)
    got(r.gfr, r.s_gfr.at[0])
    r.gall[...] = r.gacc[...] + r.gfr[...]
    from_sibling(0, kv_half)

    def wide(first):
        return jnp.concatenate([r.gall[first + j : first + j + 1, :] for j in range(8)], 1)

    gain_a, gain_f = wide(0), wide(8)
    gain_q, gain_k = r.gall[16:17, :], r.gall[17:18, :]

    def turn(v):
        return pltpu.roll(v, HEAD // 2, 1)

    x_partner = {"seq": s, "ctx": 2 * y + 1 - xl}
    def headed(u, b, h):
        r.pj[b, h * HEAD : (h + 1) * HEAD] = u
        ui = lax.rsqrt(jnp.mean(u * u, axis=1, keepdims=True) + EPS)
        u = u * ui * (gain_q if h < 4 else gain_k)
        return (u * r.cos[b, :] + turn(u) * r.sin[b, :]).astype(BF16)

    for k in (0, 1, 3, 2):
        j = y if k == 0 else y_from[k]
        b = rows(j * TOK, TOK)
        if k:
            got(r.xs.at[b], r.s_x.at[k])
        v = r.xs[b, :].astype(F32)
        inv = lax.rsqrt(jnp.mean(v * v, axis=1, keepdims=True) + EPS)
        n = (v * inv * gain_a).astype(BF16)
        r.ns[b, :] = n
        out = dot(n, all_p(512, D))
        mine = 2 * j + xl
        for g in range(2):
            r.kv[mine, g] = headed(out[:, g * 256 : g * 256 + HEAD], b, 4 + g)
            r.kv[mine, 2 + g] = out[:, g * 256 + HEAD : g * 256 + 256].astype(BF16)
        send(r.kv.at[mine], r.kv.at[mine], r.s_kv.at[j], x_partner)

    for k in (1, 3, 2):
        send(r.dyi, r.dy.at[my4], r.s_dy.at[k], {"seq": s, "ctx": 2 * y_peer[k] + xl})

    for k in range(1, 8):
        got(r.ea.at[ctx_from[k]], r.s_ea.at[k])
    r.ew[z, xh, core] = jnp.concatenate([r.ea[j].astype(F32) for j in range(8)], 0).astype(BF16)
    own_e = r.ew.at[z, xh, core]
    for k in (1, 3, 2):
        send(own_e, own_e, r.s_eb.at[0, k], at(z_peer[k], xh, core, c))
    for zz in range(4):
        send(
            r.ci,
            r.cb.at[xh, core, y, xl],
            r.s_c1.at[y],
            at(zz, xh, core, 2 * z + xl),
            unless=diag & (z == zz),
        )

    pass_on(1, q_half)
    from_sibling(1, q_half)
    for j in range(4):
        b = pl.ds(j * TOK, TOK)
        out = dot(r.ns[b, :], all_p(0, 512))
        for h in range(4):
            u = headed(out[:, h * HEAD : (h + 1) * HEAD], b, h)
            r.qs[h // 2, j, pl.ds((h % 2) * TOK, TOK), :] = u
    finish(first_sends)

    for j in range(4):

        @pl.when(jnp.logical_not(diag & (y == j)))
        def _():
            got(r.ow.at[xh, core, j, xl], r.s_o1.at[j])

    blk = r.ow.at[xh, core, :, xl]
    for n, (xx, ll) in enumerate(x_line):
        send(blk, blk, r.s_o2.at[n], at(z, xx, core, 2 * y + ll))
    send(own_e, own_e, r.s_eb.at[0, 0], at(z, 1 - xh, core, c))


    def mask(j):
        n = (2 * j + 2) * TOK
        row = lax.broadcasted_iota(jnp.int32, (QB, n), 0)
        t = (2 * j + xl) * TOK + jnp.where(row < TOK, row, row - TOK)
        u = lax.broadcasted_iota(jnp.int32, (QB, n), 1)
        return (u <= t) & (r.segr[:, :n] == r.segc[:, j : j + 1])

    def at_p(g, j):
        n = (2 * j + 2) * TOK
        if j == 1:
            return r.gpx.at[D : D + QB, g * n : (g + 1) * n]
        first = g * QB + (0 if j == 3 else 2 * QB)
        return r.gpx.at[first : first + QB, 0:n] if j else r.gpx.at[first : first + QB, D - n : D]

    def keys(h, j):
        n = 2 * j + 2
        return r.kv[:n, h].reshape(n * TOK, HEAD)

    for j in range(4):
        got(r.kv.at[2 * j + 1 - xl], r.s_kv.at[j])
        ok = mask(j)
        b = pl.ds(j * TOK, TOK)
        for g in range(2):
            sc = dot(r.qs[g, j], keys(g, j), 1, 1) * SCALE
            sc = jnp.where(ok, sc, NEGATIVE)
            top = jnp.max(sc, axis=1, keepdims=True)
            e = jnp.exp(sc - top)
            tot = jnp.sum(e, axis=1, keepdims=True)
            p = (e * (1.0 / tot)).astype(BF16)
            at_p(g, j)[...] = p
            o = dot(p, keys(2 + g, j)).astype(BF16)
            r.mx[b, (2 * g) * HEAD : (2 * g + 1) * HEAD] = o[:TOK, :]
            r.mx[b, (2 * g + 1) * HEAD : (2 * g + 2) * HEAD] = o[TOK:, :]
        if j == 2:
            for n, (xx, ll) in enumerate(x_line):
                got(r.ow.at[xx, core, :, ll], r.s_o2.at[n])
            for n in range(2):
                send(r.ow.at[n, core], r.ow.at[n, core], r.s_o3.at[n], me_sib)
    for n in range(2):
        got(r.ow.at[n, sib], r.s_o3.at[n])
    for k in (2, 1, 3, 0):
        j = y_peer[k] if k else y
        r.ps[j] = dot(r.mx[rows(j * TOK, TOK), :], all_o()).astype(BF16)
        if k:
            send(r.ps.at[j], r.r1.at[y], r.s_r1.at[y], {"seq": s, "ctx": 2 * j + xl})

    blk = e_block(z, 1 - xh, core)
    got(blk, r.s_eb.at[0, 0])
    for k in (1, 3, 2):
        send(blk, blk, r.s_eb.at[1, k], at(z_peer[k], xh, core, c))
    for k in (1, 3, 2):
        got(e_block(z_from[k], xh, core), r.s_eb.at[0, k])
    blk = r.ew.at[:, xh, core]
    send(blk, blk, r.s_es.at[0], me_sib)
    for j in range(4):

        @pl.when(jnp.logical_not(diag & (y == j)))
        def _():
            got(r.cb.at[xh, core, j, xl], r.s_c1.at[j])

    blk = r.cb.at[xh, core, :, xl]
    for n, (xx, ll) in enumerate(x_line):
        send(blk, blk, r.s_c2.at[n], at(z, xx, core, 2 * y + ll))

    hidden = r.xs[my4, :].astype(F32) + r.ps[y].astype(F32)
    for k in range(1, 4):
        got(r.r1.at[y_from[k]], r.s_r1.at[y_from[k]])
        hidden = hidden + r.r1[y_from[k]].astype(F32)
    r.hid[...] = hidden
    inv_h = lax.rsqrt(jnp.mean(hidden * hidden, axis=1, keepdims=True) + EPS)
    r.nm[my4, :] = (hidden * inv_h * gain_f).astype(BF16)
    def send_nm(k):
        send(
            r.nm.at[my4], r.nm.at[my4], r.s_nm.at[k], {"seq": s, "ctx": 2 * y_peer[k] + xl}
        )

    older = list(sends)
    send_nm(1)
    send_nm(3)
    for k in (1, 3, 2):
        got(e_block(z_from[k], 1 - xh, core), r.s_eb.at[1, k])
    blk = r.ew.at[:, 1 - xh, core]
    send(blk, blk, r.s_es.at[1], me_sib)

    for n, (xx, ll) in enumerate(x_line):
        got(r.cb.at[xx, core, :, ll], r.s_c2.at[n])
    for n in range(2):
        send(r.cb.at[n, core], r.cb.at[n, core], r.s_c3.at[n], me_sib)
    for k in range(1, 4):
        got(r.dy.at[rows(y_from[k] * TOK, TOK)], r.s_dy.at[k])
    finish(older)
    for n in range(2):
        got(r.cb.at[n, sib], r.s_c3.at[n])
    got(r.ew.at[:, xh, sib], r.s_es.at[0])
    got(r.ew.at[:, 1 - xh, sib], r.s_es.at[1])
    for j in range(16):
        r.cw[48 * j : 48 * j + 48, :] = jnp.concatenate(
            [r.cb[j // 8, j // 4 % 2, j % 4, n].astype(F32) for n in range(2)], 0
        ).astype(BF16)

    def grad_act(k, _):
        b = rows(k * TOK, TOK)
        g = dot(r.dy[b, :], r.cw[...], 1, 1)
        for h in range(6):
            r.f4[rows(h * 512 + k * TOK, TOK), :] = g[:, h * HEAD : (h + 1) * HEAD]
        return 0

    lax.fori_loop(0, 4, grad_act, 0)

    for k in (0, 1, 3, 2):
        b4 = y if k == 0 else y_from[k]
        b = rows(b4 * TOK, TOK)
        if k:
            got(r.nm.at[b], r.s_nm.at[k])
        gu = dot(r.nm[b, :], all_e())
        gate, up = gu[:, :FL], gu[:, FL:]
        sg = 1.0 / (1.0 + jnp.exp(-gate))
        sl = gate * sg
        r.act[b, :] = (sl * up).astype(BF16)
        gt = jnp.concatenate([r.f4[rows(h * 512 + b4 * TOK, TOK), :] for h in range(6)], 1)
        r.ggu[b, :FL] = (gt * up * sg * (1.0 + gate * (1.0 - sg))).astype(BF16)
        r.ggu[b, FL:] = (gt * sl).astype(BF16)
        r.gs[b4] = dot(r.ggu[b, :], all_e(), 1, 1).astype(BF16)
        if k == 0:
            send_nm(2)
        if k:
            send(r.gs.at[b4], r.r2.at[y], r.s_r2.at[k], {"seq": s, "ctx": 2 * b4 + xl})
    for k in (0, 1, 3, 2):
        b4 = y if k == 0 else y_from[k]
        r.los[b4] = dot(r.act[rows(b4 * TOK, TOK), :], r.cw[...]).astype(BF16)

    for j in range(4):
        g = dot(r.nm[:, j * 256 : (j + 1) * 256], r.ggu[...], 0, 0).astype(BF16)
        for q in range(4):
            r.ge[q % 2, 2 * j + q // 2] = g[64 * q : 64 * q + 64, :]
    send(r.ge.at[sib], r.ge1, r.s_e1.at[0], me_sib)
    for j in range(2):
        g = dot(r.act[:, j * 384 : (j + 1) * 384], r.dy[...], 0, 0)
        for q in range(16):
            r.gc[q // 8, j, q % 8] = g[24 * q : 24 * q + 24, :].astype(BF16)
    for j in range(2):
        send(r.gc.at[sib, j], r.gc1.at[j], r.s_c4.at[j], me_sib)

    g_mlp = r.gs[y].astype(F32)
    for k in range(1, 4):
        got(r.r2.at[y_peer[k]], r.s_r2.at[k])
        g_mlp = g_mlp + r.r2[y_peer[k]].astype(F32)
    hidden = r.hid[...]
    inv_h = lax.rsqrt(jnp.mean(hidden * hidden, axis=1, keepdims=True) + EPS)
    unit = hidden * inv_h
    feed = jnp.sum(g_mlp * unit, axis=0, keepdims=True)
    g = g_mlp * gain_f
    g = r.dy[my4, :].astype(F32) + inv_h * (g - unit * jnp.mean(g * unit, axis=1, keepdims=True))
    r.gh[...] = g
    r.g4[my4, :] = g.astype(BF16)
    def send_g4(k):
        send(
            r.g4.at[my4], r.g4.at[my4], r.s_g4.at[k], {"seq": s, "ctx": 2 * y_peer[k] + xl}
        )

    send_g4(1)
    send_g4(3)
    r.gg0[...] = jnp.zeros((24, 128), F32)
    for j in range(8):
        r.gg0[8 + j : 9 + j, :] = feed[:, 128 * j : 128 * j + 128]

    got(r.ge1, r.s_e1.at[0])

    def pair_e(j, _):
        r.ges[j] = (r.ge[core, j].astype(F32) + r.ge1[j].astype(F32)).astype(BF16)
        return 0

    lax.fori_loop(0, 8, pair_e, 0)
    for k in (1, 3, 2):
        send(
            r.ges.at[pl.ds(pl.multiple_of(2 * z_peer[k], 2), 2)], r.ge2.at[z], r.s_e2.at[k],
            at(z_peer[k], xh, core, c),
        )
    for j in range(2):
        got(r.gc1.at[j], r.s_c4.at[j])
        for q in range(8):
            r.gcs[j, q % 2, q // 2] = (
                r.gc[core, j, q].astype(F32) + r.gc1[j, q].astype(F32)
            ).astype(BF16)
    for n, (xx, ll) in enumerate(x_line):
        send(
            r.gcs.at[xx, ll], r.gc2.at[xh * 2 + xl], r.s_c5.at[n],
            at(z, xx, core, 2 * y + ll),
        )

    send_g4(2)

    for k in (0, 1, 3, 2):
        j = y if k == 0 else y_from[k]
        b = rows(j * TOK, TOK)
        if k:
            got(r.g4.at[b], r.s_g4.at[k])
        gm = dot(r.g4[b, :], all_o(), 1, 1).astype(BF16)
        for h in range(4):
            r.gm[h // 2, j, pl.ds((h % 2) * TOK, TOK), :] = gm[:, h * HEAD : (h + 1) * HEAD]

    older = list(sends)
    for k in (1, 3, 2):
        b4 = y_from[k]
        send(r.los.at[b4], r.r3.at[y], r.s_r3.at[k], {"seq": s, "ctx": 2 * b4 + xl})

    for j in range(2):
        g = dot(r.mx[:, j * 256 : (j + 1) * 256], r.g4[...], 0, 0).astype(BF16)
        for q in range(16):
            r.go[q // 8, j, q % 8] = g[16 * q : 16 * q + 16, :]
    for j in range(2):
        send(r.go.at[sib, j], r.go1.at[j], r.s_o4.at[j], me_sib)

    for g in range(2):
        for j in (3, 2, 1, 0):
            n = (2 * j + 2) * TOK
            q, kk, gmh = r.qs[g, j], keys(g, j), r.gm[g, j]
            low = at_p(g, j)[...]
            p = low.astype(F32)
            gat = dot(gmh, keys(2 + g, j), 1, 1)
            ds = (p * (gat - jnp.sum(p * gat, axis=1, keepdims=True))).astype(BF16)
            r.dq[g, j] = dot(ds, kk) * SCALE
            dk = dot(ds, q, 0, 0) * SCALE
            dv = dot(low, gmh, 0, 0)
            kr, vr = g * SEQ, (2 + g) * SEQ
            if j == 3:
                r.f4[kr : kr + n, :] = dk
                r.f4[vr : vr + n, :] = dv
            else:
                r.f4[kr : kr + n, :] += dk
                r.f4[vr : vr + n, :] += dv
            theirs = (2 * j + 1 - xl) * TOK
            r.ds[g, j, 0] = r.f4[rows(kr + theirs, TOK), :].astype(BF16)
            r.ds[g, j, 1] = r.f4[rows(vr + theirs, TOK), :].astype(BF16)
            send(r.ds.at[g, j], r.dr.at[g, j], r.s_dr.at[g, j], x_partner)
            if g or j != 3:
                continue
            for j in range(2):
                got(r.go1.at[j], r.s_o4.at[j])
                for q in range(8):
                    r.gos[j, q % 2, q // 2] = (
                        r.go[core, j, q].astype(F32) + r.go1[j, q].astype(F32)
                    ).astype(BF16)
            for n, (xx, ll) in enumerate(x_line):
                send(
                    r.gos.at[xx, ll], r.go2.at[xh * 2 + xl], r.s_o5.at[n],
                    at(z, xx, core, 2 * y + ll),
                )

    total = r.hid[...] + r.los[y].astype(F32)
    for k in range(1, 4):
        got(r.r3.at[y_peer[k]], r.s_r3.at[k])
        total = total + r.r3[y_peer[k]].astype(F32)
    r.lo[...] = total.astype(BF16)

    r.attg[...] = jnp.zeros((1, D), F32)
    r.hgq[...] = jnp.zeros((1, HEAD), F32)
    r.hgk[...] = jnp.zeros((1, HEAD), F32)

    def norms(g, j):
        b = rows(j * TOK, TOK)
        mine = (2 * j + xl) * TOK
        cosine, sine = r.cos[b, :], r.sin[b, :]
        got(r.dr.at[g, j], r.s_dr.at[g, j])
        for h in (2 * g, 2 * g + 1, 4 + g):
            if h < 4:
                wv = r.dq[g, j, (h % 2) * TOK : (h % 2 + 1) * TOK, :]
            else:
                wv = r.f4[rows(g * SEQ + mine, TOK), :] + r.dr[g, j, 0].astype(F32)
            gn = wv * cosine - turn(wv) * sine
            v = r.pj[b, h * HEAD : (h + 1) * HEAD]
            inv = lax.rsqrt(jnp.mean(v * v, axis=1, keepdims=True) + EPS)
            unit = v * inv
            acc = r.hgq if h < 4 else r.hgk
            acc[...] += jnp.sum(gn * unit, axis=0, keepdims=True)
            t = gn * (gain_q if h < 4 else gain_k)
            gx = inv * (t - unit * jnp.mean(t * unit, axis=1, keepdims=True))
            r.gp[b, HEADS[h] : HEADS[h] + HEAD] = gx.astype(BF16)
        r.gp[b, 640 + g * 256 : 768 + g * 256] = (
            r.f4[rows((2 + g) * SEQ + mine, TOK), :] + r.dr[g, j, 1].astype(F32)
        ).astype(BF16)

    def grad_projection(g):
        half = pl.ds(g * 512, 512)
        for j in range(4):
            left = r.ns[:, j * 256 : (j + 1) * 256]
            for n in range(2):
                t = dot(left, r.gp[:, n * 512 + g * 256 : n * 512 + (g + 1) * 256], 0, 0)
                t = t.astype(BF16)
                at_lane = g * 512 + n * 256
                for q in range(4):
                    first = (q % 2) * 512 + (2 * j + q // 2) * 64
                    r.gpx[first : first + 64, at_lane : at_lane + 256] = t[64 * q : 64 * q + 64, :]
        send(r.gpx.at[rows(sib * 512, 512), half], r.gp1.at[:, half], r.s_p1.at[g], me_sib)

    def pair_projection(g):
        half = pl.ds(g * 512, 512)
        got(r.gp1.at[:, half], r.s_p1.at[g])
        r.gpx[D:, half] = (
            r.gpx[rows(core * 512, 512), half].astype(F32) + r.gp1[:, half].astype(F32)
        ).astype(BF16)
        for k in range(1, 8):
            send(
                r.gpx.at[rows(D + w_peer[k] * 64, 64), half], r.gp2.at[w, :, half],
                r.s_p2.at[g, k], on_w(w_peer[k], core, c),
            )

    finish(older)
    for j in (3, 2, 1, 0):
        norms(0, j)
    grad_projection(0)
    for j in (3, 2, 1, 0):
        norms(1, j)
    grad_projection(1)
    pair_projection(0)
    for k in (1, 3, 2):
        got(r.ge2.at[z_from[k]], r.s_e2.at[k])
    for xx in range(2):
        total = r.ges[2 * z + xx].astype(F32)
        for k in range(1, 4):
            total = total + r.ge2[z_from[k], xx].astype(F32)
        r.get[xx] = total.astype(BF16)
    send(r.get.at[1 - xh], r.gex, r.s_ex.at[0], at(z, 1 - xh, core, c))

    for k in (2, 1, 3, 0):
        j = y_peer[k] if k else y
        b = rows(j * TOK, TOK)
        part = dot(r.gp[b, :], all_p(0, D), 1, 1)
        r.ps[j] = part.astype(BF16)
        if k:
            send(r.ps.at[j], r.r1.at[y], r.s_r4.at[y], {"seq": s, "ctx": 2 * j + xl})
        v = r.xs[b, :].astype(F32)
        inv = lax.rsqrt(jnp.mean(v * v, axis=1, keepdims=True) + EPS)
        r.attg[...] += jnp.sum(part * (v * inv), axis=0, keepdims=True)

    for j in range(8):
        r.gg0[j : j + 1, :] = r.attg[:, 128 * j : 128 * j + 128]
    r.gg0[16:17, :] = r.hgq[...]
    r.gg0[17:18, :] = r.hgk[...]
    send(r.gg0, r.gg1, r.s_a1.at[0], me_sib)

    got(r.gg1, r.s_a1.at[0])
    r.ggt[...] = r.gg0[...] + r.gg1[...]
    for k in range(1, 8):
        send(r.ggt, r.gg2.at[w], r.s_a2.at[k], on_w(w_peer[k], core, c))

    pair_projection(1)

    got(r.gex, r.s_ex.at[0])
    total = r.get[xh].astype(F32) + r.gex[...].astype(F32)
    for j in range(8):
        r.gef[j] = total[8 * j : 8 * j + 8, :].astype(BF16)
    for k in range(1, 8):
        send(r.gef.at[ctx_peer[k]], r.ge3.at[c], r.s_e3.at[k], {"seq": s, "ctx": ctx_peer[k]})
    r.ge3[c] = r.gef[c]
    for n, (xx, ll) in enumerate(x_line):
        got(r.gc2.at[xx * 2 + ll], r.s_c5.at[n])
    for n, (xx, ll) in enumerate(x_line):
        got(r.go2.at[xx * 2 + ll], r.s_o5.at[n])
    for mine, theirs, out, last, sem in (
        (r.gcs, r.gc2, r.gcf, r.gc3, r.s_c6), (r.gos, r.go2, r.gof, r.go3, r.s_o6),
    ):
        for j in range(4):
            total = mine[xh, xl, j].astype(F32)
            for xx, ll in x_line:
                total = total + theirs[xx * 2 + ll, j].astype(F32)
            out[j] = total.astype(BF16)
            send(
                out.at[j], last.at[z], sem.at[z], at(y, xh, core, 2 * j + xl),
                unless=diag & (y == j),
            )

    @pl.when(diag)
    def _():
        r.gc3[z] = r.gcf[y]
        r.go3[z] = r.gof[y]

    total = r.ggt[...]
    for k in range(1, 8):
        got(r.gg2.at[w_from[k]], r.s_a2.at[k])
        total = total + r.gg2[w_from[k]]
    r.ggt2[...] = total
    for k in range(1, 8):
        send(r.ggt2, r.gg3.at[c], r.s_a3.at[k], {"seq": s, "ctx": ctx_peer[k]})

    for g in range(2):
        for k in range(1, 8):
            got(r.gp2.at[w_from[k], :, pl.ds(g * 512, 512)], r.s_p2.at[g, k])
    total = r.gpx[rows(D + w * 64, 64), :].astype(F32)
    for k in range(1, 8):
        total = total + r.gp2[w_from[k]].astype(F32)
    for j in range(8):
        r.gpf[j] = total[8 * j : 8 * j + 8, :].astype(BF16)
    for k in range(1, 8):
        send(r.gpf.at[ctx_peer[k]], r.gp3.at[c], r.s_p3.at[k], {"seq": s, "ctx": ctx_peer[k]})
    r.gp3[c] = r.gpf[c]

    for k in range(1, 8):
        got(r.ge3.at[ctx_from[k]], r.s_e3.at[k])
    for j in range(4):
        t = r.ge3[2 * j].astype(F32) + r.ge3[2 * j + 1].astype(F32)
        r.geo[:, j * FL : (j + 1) * FL] = t[:, :FL]
        r.geo[:, FF + j * FL : FF + (j + 1) * FL] = t[:, FL:]
    for j in range(4):

        @pl.when(jnp.logical_not(diag & (z == j)))
        def _():
            got(r.gc3.at[j], r.s_c6.at[j])
            got(r.go3.at[j], r.s_o6.at[j])

    for last, out in ((r.gc3, r.gco), (r.go3, r.goo)):
        out[...] = (last[0].astype(F32) + last[1].astype(F32)) + (
            last[2].astype(F32) + last[3].astype(F32)
        )

    total = r.gh[...]
    g = r.ps[y].astype(F32)
    for k in range(1, 4):
        got(r.r1.at[y_from[k]], r.s_r4.at[y_from[k]])
        g = g + r.r1[y_from[k]].astype(F32)
    v = r.xs[my4, :].astype(F32)
    inv = lax.rsqrt(jnp.mean(v * v, axis=1, keepdims=True) + EPS)
    unit = v * inv
    g = g * gain_a
    r.gt[...] = total + inv * (g - unit * jnp.mean(g * unit, axis=1, keepdims=True))

    for k in range(1, 8):
        got(r.gp3.at[ctx_from[k]], r.s_p3.at[k])
    for j in range(4):
        t = r.gp3[2 * j].astype(F32) + r.gp3[2 * j + 1].astype(F32)
        for place, (start, size) in PLACES:
            n = 0 if start < 512 else 1 if start < 768 else 2
            to = PCOLS[n][0] + j * PCOLS[n][1] + start - PCOLS[n][2]
            r.gpo[:, to : to + size] = t[:, place : place + size]
    total = r.ggt2[...]
    for k in range(1, 8):
        got(r.gg3.at[ctx_from[k]], r.s_a3.at[k])
        total = total + r.gg3[ctx_from[k]]
    r.ggo[...] = total

    finish(list(sends))


def hand_over(ggo, lo, gt, gpo, goo, geo, gco, *refs):
    outs, (ag, fg, hg), kept, sem = refs[:6], refs[6:9], refs[9:15], refs[15]
    ins = (lo, gt, gpo, goo, geo, gco)
    loads = [pltpu.make_async_copy(ins[n], kept[n], sem.at[n]) for n in range(6)]
    stores = [pltpu.make_async_copy(kept[n], outs[n], sem.at[6 + n]) for n in range(6)]
    for cp in loads:
        cp.start()
    for load, store in zip(loads, stores, strict=True):
        load.wait()
        store.start()
    place = 8 * lax.axis_index("seq") + lax.axis_index("ctx")
    row = lax.broadcasted_iota(jnp.int32, (8, 128), 0)
    lane = lax.broadcasted_iota(jnp.int32, (8, 128), 1)
    for n, (ref, size) in enumerate(((ag, 8), (fg, 8), (hg, 2))):
        tile = ggo[8 * n : 8 * n + 8, :]
        got = jnp.zeros((1, size), F32)
        at = lax.broadcasted_iota(jnp.int32, (1, size), 1)
        for j in range(size):
            value = jnp.where(row * 128 + lane == place * size + j, tile, 0.0)
            value = jnp.sum(jnp.sum(value, axis=1, keepdims=True), axis=0, keepdims=True)
            got = jnp.where(at == j, value, got)
        ref[...] = got
    for cp in stores:
        cp.wait()


def per_device(x, dy, segments, positions, ag, proj, hg, out, fg, expn, con):
    del positions
    vmem = pl.BlockSpec(memory_space=pltpu.VMEM)
    hbm = pl.BlockSpec(memory_space=pl.ANY)
    scratch = [pltpu.VMEM(shape, kind) for shape, kind in SCRATCH.values()]
    sems = [pltpu.SemaphoreType.DMA(n if isinstance(n, tuple) else (n,)) for n in RECV.values()]
    res = pl.pallas_call(
        kernel,
        name="layer",
        out_shape=(
            jax.ShapeDtypeStruct((TOK, D), BF16),
            jax.ShapeDtypeStruct((TOK, D), F32),
            jax.ShapeDtypeStruct((8, 4096), F32),
            jax.ShapeDtypeStruct((16, D), F32),
            jax.ShapeDtypeStruct((8, 6144), F32),
            jax.ShapeDtypeStruct((24, D), F32),
            jax.ShapeDtypeStruct((24, 128), F32),
        ),
        in_specs=[hbm] * 6 + [vmem] * 4,
        out_specs=(vmem,) * 7,
        scratch_shapes=scratch
        + sems
        + [pltpu.SemaphoreType.DMA((N_SEND,)), pltpu.SemaphoreType.DMA((16,))],
        compiler_params=pltpu.CompilerParams(
            collective_id=0, has_side_effects=True, vmem_limit_bytes=63 * 2**20
        ),
    )(
        x.reshape(TOK, D), dy.reshape(TOK, D), proj, out, expn, con,
        ag.reshape(1, 8), fg.reshape(1, 8), hg.reshape(1, 2), segments,
    )
    big, gains = res[:6], res[6]
    lo, gt, gpo, goo, geo, gco, gag, gfg, ghg = pl.pallas_call(
        hand_over,
        name="hand_over",
        out_shape=tuple(jax.ShapeDtypeStruct(a.shape, a.dtype) for a in big)
        + tuple(jax.ShapeDtypeStruct((1, n), F32) for n in (8, 8, 2)),
        in_specs=[vmem] + [pl.BlockSpec(memory_space=pltpu.HBM)] * 6,
        out_specs=(pl.BlockSpec(memory_space=pltpu.HBM),) * 6 + (vmem,) * 3,
        scratch_shapes=[pltpu.VMEM(a.shape, a.dtype) for a in big]
        + [pltpu.SemaphoreType.DMA((12,))],
        compiler_params=pltpu.CompilerParams(vmem_limit_bytes=63 * 2**20),
    )(gains, *big)
    return (
        lo.reshape(1, TOK, D),
        gt.reshape(1, TOK, D),
        gag.reshape(8),
        gpo,
        ghg.reshape(2),
        goo,
        gfg.reshape(8),
        geo,
        gco,
    )


def solution(mesh):
    return jax.shard_map(
        per_device,
        mesh=mesh,
        in_specs=(
            P("seq", "ctx", None),
            P("seq", "ctx", None),
            P("seq", None),
            P("seq", "ctx"),
            P(("seq", "ctx")),
            P(("seq", "ctx"), None),
            P(("seq", "ctx")),
            P(("seq", "ctx"), None),
            P(("seq", "ctx")),
            P(("seq", "ctx"), None),
            P(("seq", "ctx"), None),
        ),
        out_specs=(
            P("seq", "ctx", None),
            P("seq", "ctx", None),
            P(("seq", "ctx")),
            P(("seq", "ctx"), None),
            P(("seq", "ctx")),
            P(("seq", "ctx"), None),
            P(("seq", "ctx")),
            P(("seq", "ctx"), None),
            P(("seq", "ctx"), None),
        ),
        check_vma=False,
    )
```

```python
import math

import jax
import jax.numpy as jnp
from jax import lax
from jax.experimental import pallas as pl
from jax.experimental.pallas import tpu as pltpu
from jax.sharding import PartitionSpec as P

F32 = jnp.float32
BF16 = jnp.bfloat16
MESH = pl.DeviceIdType.MESH
EPS = 1e-06
THETA = 1000000.0
NEGATIVE = -1e30
D = 1024
HEAD = 128
FF = 3072
FL = 768
TOK = 128
SEQ = 1024
QB = 256
SCALE = HEAD**-0.5


def dot(a, b, da=1, db=0):
    return lax.dot_general(a, b, (((da,), (db,)), ((), ())), preferred_element_type=F32)


def rows(start, size):
    return pl.ds(pl.multiple_of(start, size), size)


SCRATCH = dict(
    pa=((8, 8, D), BF16),
    pw=((8, 2, 64, D), BF16),
    ea=((8, 8, 1536), BF16),
    ew=((4, 2, 2, 64, 1536), BF16),
    ow=((2, 2, 4, 2, 16, D), BF16),
    cb=((2, 2, 4, 2, 24, D), BF16),
    cw=((FL, D), BF16),
    gi=((24, 128), F32),
    ga=((8, 24, 128), F32),
    gb=((8, 24, 128), F32),
    gsum=((24, 128), F32),
    gacc=((24, 128), F32),
    gfr=((24, 128), F32),
    gall=((24, 128), F32),
    cos=((512, HEAD), F32),
    sin=((512, HEAD), F32),
    segc=((QB, 128), jnp.int32),
    xs=((512, D), BF16),
    ns=((512, D), BF16),
    pj=((512, 768), F32),
    qs=((2, 4, QB, HEAD), BF16),
    kv=((8, 4, TOK, HEAD), BF16),
    mx=((512, 512), BF16),
    ps=((4, TOK, D), BF16),
    r1=((4, TOK, D), BF16),
    hid=((TOK, D), F32),
    nm=((512, D), BF16),
    dy=((512, D), BF16),
    act=((512, FL), BF16),
    ggu=((512, 1536), BF16),
    gs=((4, TOK, D), BF16),
    r2=((4, TOK, D), BF16),
    los=((4, TOK, D), BF16),
    r3=((4, TOK, D), BF16),
    gh=((TOK, D), F32),
    g4=((512, D), BF16),
    gm=((2, 4, QB, HEAD), BF16),
    f4=((4096, HEAD), F32),
    dq=((2, 4, QB, HEAD), F32),
    ds=((2, 4, 2, TOK, HEAD), BF16),
    dr=((2, 4, 2, TOK, HEAD), BF16),
    gp=((512, D), BF16),
    attg=((1, D), F32),
    hgq=((1, HEAD), F32),
    hgk=((1, HEAD), F32),
    gg0=((24, 128), F32),
    gg1=((24, 128), F32),
    ggt=((24, 128), F32),
    ggt2=((24, 128), F32),
    gg2=((8, 24, 128), F32),
    gg3=((8, 24, 128), F32),
    ge=((2, 8, 64, 1536), BF16),
    ge1=((8, 64, 1536), BF16),
    ges=((8, 64, 1536), BF16),
    ge2=((4, 2, 64, 1536), BF16),
    get=((2, 64, 1536), BF16),
    gex=((64, 1536), BF16),
    gef=((8, 8, 1536), BF16),
    ge3=((8, 8, 1536), BF16),
    gc=((2, 2, 8, 24, D), BF16),
    gc1=((2, 8, 24, D), BF16),
    gcs=((2, 2, 4, 24, D), BF16),
    gc2=((4, 4, 24, D), BF16),
    gcf=((4, 24, D), BF16),
    gc3=((4, 24, D), BF16),
    go=((2, 2, 8, 16, D), BF16),
    go1=((2, 8, 16, D), BF16),
    gos=((2, 2, 4, 16, D), BF16),
    go2=((4, 4, 16, D), BF16),
    gof=((4, 16, D), BF16),
    go3=((4, 16, D), BF16),
    gpx=((1536, D), BF16),
    gp1=((512, D), BF16),
    gp2=((8, 64, D), BF16),
    gpf=((8, 8, D), BF16),
    gp3=((8, 8, D), BF16),
)
RECV = dict(
    pa=(8, 2), ea=8, ga=8, gb=8, gfr=1, x=4, dy=4, pb=(2, 8), eb=(2, 4), ps=2, es=2,
    o1=4, o2=4, o3=2, c1=4, c2=4, c3=2, kv=4, r1=4, nm=4, r2=4, r3=4, g4=4, dr=(2, 4), r4=4,
    e1=1, e2=4, ex=1, e3=8, c4=2, c5=4, c6=4, o4=2, o5=4, o6=4, p1=2, p2=(2, 8), p3=8, a1=1, a2=8, a3=8,
)
N_SEND = 88
NAMES = (
    ["x", "dyi", "pi", "oi", "ei", "ci", "agi", "fgi", "hgi", "segr"]
    + ["lo", "gt", "gpo", "goo", "geo", "gco", "ggo"]
    + list(SCRATCH)
    + ["s_" + n for n in RECV]
    + ["send", "loc"]
)
PLACES = (
    (0, (0, 256)), (256, (512, 128)), (384, (768, 128)),
    (512, (256, 256)), (768, (640, 128)), (896, (896, 128)),
)
HEADS = (0, 128, 256, 384, 512, 768)
PCOLS = ((0, 512, 0), (2048, 256, 512), (3072, 256, 768))


class Box:
    pass


def kernel(*refs):
    r = Box()
    for name, ref in zip(NAMES, refs, strict=True):
        setattr(r, name, ref)
    s, c = lax.axis_index("seq"), lax.axis_index("ctx")
    z, xh, core = s // 4, (s // 2) % 2, s % 2
    y, xl = c // 2, c % 2
    w = s // 2
    sib = 1 - core

    def at(zz, xx, cc, ctx):
        return {"seq": zz * 4 + xx * 2 + cc, "ctx": ctx}

    def on_w(ww, cc, ctx):
        return {"seq": ww * 2 + cc, "ctx": ctx}

    me_sib = on_w(w, sib, c)
    ctx_peer = [None] + [lax.rem(c + k, 8) for k in range(1, 8)]
    ctx_from = [None] + [lax.rem(c + 8 - k, 8) for k in range(1, 8)]
    w_peer = [None] + [lax.rem(w + k, 8) for k in range(1, 8)]
    w_from = [None] + [lax.rem(w + 8 - k, 8) for k in range(1, 8)]
    y_peer = [None] + [lax.rem(y + k, 4) for k in range(1, 4)]
    y_from = [None] + [lax.rem(y + 4 - k, 4) for k in range(1, 4)]
    z_peer = [None] + [lax.rem(z + k, 4) for k in range(1, 4)]
    z_from = [None] + [lax.rem(z + 4 - k, 4) for k in range(1, 4)]
    x_line = [(xh, 1 - xl), (1 - xh, xl), (1 - xh, 1 - xl)]
    diag = y == z

    def e_block(zz, xx, cc):
        return r.ew.at[zz, xx, cc]

    def all_p(start, stop):
        return r.pw[:, :, :, start:stop].reshape(D, stop - start)

    def all_e():
        return r.ew[...].reshape(D, 1536)

    def all_o():
        return r.ow[...].reshape(512, D)

    free, sends = list(range(N_SEND - 1)), []

    def send(src, dst, sem, dev, unless=None):
        at = free.pop(0)
        cp = pltpu.make_async_remote_copy(
            src_ref=src, dst_ref=dst, send_sem=r.send.at[at], recv_sem=sem,
            device_id=dev, device_id_type=MESH,
        )
        sends.append((cp, unless, at))
        if unless is None:
            cp.start()
        else:
            pl.when(jnp.logical_not(unless))(cp.start)

    def finish(some):
        for entry in some:
            cp, unless, at = entry
            if unless is None:
                cp.wait_send()
            else:
                pl.when(jnp.logical_not(unless))(cp.wait_send)
            free.append(at)
        sends[:] = [e for e in sends if not any(e is f for f in some)]

    def got(dst, sem):
        pltpu.make_async_remote_copy(
            src_ref=dst, dst_ref=dst, send_sem=r.send.at[N_SEND - 1], recv_sem=sem,
            device_id=me_sib, device_id_type=MESH,
        ).wait_recv()

    bar = pltpu.get_barrier_semaphore()

    def greet(dev):
        pl.semaphore_signal(bar, inc=1, device_id=dev, device_id_type=MESH)

    greet(me_sib)
    for k in range(1, 8):
        greet({"seq": s, "ctx": ctx_peer[k]})
        greet(on_w(w_peer[k], core, c))
    greet(at(z, x_line[2][0], core, 2 * y + x_line[2][1]))
    for zz in range(4):

        @pl.when(jnp.logical_not(diag & (z == zz)))
        def _():
            greet(at(zz, xh, core, 2 * z + xl))
            greet(at(y, xh, core, 2 * zz + xl))

    own = []

    def own_copy(src, dst):
        cp = pltpu.make_async_copy(src, dst, r.loc.at[len(own)])
        own.append(cp)
        cp.start()

    my4 = rows(y * TOK, TOK)
    own_copy(r.x, r.xs.at[my4])
    own_copy(r.dyi, r.dy.at[my4])
    for start, size, place in PCOLS:
        own_copy(
            r.pi.at[:, pl.ds(pl.multiple_of(start + y * size, size), size)],
            r.pa.at[c, :, pl.ds(place, size)],
        )
    for part in range(2):
        own_copy(
            r.ei.at[:, pl.ds(pl.multiple_of(part * FF + y * FL, FL), FL)],
            r.ea.at[c, :, pl.ds(part * FL, FL)],
        )

    tile_row = lax.broadcasted_iota(jnp.int32, (8, 128), 0)
    tile_lane = lax.broadcasted_iota(jnp.int32, (8, 128), 1)
    flat = tile_row * 128 + tile_lane
    place = 8 * s + c
    for n, (ref, size) in enumerate(((r.agi, 8), (r.fgi, 8), (r.hgi, 2))):
        values = ref[...].astype(F32)
        tile = jnp.zeros((8, 128), F32)
        for j in range(size):
            tile = jnp.where(flat == place * size + j, values[:, j : j + 1], tile)
        r.gi[8 * n : 8 * n + 8, :] = tile

    pl.semaphore_wait(bar, 24 - jnp.where(diag, 2, 0))

    for k in range(1, 8):
        send(r.gi, r.ga.at[c], r.s_ga.at[k], {"seq": s, "ctx": ctx_peer[k]})
    for part in (1, 2, 0):
        start, size, place = PCOLS[part]
        for k in range(1, 8):
            to = ctx_peer[k]
            send(
                r.pi.at[:, pl.ds(pl.multiple_of(start + (to // 2) * size, size), size)],
                r.pa.at[c, :, pl.ds(place, size)],
                r.s_pa.at[k, min(part, 1)],
                {"seq": s, "ctx": to},
            )
    for k in (1, 3):
        send(r.x, r.xs.at[my4], r.s_x.at[k], {"seq": s, "ctx": 2 * y_peer[k] + xl})

    @pl.when(diag)
    def _():
        a = pltpu.make_async_copy(
            r.oi,
            r.ow.at[xh, core, y, xl],
            r.loc.at[14],
        )
        b = pltpu.make_async_copy(r.ci, r.cb.at[xh, core, y, xl], r.loc.at[15])
        a.start()
        b.start()
        a.wait()
        b.wait()

    for cp in own:
        cp.wait()

    lane = lax.broadcasted_iota(jnp.int32, (1, HEAD), 1)
    index = jnp.where(lane < HEAD // 2, lane, lane - HEAD // 2).astype(F32)
    inverse = jnp.exp(index * (-2.0 / HEAD * math.log(THETA)))
    sign = jnp.where(lane < HEAD // 2, -1.0, 1.0)
    eye = lax.broadcasted_iota(jnp.int32, (TOK, TOK), 0) == lax.broadcasted_iota(
        jnp.int32, (TOK, TOK), 1
    )
    for j in range(4):
        b = pl.ds(j * TOK, TOK)
        seg = r.segr[:, pl.ds(pl.multiple_of((2 * j + xl) * TOK, TOK), TOK)]
        seg = jnp.sum(jnp.where(eye, seg.astype(F32), 0.0), axis=1, keepdims=True)
        r.segc[:, j : j + 1] = jnp.concatenate([seg, seg], 0).astype(jnp.int32)
        before = jnp.sum((r.segr[...].astype(F32) < seg).astype(F32), axis=1, keepdims=True)
        t = lax.broadcasted_iota(jnp.int32, (TOK, 1), 0) + (2 * j + xl) * TOK
        phase = (t.astype(F32) - before) * inverse
        r.cos[b, :] = jnp.cos(phase)
        r.sin[b, :] = jnp.sin(phase) * sign

    kv_half, q_half = pl.ds(512, 512), pl.ds(0, 512)

    def spread(n, half):
        blk = r.pw.at[w, core, :, half]
        for k in range(1, 8):
            send(blk, blk, r.s_pb.at[n, k], on_w(w_peer[k], core, c))

    def pass_on(n, half):
        for k in range(1, 8):
            got(r.pw.at[w_from[k], core, :, half], r.s_pb.at[n, k])
        blk = r.pw.at[:, core, :, half]
        send(blk, blk, r.s_ps.at[n], me_sib)

    def from_sibling(n, half):
        got(r.pw.at[:, sib, :, half], r.s_ps.at[n])

    def joined(start, size):
        return jnp.concatenate(
            [r.pa[j, :, start : start + size].astype(F32) for j in range(8)], 0
        ).astype(BF16)

    total = r.gi[...]
    for k in range(1, 8):
        got(r.ga.at[ctx_from[k]], r.s_ga.at[k])
        total = total + r.ga[ctx_from[k]]
    r.gsum[...] = total
    for k in range(1, 8):
        send(r.gsum, r.gb.at[w], r.s_gb.at[k], on_w(w_peer[k], core, c))
    for k in range(1, 8):
        got(r.pa.at[ctx_from[k], :, kv_half], r.s_pa.at[k, 1])
    for g in range(2):
        r.pw[w, core, :, 512 + g * 256 : 640 + g * 256] = joined(512 + g * 128, 128)
        r.pw[w, core, :, 640 + g * 256 : 768 + g * 256] = joined(768 + g * 128, 128)
    first_sends = list(sends)
    spread(0, kv_half)
    send(r.x, r.xs.at[my4], r.s_x.at[2], {"seq": s, "ctx": 2 * y_peer[2] + xl})
    for k in range(1, 8):
        to = ctx_peer[k]
        for part in range(2):
            send(
                r.ei.at[:, pl.ds(pl.multiple_of(part * FF + (to // 2) * FL, FL), FL)],
                r.ea.at[c, :, pl.ds(part * FL, FL)],
                r.s_ea.at[k],
                {"seq": s, "ctx": to},
            )
    for k in range(1, 8):
        got(r.pa.at[ctx_from[k], :, q_half], r.s_pa.at[k, 0])
    r.pw[w, core, :, 0:512] = joined(0, 512)
    total = r.gsum[...]
    for k in range(1, 8):
        got(r.gb.at[w_from[k]], r.s_gb.at[k])
        total = total + r.gb[w_from[k]]
    r.gacc[...] = total
    send(r.gacc, r.gfr, r.s_gfr.at[0], me_sib)
    for zz in range(4):
        send(
            r.oi,
            r.ow.at[xh, core, y, xl],
            r.s_o1.at[y],
            at(zz, xh, core, 2 * z + xl),
            unless=diag & (z == zz),
        )
    pass_on(0, kv_half)
    spread(1, q_half)
    got(r.gfr, r.s_gfr.at[0])
    r.gall[...] = r.gacc[...] + r.gfr[...]
    from_sibling(0, kv_half)

    def wide(first):
        return jnp.concatenate([r.gall[first + j : first + j + 1, :] for j in range(8)], 1)

    gain_a, gain_f = wide(0), wide(8)
    gain_q, gain_k = r.gall[16:17, :], r.gall[17:18, :]

    def turn(v):
        return pltpu.roll(v, HEAD // 2, 1)

    x_partner = {"seq": s, "ctx": 2 * y + 1 - xl}
    def headed(u, b, h):
        r.pj[b, h * HEAD : (h + 1) * HEAD] = u
        ui = lax.rsqrt(jnp.mean(u * u, axis=1, keepdims=True) + EPS)
        u = u * ui * (gain_q if h < 4 else gain_k)
        return (u * r.cos[b, :] + turn(u) * r.sin[b, :]).astype(BF16)

    for k in (0, 1, 3, 2):
        j = y if k == 0 else y_from[k]
        b = rows(j * TOK, TOK)
        if k:
            got(r.xs.at[b], r.s_x.at[k])
        v = r.xs[b, :].astype(F32)
        inv = lax.rsqrt(jnp.mean(v * v, axis=1, keepdims=True) + EPS)
        n = (v * inv * gain_a).astype(BF16)
        r.ns[b, :] = n
        out = dot(n, all_p(512, D))
        mine = 2 * j + xl
        for g in range(2):
            r.kv[mine, g] = headed(out[:, g * 256 : g * 256 + HEAD], b, 4 + g)
            r.kv[mine, 2 + g] = out[:, g * 256 + HEAD : g * 256 + 256].astype(BF16)
        send(r.kv.at[mine], r.kv.at[mine], r.s_kv.at[j], x_partner)

    for k in (1, 3, 2):
        send(r.dyi, r.dy.at[my4], r.s_dy.at[k], {"seq": s, "ctx": 2 * y_peer[k] + xl})

    for k in range(1, 8):
        got(r.ea.at[ctx_from[k]], r.s_ea.at[k])
    r.ew[z, xh, core] = jnp.concatenate([r.ea[j].astype(F32) for j in range(8)], 0).astype(BF16)
    own_e = r.ew.at[z, xh, core]
    for k in (1, 3, 2):
        send(own_e, own_e, r.s_eb.at[0, k], at(z_peer[k], xh, core, c))
    for zz in range(4):
        send(
            r.ci,
            r.cb.at[xh, core, y, xl],
            r.s_c1.at[y],
            at(zz, xh, core, 2 * z + xl),
            unless=diag & (z == zz),
        )

    pass_on(1, q_half)
    from_sibling(1, q_half)
    for j in range(4):
        b = pl.ds(j * TOK, TOK)
        out = dot(r.ns[b, :], all_p(0, 512))
        for h in range(4):
            u = headed(out[:, h * HEAD : (h + 1) * HEAD], b, h)
            r.qs[h // 2, j, pl.ds((h % 2) * TOK, TOK), :] = u
    finish(first_sends)

    for j in range(4):

        @pl.when(jnp.logical_not(diag & (y == j)))
        def _():
            got(r.ow.at[xh, core, j, xl], r.s_o1.at[j])

    blk = r.ow.at[xh, core, :, xl]
    for n, (xx, ll) in enumerate(x_line):
        send(blk, blk, r.s_o2.at[n], at(z, xx, core, 2 * y + ll))
    send(own_e, own_e, r.s_eb.at[0, 0], at(z, 1 - xh, core, c))


    def mask(j):
        n = (2 * j + 2) * TOK
        row = lax.broadcasted_iota(jnp.int32, (QB, n), 0)
        t = (2 * j + xl) * TOK + jnp.where(row < TOK, row, row - TOK)
        u = lax.broadcasted_iota(jnp.int32, (QB, n), 1)
        return (u <= t) & (r.segr[:, :n] == r.segc[:, j : j + 1])

    def at_p(g, j):
        n = (2 * j + 2) * TOK
        if j == 1:
            return r.gpx.at[D : D + QB, g * n : (g + 1) * n]
        first = g * QB + (0 if j == 3 else 2 * QB)
        return r.gpx.at[first : first + QB, 0:n] if j else r.gpx.at[first : first + QB, D - n : D]

    def keys(h, j):
        n = 2 * j + 2
        return r.kv[:n, h].reshape(n * TOK, HEAD)

    for j in range(4):
        got(r.kv.at[2 * j + 1 - xl], r.s_kv.at[j])
        ok = mask(j)
        b = pl.ds(j * TOK, TOK)
        for g in range(2):
            sc = dot(r.qs[g, j], keys(g, j), 1, 1) * SCALE
            sc = jnp.where(ok, sc, NEGATIVE)
            top = jnp.max(sc, axis=1, keepdims=True)
            e = jnp.exp(sc - top)
            tot = jnp.sum(e, axis=1, keepdims=True)
            p = (e * (1.0 / tot)).astype(BF16)
            at_p(g, j)[...] = p
            o = dot(p, keys(2 + g, j)).astype(BF16)
            r.mx[b, (2 * g) * HEAD : (2 * g + 1) * HEAD] = o[:TOK, :]
            r.mx[b, (2 * g + 1) * HEAD : (2 * g + 2) * HEAD] = o[TOK:, :]
        if j == 2:
            for n, (xx, ll) in enumerate(x_line):
                got(r.ow.at[xx, core, :, ll], r.s_o2.at[n])
            for n in range(2):
                send(r.ow.at[n, core], r.ow.at[n, core], r.s_o3.at[n], me_sib)
    for n in range(2):
        got(r.ow.at[n, sib], r.s_o3.at[n])
    for k in (2, 1, 3, 0):
        j = y_peer[k] if k else y
        r.ps[j] = dot(r.mx[rows(j * TOK, TOK), :], all_o()).astype(BF16)
        if k:
            send(r.ps.at[j], r.r1.at[y], r.s_r1.at[y], {"seq": s, "ctx": 2 * j + xl})

    blk = e_block(z, 1 - xh, core)
    got(blk, r.s_eb.at[0, 0])
    for k in (1, 3, 2):
        send(blk, blk, r.s_eb.at[1, k], at(z_peer[k], xh, core, c))
    for k in (1, 3, 2):
        got(e_block(z_from[k], xh, core), r.s_eb.at[0, k])
    blk = r.ew.at[:, xh, core]
    send(blk, blk, r.s_es.at[0], me_sib)
    for j in range(4):

        @pl.when(jnp.logical_not(diag & (y == j)))
        def _():
            got(r.cb.at[xh, core, j, xl], r.s_c1.at[j])

    blk = r.cb.at[xh, core, :, xl]
    for n, (xx, ll) in enumerate(x_line):
        send(blk, blk, r.s_c2.at[n], at(z, xx, core, 2 * y + ll))

    hidden = r.xs[my4, :].astype(F32) + r.ps[y].astype(F32)
    for k in range(1, 4):
        got(r.r1.at[y_from[k]], r.s_r1.at[y_from[k]])
        hidden = hidden + r.r1[y_from[k]].astype(F32)
    r.hid[...] = hidden
    inv_h = lax.rsqrt(jnp.mean(hidden * hidden, axis=1, keepdims=True) + EPS)
    r.nm[my4, :] = (hidden * inv_h * gain_f).astype(BF16)
    def send_nm(k):
        send(
            r.nm.at[my4], r.nm.at[my4], r.s_nm.at[k], {"seq": s, "ctx": 2 * y_peer[k] + xl}
        )

    older = list(sends)
    send_nm(1)
    send_nm(3)
    for k in (1, 3, 2):
        got(e_block(z_from[k], 1 - xh, core), r.s_eb.at[1, k])
    blk = r.ew.at[:, 1 - xh, core]
    send(blk, blk, r.s_es.at[1], me_sib)

    for n, (xx, ll) in enumerate(x_line):
        got(r.cb.at[xx, core, :, ll], r.s_c2.at[n])
    for n in range(2):
        send(r.cb.at[n, core], r.cb.at[n, core], r.s_c3.at[n], me_sib)
    for k in range(1, 4):
        got(r.dy.at[rows(y_from[k] * TOK, TOK)], r.s_dy.at[k])
    finish(older)
    for n in range(2):
        got(r.cb.at[n, sib], r.s_c3.at[n])
    got(r.ew.at[:, xh, sib], r.s_es.at[0])
    got(r.ew.at[:, 1 - xh, sib], r.s_es.at[1])
    for j in range(16):
        r.cw[48 * j : 48 * j + 48, :] = jnp.concatenate(
            [r.cb[j // 8, j // 4 % 2, j % 4, n].astype(F32) for n in range(2)], 0
        ).astype(BF16)

    def grad_act(k, _):
        b = rows(k * TOK, TOK)
        g = dot(r.dy[b, :], r.cw[...], 1, 1)
        for h in range(6):
            r.f4[rows(h * 512 + k * TOK, TOK), :] = g[:, h * HEAD : (h + 1) * HEAD]
        return 0

    lax.fori_loop(0, 4, grad_act, 0)

    for k in (0, 1, 3, 2):
        b4 = y if k == 0 else y_from[k]
        b = rows(b4 * TOK, TOK)
        if k:
            got(r.nm.at[b], r.s_nm.at[k])
        gu = dot(r.nm[b, :], all_e())
        gate, up = gu[:, :FL], gu[:, FL:]
        sg = 1.0 / (1.0 + jnp.exp(-gate))
        sl = gate * sg
        r.act[b, :] = (sl * up).astype(BF16)
        gt = jnp.concatenate([r.f4[rows(h * 512 + b4 * TOK, TOK), :] for h in range(6)], 1)
        r.ggu[b, :FL] = (gt * up * sg * (1.0 + gate * (1.0 - sg))).astype(BF16)
        r.ggu[b, FL:] = (gt * sl).astype(BF16)
        r.gs[b4] = dot(r.ggu[b, :], all_e(), 1, 1).astype(BF16)
        if k == 0:
            send_nm(2)
        if k:
            send(r.gs.at[b4], r.r2.at[y], r.s_r2.at[k], {"seq": s, "ctx": 2 * b4 + xl})
    for k in (0, 1, 3, 2):
        b4 = y if k == 0 else y_from[k]
        r.los[b4] = dot(r.act[rows(b4 * TOK, TOK), :], r.cw[...]).astype(BF16)

    for j in range(4):
        g = dot(r.nm[:, j * 256 : (j + 1) * 256], r.ggu[...], 0, 0).astype(BF16)
        for q in range(4):
            r.ge[q % 2, 2 * j + q // 2] = g[64 * q : 64 * q + 64, :]
    send(r.ge.at[sib], r.ge1, r.s_e1.at[0], me_sib)
    for j in range(2):
        g = dot(r.act[:, j * 384 : (j + 1) * 384], r.dy[...], 0, 0)
        for q in range(16):
            r.gc[q // 8, j, q % 8] = g[24 * q : 24 * q + 24, :].astype(BF16)
    for j in range(2):
        send(r.gc.at[sib, j], r.gc1.at[j], r.s_c4.at[j], me_sib)

    g_mlp = r.gs[y].astype(F32)
    for k in range(1, 4):
        got(r.r2.at[y_peer[k]], r.s_r2.at[k])
        g_mlp = g_mlp + r.r2[y_peer[k]].astype(F32)
    hidden = r.hid[...]
    inv_h = lax.rsqrt(jnp.mean(hidden * hidden, axis=1, keepdims=True) + EPS)
    unit = hidden * inv_h
    feed = jnp.sum(g_mlp * unit, axis=0, keepdims=True)
    g = g_mlp * gain_f
    g = r.dy[my4, :].astype(F32) + inv_h * (g - unit * jnp.mean(g * unit, axis=1, keepdims=True))
    r.gh[...] = g
    r.g4[my4, :] = g.astype(BF16)
    def send_g4(k):
        send(
            r.g4.at[my4], r.g4.at[my4], r.s_g4.at[k], {"seq": s, "ctx": 2 * y_peer[k] + xl}
        )

    send_g4(1)
    send_g4(3)
    r.gg0[...] = jnp.zeros((24, 128), F32)
    for j in range(8):
        r.gg0[8 + j : 9 + j, :] = feed[:, 128 * j : 128 * j + 128]

    got(r.ge1, r.s_e1.at[0])

    def pair_e(j, _):
        r.ges[j] = (r.ge[core, j].astype(F32) + r.ge1[j].astype(F32)).astype(BF16)
        return 0

    lax.fori_loop(0, 8, pair_e, 0)
    for k in (1, 3, 2):
        send(
            r.ges.at[pl.ds(pl.multiple_of(2 * z_peer[k], 2), 2)], r.ge2.at[z], r.s_e2.at[k],
            at(z_peer[k], xh, core, c),
        )
    for j in range(2):
        got(r.gc1.at[j], r.s_c4.at[j])
        for q in range(8):
            r.gcs[j, q % 2, q // 2] = (
                r.gc[core, j, q].astype(F32) + r.gc1[j, q].astype(F32)
            ).astype(BF16)
    for n, (xx, ll) in enumerate(x_line):
        send(
            r.gcs.at[xx, ll], r.gc2.at[xh * 2 + xl], r.s_c5.at[n],
            at(z, xx, core, 2 * y + ll),
        )

    send_g4(2)

    for k in (0, 1, 3, 2):
        j = y if k == 0 else y_from[k]
        b = rows(j * TOK, TOK)
        if k:
            got(r.g4.at[b], r.s_g4.at[k])
        gm = dot(r.g4[b, :], all_o(), 1, 1).astype(BF16)
        for h in range(4):
            r.gm[h // 2, j, pl.ds((h % 2) * TOK, TOK), :] = gm[:, h * HEAD : (h + 1) * HEAD]

    older = list(sends)
    for k in (1, 3, 2):
        b4 = y_from[k]
        send(r.los.at[b4], r.r3.at[y], r.s_r3.at[k], {"seq": s, "ctx": 2 * b4 + xl})

    for j in range(2):
        g = dot(r.mx[:, j * 256 : (j + 1) * 256], r.g4[...], 0, 0).astype(BF16)
        for q in range(16):
            r.go[q // 8, j, q % 8] = g[16 * q : 16 * q + 16, :]
    for j in range(2):
        send(r.go.at[sib, j], r.go1.at[j], r.s_o4.at[j], me_sib)

    for g in range(2):
        for j in (3, 2, 1, 0):
            n = (2 * j + 2) * TOK
            q, kk, gmh = r.qs[g, j], keys(g, j), r.gm[g, j]
            low = at_p(g, j)[...]
            p = low.astype(F32)
            gat = dot(gmh, keys(2 + g, j), 1, 1)
            ds = (p * (gat - jnp.sum(p * gat, axis=1, keepdims=True))).astype(BF16)
            r.dq[g, j] = dot(ds, kk) * SCALE
            dk = dot(ds, q, 0, 0) * SCALE
            dv = dot(low, gmh, 0, 0)
            kr, vr = g * SEQ, (2 + g) * SEQ
            if j == 3:
                r.f4[kr : kr + n, :] = dk
                r.f4[vr : vr + n, :] = dv
            else:
                r.f4[kr : kr + n, :] += dk
                r.f4[vr : vr + n, :] += dv
            theirs = (2 * j + 1 - xl) * TOK
            r.ds[g, j, 0] = r.f4[rows(kr + theirs, TOK), :].astype(BF16)
            r.ds[g, j, 1] = r.f4[rows(vr + theirs, TOK), :].astype(BF16)
            send(r.ds.at[g, j], r.dr.at[g, j], r.s_dr.at[g, j], x_partner)
            if g or j != 3:
                continue
            for j in range(2):
                got(r.go1.at[j], r.s_o4.at[j])
                for q in range(8):
                    r.gos[j, q % 2, q // 2] = (
                        r.go[core, j, q].astype(F32) + r.go1[j, q].astype(F32)
                    ).astype(BF16)
            for n, (xx, ll) in enumerate(x_line):
                send(
                    r.gos.at[xx, ll], r.go2.at[xh * 2 + xl], r.s_o5.at[n],
                    at(z, xx, core, 2 * y + ll),
                )

    total = r.hid[...] + r.los[y].astype(F32)
    for k in range(1, 4):
        got(r.r3.at[y_peer[k]], r.s_r3.at[k])
        total = total + r.r3[y_peer[k]].astype(F32)
    r.lo[...] = total.astype(BF16)

    r.attg[...] = jnp.zeros((1, D), F32)
    r.hgq[...] = jnp.zeros((1, HEAD), F32)
    r.hgk[...] = jnp.zeros((1, HEAD), F32)

    def norms(g, j):
        b = rows(j * TOK, TOK)
        mine = (2 * j + xl) * TOK
        cosine, sine = r.cos[b, :], r.sin[b, :]
        got(r.dr.at[g, j], r.s_dr.at[g, j])
        for h in (2 * g, 2 * g + 1, 4 + g):
            if h < 4:
                wv = r.dq[g, j, (h % 2) * TOK : (h % 2 + 1) * TOK, :]
            else:
                wv = r.f4[rows(g * SEQ + mine, TOK), :] + r.dr[g, j, 0].astype(F32)
            gn = wv * cosine - turn(wv) * sine
            v = r.pj[b, h * HEAD : (h + 1) * HEAD]
            inv = lax.rsqrt(jnp.mean(v * v, axis=1, keepdims=True) + EPS)
            unit = v * inv
            acc = r.hgq if h < 4 else r.hgk
            acc[...] += jnp.sum(gn * unit, axis=0, keepdims=True)
            t = gn * (gain_q if h < 4 else gain_k)
            gx = inv * (t - unit * jnp.mean(t * unit, axis=1, keepdims=True))
            r.gp[b, HEADS[h] : HEADS[h] + HEAD] = gx.astype(BF16)
        r.gp[b, 640 + g * 256 : 768 + g * 256] = (
            r.f4[rows((2 + g) * SEQ + mine, TOK), :] + r.dr[g, j, 1].astype(F32)
        ).astype(BF16)

    def grad_projection(g):
        half = pl.ds(g * 512, 512)
        for j in range(4):
            left = r.ns[:, j * 256 : (j + 1) * 256]
            for n in range(2):
                t = dot(left, r.gp[:, n * 512 + g * 256 : n * 512 + (g + 1) * 256], 0, 0)
                t = t.astype(BF16)
                at_lane = g * 512 + n * 256
                for q in range(4):
                    first = (q % 2) * 512 + (2 * j + q // 2) * 64
                    r.gpx[first : first + 64, at_lane : at_lane + 256] = t[64 * q : 64 * q + 64, :]
        send(r.gpx.at[rows(sib * 512, 512), half], r.gp1.at[:, half], r.s_p1.at[g], me_sib)

    def pair_projection(g):
        half = pl.ds(g * 512, 512)
        got(r.gp1.at[:, half], r.s_p1.at[g])
        r.gpx[D:, half] = (
            r.gpx[rows(core * 512, 512), half].astype(F32) + r.gp1[:, half].astype(F32)
        ).astype(BF16)
        for k in range(1, 8):
            send(
                r.gpx.at[rows(D + w_peer[k] * 64, 64), half], r.gp2.at[w, :, half],
                r.s_p2.at[g, k], on_w(w_peer[k], core, c),
            )

    finish(older)
    for j in (3, 2, 1, 0):
        norms(0, j)
    grad_projection(0)

    for k in (1, 3, 2):
        got(r.ge2.at[z_from[k]], r.s_e2.at[k])
    for xx in range(2):
        total = r.ges[2 * z + xx].astype(F32)
        for k in range(1, 4):
            total = total + r.ge2[z_from[k], xx].astype(F32)
        r.get[xx] = total.astype(BF16)
    send(r.get.at[1 - xh], r.gex, r.s_ex.at[0], at(z, 1 - xh, core, c))

    pair_projection(0)

    for j in (3, 2, 1, 0):
        norms(1, j)
    grad_projection(1)
    for k in (2, 1, 3, 0):
        j = y_peer[k] if k else y
        b = rows(j * TOK, TOK)
        part = dot(r.gp[b, :], all_p(0, D), 1, 1)
        r.ps[j] = part.astype(BF16)
        if k:
            send(r.ps.at[j], r.r1.at[y], r.s_r4.at[y], {"seq": s, "ctx": 2 * j + xl})
        v = r.xs[b, :].astype(F32)
        inv = lax.rsqrt(jnp.mean(v * v, axis=1, keepdims=True) + EPS)
        r.attg[...] += jnp.sum(part * (v * inv), axis=0, keepdims=True)

    for j in range(8):
        r.gg0[j : j + 1, :] = r.attg[:, 128 * j : 128 * j + 128]
    r.gg0[16:17, :] = r.hgq[...]
    r.gg0[17:18, :] = r.hgk[...]
    send(r.gg0, r.gg1, r.s_a1.at[0], me_sib)

    got(r.gg1, r.s_a1.at[0])
    r.ggt[...] = r.gg0[...] + r.gg1[...]
    for k in range(1, 8):
        send(r.ggt, r.gg2.at[w], r.s_a2.at[k], on_w(w_peer[k], core, c))

    pair_projection(1)

    got(r.gex, r.s_ex.at[0])
    total = r.get[xh].astype(F32) + r.gex[...].astype(F32)
    for j in range(8):
        r.gef[j] = total[8 * j : 8 * j + 8, :].astype(BF16)
    for k in range(1, 8):
        send(r.gef.at[ctx_peer[k]], r.ge3.at[c], r.s_e3.at[k], {"seq": s, "ctx": ctx_peer[k]})
    r.ge3[c] = r.gef[c]
    for n, (xx, ll) in enumerate(x_line):
        got(r.gc2.at[xx * 2 + ll], r.s_c5.at[n])
    for n, (xx, ll) in enumerate(x_line):
        got(r.go2.at[xx * 2 + ll], r.s_o5.at[n])
    for mine, theirs, out, last, sem in (
        (r.gcs, r.gc2, r.gcf, r.gc3, r.s_c6), (r.gos, r.go2, r.gof, r.go3, r.s_o6),
    ):
        for j in range(4):
            total = mine[xh, xl, j].astype(F32)
            for xx, ll in x_line:
                total = total + theirs[xx * 2 + ll, j].astype(F32)
            out[j] = total.astype(BF16)
            send(
                out.at[j], last.at[z], sem.at[z], at(y, xh, core, 2 * j + xl),
                unless=diag & (y == j),
            )

    @pl.when(diag)
    def _():
        r.gc3[z] = r.gcf[y]
        r.go3[z] = r.gof[y]

    total = r.ggt[...]
    for k in range(1, 8):
        got(r.gg2.at[w_from[k]], r.s_a2.at[k])
        total = total + r.gg2[w_from[k]]
    r.ggt2[...] = total
    for k in range(1, 8):
        send(r.ggt2, r.gg3.at[c], r.s_a3.at[k], {"seq": s, "ctx": ctx_peer[k]})

    for g in range(2):
        for k in range(1, 8):
            got(r.gp2.at[w_from[k], :, pl.ds(g * 512, 512)], r.s_p2.at[g, k])
    total = r.gpx[rows(D + w * 64, 64), :].astype(F32)
    for k in range(1, 8):
        total = total + r.gp2[w_from[k]].astype(F32)
    for j in range(8):
        r.gpf[j] = total[8 * j : 8 * j + 8, :].astype(BF16)
    for k in range(1, 8):
        send(r.gpf.at[ctx_peer[k]], r.gp3.at[c], r.s_p3.at[k], {"seq": s, "ctx": ctx_peer[k]})
    r.gp3[c] = r.gpf[c]

    for k in range(1, 8):
        got(r.ge3.at[ctx_from[k]], r.s_e3.at[k])
    for j in range(4):
        t = r.ge3[2 * j].astype(F32) + r.ge3[2 * j + 1].astype(F32)
        r.geo[:, j * FL : (j + 1) * FL] = t[:, :FL]
        r.geo[:, FF + j * FL : FF + (j + 1) * FL] = t[:, FL:]
    for j in range(4):

        @pl.when(jnp.logical_not(diag & (z == j)))
        def _():
            got(r.gc3.at[j], r.s_c6.at[j])
            got(r.go3.at[j], r.s_o6.at[j])

    for last, out in ((r.gc3, r.gco), (r.go3, r.goo)):
        out[...] = (last[0].astype(F32) + last[1].astype(F32)) + (
            last[2].astype(F32) + last[3].astype(F32)
        )

    total = r.gh[...]
    g = r.ps[y].astype(F32)
    for k in range(1, 4):
        got(r.r1.at[y_from[k]], r.s_r4.at[y_from[k]])
        g = g + r.r1[y_from[k]].astype(F32)
    v = r.xs[my4, :].astype(F32)
    inv = lax.rsqrt(jnp.mean(v * v, axis=1, keepdims=True) + EPS)
    unit = v * inv
    g = g * gain_a
    r.gt[...] = total + inv * (g - unit * jnp.mean(g * unit, axis=1, keepdims=True))

    for k in range(1, 8):
        got(r.gp3.at[ctx_from[k]], r.s_p3.at[k])
    for j in range(4):
        t = r.gp3[2 * j].astype(F32) + r.gp3[2 * j + 1].astype(F32)
        for place, (start, size) in PLACES:
            n = 0 if start < 512 else 1 if start < 768 else 2
            to = PCOLS[n][0] + j * PCOLS[n][1] + start - PCOLS[n][2]
            r.gpo[:, to : to + size] = t[:, place : place + size]
    total = r.ggt2[...]
    for k in range(1, 8):
        got(r.gg3.at[ctx_from[k]], r.s_a3.at[k])
        total = total + r.gg3[ctx_from[k]]
    r.ggo[...] = total

    finish(list(sends))


def hand_over(ggo, lo, gt, gpo, goo, geo, gco, *refs):
    outs, (ag, fg, hg), kept, sem = refs[:6], refs[6:9], refs[9:15], refs[15]
    ins = (lo, gt, gpo, goo, geo, gco)
    loads = [pltpu.make_async_copy(ins[n], kept[n], sem.at[n]) for n in range(6)]
    stores = [pltpu.make_async_copy(kept[n], outs[n], sem.at[6 + n]) for n in range(6)]
    for cp in loads:
        cp.start()
    for load, store in zip(loads, stores, strict=True):
        load.wait()
        store.start()
    place = 8 * lax.axis_index("seq") + lax.axis_index("ctx")
    row = lax.broadcasted_iota(jnp.int32, (8, 128), 0)
    lane = lax.broadcasted_iota(jnp.int32, (8, 128), 1)
    for n, (ref, size) in enumerate(((ag, 8), (fg, 8), (hg, 2))):
        tile = ggo[8 * n : 8 * n + 8, :]
        got = jnp.zeros((1, size), F32)
        at = lax.broadcasted_iota(jnp.int32, (1, size), 1)
        for j in range(size):
            value = jnp.where(row * 128 + lane == place * size + j, tile, 0.0)
            value = jnp.sum(jnp.sum(value, axis=1, keepdims=True), axis=0, keepdims=True)
            got = jnp.where(at == j, value, got)
        ref[...] = got
    for cp in stores:
        cp.wait()


def per_device(x, dy, segments, positions, ag, proj, hg, out, fg, expn, con):
    del positions
    vmem = pl.BlockSpec(memory_space=pltpu.VMEM)
    hbm = pl.BlockSpec(memory_space=pl.ANY)
    scratch = [pltpu.VMEM(shape, kind) for shape, kind in SCRATCH.values()]
    sems = [pltpu.SemaphoreType.DMA(n if isinstance(n, tuple) else (n,)) for n in RECV.values()]
    res = pl.pallas_call(
        kernel,
        name="layer",
        out_shape=(
            jax.ShapeDtypeStruct((TOK, D), BF16),
            jax.ShapeDtypeStruct((TOK, D), F32),
            jax.ShapeDtypeStruct((8, 4096), F32),
            jax.ShapeDtypeStruct((16, D), F32),
            jax.ShapeDtypeStruct((8, 6144), F32),
            jax.ShapeDtypeStruct((24, D), F32),
            jax.ShapeDtypeStruct((24, 128), F32),
        ),
        in_specs=[hbm] * 6 + [vmem] * 4,
        out_specs=(vmem,) * 7,
        scratch_shapes=scratch
        + sems
        + [pltpu.SemaphoreType.DMA((N_SEND,)), pltpu.SemaphoreType.DMA((16,))],
        compiler_params=pltpu.CompilerParams(
            collective_id=0, has_side_effects=True, vmem_limit_bytes=63 * 2**20
        ),
    )(
        x.reshape(TOK, D), dy.reshape(TOK, D), proj, out, expn, con,
        ag.reshape(1, 8), fg.reshape(1, 8), hg.reshape(1, 2), segments,
    )
    big, gains = res[:6], res[6]
    lo, gt, gpo, goo, geo, gco, gag, gfg, ghg = pl.pallas_call(
        hand_over,
        name="hand_over",
        out_shape=tuple(jax.ShapeDtypeStruct(a.shape, a.dtype) for a in big)
        + tuple(jax.ShapeDtypeStruct((1, n), F32) for n in (8, 8, 2)),
        in_specs=[vmem] + [pl.BlockSpec(memory_space=pltpu.HBM)] * 6,
        out_specs=(pl.BlockSpec(memory_space=pltpu.HBM),) * 6 + (vmem,) * 3,
        scratch_shapes=[pltpu.VMEM(a.shape, a.dtype) for a in big]
        + [pltpu.SemaphoreType.DMA((12,))],
        compiler_params=pltpu.CompilerParams(vmem_limit_bytes=63 * 2**20),
    )(gains, *big)
    return (
        lo.reshape(1, TOK, D),
        gt.reshape(1, TOK, D),
        gag.reshape(8),
        gpo,
        ghg.reshape(2),
        goo,
        gfg.reshape(8),
        geo,
        gco,
    )


def solution(mesh):
    return jax.shard_map(
        per_device,
        mesh=mesh,
        in_specs=(
            P("seq", "ctx", None),
            P("seq", "ctx", None),
            P("seq", None),
            P("seq", "ctx"),
            P(("seq", "ctx")),
            P(("seq", "ctx"), None),
            P(("seq", "ctx")),
            P(("seq", "ctx"), None),
            P(("seq", "ctx")),
            P(("seq", "ctx"), None),
            P(("seq", "ctx"), None),
        ),
        out_specs=(
            P("seq", "ctx", None),
            P("seq", "ctx", None),
            P(("seq", "ctx")),
            P(("seq", "ctx"), None),
            P(("seq", "ctx")),
            P(("seq", "ctx"), None),
            P(("seq", "ctx")),
            P(("seq", "ctx"), None),
            P(("seq", "ctx"), None),
        ),
        check_vma=False,
    )
```
